32 devices in a mesh: seq: 4 (over z), enc: 8 (over y, x, core).
Axes of the slice: x: 2, y: 2, z: 4, core: 2. Of those that a mesh axis runs over, the one named last changes fastest.
Arguments:
- queries: bfloat16 [4096, 4096], P(('seq', 'enc')), may hold values from -8 to 8
- keys: bfloat16 [8, 1601, 512], P('enc'), may hold values from -8 to 8
- values: bfloat16 [8, 1601, 512], P('enc'), may hold values from -24 to 24
- reads: int32 [32, 4], replicated, may hold values from 0 to 7, all different within a row; in each aligned block of 8 rows (0 to 7, 8 to 15, ...) at most 6 rows name the same one
- grad_out: bfloat16 [4096, 4096], P(('seq', 'enc')), may hold values from -24 to 24
Outputs:
- attended: bfloat16 [4096, 4096], P(('seq', 'enc'))
- grad_queries: bfloat16 [4096, 4096], P(('seq', 'enc'))
- grad_keys: bfloat16 [8, 1601, 512], P('enc', None, 'seq')
- grad_values: bfloat16 [8, 1601, 512], P('enc', None, 'seq')
The draws below stay inside these ranges and needn't reach their ends.
Inputs may be any that keep to these rules, and one draw needn't show every extreme that they name: `reads`: each row names 4 different images; in each aligned block of 8 rows (the text blocks of one index of seq) no image is named by more than 6 rows, and in some such block one image is named by exactly 6.
All inputs are finite; a program needn't handle non-finite values.
Results may differ from the reference program's by a relative error of at most 0.04.
Values may be sent and summed in bfloat16 or wider, within the bound.
No kernel may reach another device: no remote copies, remote signals or barrier semaphores. Data moves between devices by JAX's collectives and lax.ppermute only.
A program may use at most 128 MiB of HBM per device.

```python
import math
import jax
import jax.numpy as jnp
import numpy as np
from jax import lax

HQ = 32
KVH = 4
HD = 128
VT = 1601
R = 4
MOST = 6
SEG = 32
IMAGES = 8
BLOCKS = 32
TOKENS = 4096
N_SEQ = 4
N_ENC = 8


def draw_queries(key, part):
    key = jax.random.fold_in(key, 11)
    base = jnp.clip(jax.random.normal(key, (TOKENS, HQ * HD), jnp.float32), -6.0, 6.0)
    return base.astype(jnp.bfloat16)


def draw_keys(key, part):
    key = jax.random.fold_in(key, 12)
    base = jnp.clip(jax.random.normal(key, (IMAGES, VT, KVH * HD), jnp.float32), -6.0, 6.0)
    return base.astype(jnp.bfloat16)


def shard_levels(key, extent, cuts, smallest, largest):
    def one(dim, shards_of):
        draws = jax.random.uniform(jax.random.fold_in(jax.random.fold_in(key, 6), dim), (shards_of,), jnp.float32, smallest / len(cuts), largest / len(cuts))
        return jnp.repeat(jnp.exp(draws), extent[dim] // shards_of).reshape((-1,) + (1,) * (len(extent) - dim - 1))

    gain = one(*cuts[0])
    for cut in cuts[1:]:
        gain = gain * one(*cut)
    return gain


def assign_block(stream_key, own, number, rows, amount, top, bound, lean):
    ranking = jax.random.permutation(stream_key, amount)
    heavy_load, common = shares(amount, rows * top, bound, lean, True), shares(amount, rows * top, bound, lean, False)
    places = jnp.arange(amount)

    def named(lengths, turn):
        used = int((lengths > 0).sum())
        fixed = max(1, used // 4)
        moved = fixed + (places - fixed + turn * (used - fixed)) % max(1, amount - fixed)
        return jnp.zeros((amount,), jnp.int32).at[ranking[jnp.where(places < fixed, places, moved)]].set(jnp.asarray(lengths, jnp.int32))

    lengths = jnp.where(number % 4 == 0, named(heavy_load, number // 4), named(common, number - number // 4 - 1))
    mixed = jax.random.permutation(jax.random.fold_in(own, 3), amount)
    source_of, receiver = mixed[0:amount // 2 * 2:2], mixed[1:amount // 2 * 2:2]
    room = jnp.minimum(lengths[source_of] - 1, bound - lengths[receiver]) // 2
    room = jnp.where((source_of == ranking[0]) | (receiver == ranking[0]) | (lengths[receiver] == 0), 0, jnp.maximum(room, 0))
    moved = jax.random.randint(jax.random.fold_in(own, 4), (amount // 2,), 0, 1 << 20) % (room + 1)
    lengths = lengths.at[source_of].add(-moved).at[receiver].add(moved)
    labels = jnp.searchsorted(jnp.cumsum(lengths), jnp.arange(rows * top), side="right").astype(jnp.int32)
    table = labels.reshape(top, rows).T
    table = table[jax.random.permutation(jax.random.fold_in(own, 1), rows)]
    turn = jax.random.randint(jax.random.fold_in(own, 2), (rows, 1), 0, top)
    return jnp.take_along_axis(table, (jnp.arange(top)[None, :] + turn) % top, axis=1)


def shares(count, total, most, lean, full):
    weights = [(1 << 20) // math.isqrt(grade ** lean) + 1 for grade in range(1, count + 1)]
    largest = most if full else min(most, max(-(-total // count), total * weights[0] // sum(weights)))
    least = 1 if total - largest >= count - 1 else 0
    counts, surplus = [largest] + [least] * (count - 1), total - largest - least * (count - 1)
    while surplus > 0:
        free = [i for i in range(1, count) if counts[i] < largest] or [i for i in range(1, count) if counts[i] < most]
        pool, remaining = sum([weights[i] for i in free]), surplus
        for i in free:
            extra = min(most - counts[i], max(1, remaining * weights[i] // pool), surplus)
            counts[i] = counts[i] + extra
            surplus = surplus - extra
    return np.array(counts)


def bell_draw(key, shape, deviation, most, cuts=(), kind=jnp.bfloat16):
    level = shard_levels(key, shape, cuts, -0.22, 0.18) if cuts else 1.0
    drawn = jax.random.normal(key, shape, jnp.float32) * deviation * level
    return jnp.minimum(jnp.maximum(drawn, -most), most).astype(kind)


def setup_inputs(seed: int = 0) -> dict:
    key_list = jax.random.split(jax.random.key(seed), 6)
    queries = draw_queries(jax.random.fold_in(key_list[5], 71), 0)
    keys = draw_keys(jax.random.fold_in(key_list[5], 71), 0)
    values = bell_draw(key_list[2], (IMAGES, VT, KVH * HD), 4.0, 24.0, ((0, 8),))
    reads_keys = jax.random.split(jax.random.fold_in(key_list[3], 1), BLOCKS // N_ENC)
    reads_turns = jax.random.permutation(jax.random.fold_in(key_list[3], 3), BLOCKS // N_ENC)
    reads = jax.vmap(lambda own, number: assign_block(jax.random.fold_in(key_list[3], 2), own, number, N_ENC, IMAGES, R, MOST, 2))(reads_keys, reads_turns).reshape((BLOCKS, R))
    grad_out = bell_draw(key_list[4], (TOKENS, HQ * HD), 4.0, 24.0, ((0, 32),))
    return {"queries": queries, "keys": keys, "values": values, "reads": reads, "grad_out": grad_out}


def forward_heads(rows_q, keys_img, values_img):
    count = rows_q.shape[0]
    group = HQ // KVH
    scale = HD ** -0.5
    outputs = []
    totals = []
    for head in range(KVH):
        q_head = rows_q[:, head * group * HD:(head + 1) * group * HD].reshape(count, group, HD).astype(jnp.float32)
        k_head = keys_img[:, head * HD:(head + 1) * HD].astype(jnp.float32)
        v_head = values_img[:, head * HD:(head + 1) * HD].astype(jnp.float32)
        scores = jnp.einsum("ngd,jd->ngj", q_head, k_head) * scale
        top = jnp.max(scores, axis=-1, keepdims=True)
        total = jnp.sum(jnp.exp(scores - top), axis=-1, keepdims=True)
        lse = top + jnp.log(total)
        weights = jnp.exp(scores - lse).astype(jnp.bfloat16)
        output = jnp.einsum("ngj,jd->ngd", weights.astype(jnp.float32), v_head)
        outputs.append(output.reshape(count, group * HD))
        totals.append(lse[..., 0])
    return jnp.concatenate(outputs, axis=-1).astype(jnp.bfloat16), jnp.stack(totals, axis=1)


def backward_heads(rows_q, rows_o, rows_g, lse_all, keys_img, values_img):
    count = rows_q.shape[0]
    group = HQ // KVH
    scale = HD ** -0.5
    query_parts = []
    key_parts = []
    value_parts = []
    for head in range(KVH):
        cols = slice(head * group * HD, (head + 1) * group * HD)
        q_head = rows_q[:, cols].reshape(count, group, HD).astype(jnp.float32)
        o_head = rows_o[:, cols].reshape(count, group, HD).astype(jnp.float32)
        g_head = rows_g[:, cols].reshape(count, group, HD).astype(jnp.float32)
        k_head = keys_img[:, head * HD:(head + 1) * HD].astype(jnp.float32)
        v_head = values_img[:, head * HD:(head + 1) * HD].astype(jnp.float32)
        scores = jnp.einsum("ngd,jd->ngj", q_head, k_head) * scale
        prob = jnp.exp(scores - lse_all[:, head][..., None])
        weights = prob.astype(jnp.bfloat16).astype(jnp.float32)
        delta = jnp.sum(g_head * o_head, axis=-1)
        dprob = jnp.einsum("ngd,jd->ngj", g_head, v_head)
        dscore = (prob * (dprob - delta[..., None])).astype(jnp.bfloat16).astype(jnp.float32)
        query_parts.append((jnp.einsum("ngj,jd->ngd", dscore, k_head) * scale).reshape(count, group * HD))
        key_parts.append(jnp.einsum("ngj,ngd->jd", dscore, q_head) * scale)
        value_parts.append(jnp.einsum("ngj,ngd->jd", weights, g_head))
    grad_rows = jnp.concatenate(query_parts, axis=-1).astype(jnp.bfloat16)
    return grad_rows, jnp.concatenate(key_parts, axis=-1), jnp.concatenate(value_parts, axis=-1)


def reference(queries, keys, values, reads, grad_out):
    width = HQ * HD
    span = KVH * HD
    q_rows = queries.reshape(N_SEQ, N_ENC, R, SEG, width)
    g_rows = grad_out.reshape(N_SEQ, N_ENC, R, SEG, width)
    r_rows = reads.reshape(N_SEQ, N_ENC, R)
    empty = jnp.zeros((IMAGES, VT, span), jnp.float32)

    def one_block(carry, item):
        key_sum, value_sum = carry
        q_block, g_block, r_block = item
        outputs = []
        grads = []
        for segment in range(R):
            image = r_block[segment].astype(jnp.int32)
            key_img = lax.dynamic_index_in_dim(keys, image, 0, keepdims=False)
            value_img = lax.dynamic_index_in_dim(values, image, 0, keepdims=False)
            output, lse_all = forward_heads(q_block[segment], key_img, value_img)
            grad_rows, key_part, value_part = backward_heads(q_block[segment], output, g_block[segment], lse_all, key_img, value_img)
            key_sum = key_sum.at[image].add(key_part)
            value_sum = value_sum.at[image].add(value_part)
            outputs.append(output)
            grads.append(grad_rows)
        return (key_sum, value_sum), (jnp.stack(outputs), jnp.stack(grads))

    def one_row(carry, item):
        total_keys, total_values = carry
        (row_keys, row_values), (outputs, grads) = lax.scan(one_block, (empty, empty), item)
        total_keys = total_keys + lax.optimization_barrier(row_keys.astype(jnp.bfloat16)).astype(jnp.float32)
        total_values = total_values + lax.optimization_barrier(row_values.astype(jnp.bfloat16)).astype(jnp.float32)
        return (total_keys, total_values), (outputs, grads)

    (total_keys, total_values), (outputs, grads) = lax.scan(one_row, (empty, empty), (q_rows, g_rows, r_rows))
    attended = outputs.reshape(TOKENS, width)
    grad_queries = grads.reshape(TOKENS, width)
    return attended, grad_queries, total_keys.astype(jnp.bfloat16), total_values.astype(jnp.bfloat16)
```

```python
import functools

import jax
import jax.numpy as jnp
from jax import lax
from jax.experimental import pallas as pl
from jax.experimental.pallas import tpu as pltpu
from jax.sharding import PartitionSpec as P

HQ = 32
KVH = 4
HD = 128
GROUP = HQ // KVH
WIDTH = GROUP * HD
SCALE = HD ** (-0.5)
LOG2E = 1.4426950408889634
CHUNK = 256
LOWEST = -3.0e38
PER_CHUNK = 2
ANY = pl.BlockSpec(memory_space=pl.ANY)
SMEM = pl.BlockSpec(memory_space=pltpu.SMEM)
VMEM = pl.BlockSpec(memory_space=pltpu.VMEM)


def head_at(turn):
    if lax.axis_size("seq") == KVH:
        return lax.axis_index("seq") ^ (KVH - 1 - turn)
    return turn


def route_kernel(turns, n_seg, seg_rows, reads, q_hbm, g_hbm, out, stage, in_sems, out_sems):
    row = lax.axis_index("seq") * lax.axis_size("enc") + lax.axis_index("enc")
    arriving = []
    for i, turn in enumerate(turns):
        column = pl.multiple_of(head_at(turn) * WIDTH, WIDTH)
        for which, source in enumerate((q_hbm, g_hbm)):
            arriving.append(
                pltpu.make_async_copy(
                    source.at[:, pl.ds(column, WIDTH)], stage.at[i, which], in_sems.at[i, which]
                )
            )
    for copy in arriving:
        copy.start()
    for copy in arriving:
        copy.wait()
    leaving = [
        pltpu.make_async_copy(
            stage.at[:, :, r * seg_rows : (r + 1) * seg_rows, :],
            out.at[reads[row, r]],
            out_sems.at[r],
        )
        for r in range(n_seg)
    ]
    for copy in leaving:
        copy.start()
    for copy in leaving:
        copy.wait()


def collect_kernel(chunks, n_seg, seg_rows, reads, *refs):
    returned = refs[: len(chunks)]
    o_out, dq_out, sems = refs[len(chunks) :]
    row = lax.axis_index("seq") * lax.axis_size("enc") + lax.axis_index("enc")
    copies = []
    for c, turns in enumerate(chunks):
        for i, turn in enumerate(turns):
            column = pl.multiple_of(head_at(turn) * WIDTH, WIDTH)
            for r in range(n_seg):
                for which, target in enumerate((o_out, dq_out)):
                    copies.append(
                        pltpu.make_async_copy(
                            returned[c].at[reads[row, r], i, which],
                            target.at[r * seg_rows : (r + 1) * seg_rows, pl.ds(column, WIDTH)],
                            sems.at[turn, r, which],
                        )
                    )
    for copy in copies:
        copy.start()
    for copy in copies:
        copy.wait()


def is_read(reads, row, image):
    found = jnp.int32(0)
    for r in range(reads.shape[1]):
        found = found + (reads[row, r] == image).astype(jnp.int32)
    return found > 0


def attend_kernel(turn, place, peers, seg_rows, tokens, reads, k_hbm, v_hbm, received, *refs):
    (
        returned,
        grads,
        k_raw,
        v_raw,
        k_pad,
        v_pad,
        k_turned,
        v_turned,
        inbox,
        outbox,
        scores,
        weights,
        dscores,
        dk_sum,
        dv_sum,
        kv_sems,
        in_sems,
        out_sems,
    ) = refs[-18:]
    me = lax.axis_index("enc")
    base = lax.axis_index("seq") * peers
    column = pl.multiple_of(head_at(turn) * HD, HD)
    padded = k_pad.shape[0]
    whole = tokens // 16 * 16

    kv_copies = [
        pltpu.make_async_copy(source.at[0, :, pl.ds(column, HD)], target, kv_sems.at[i])
        for i, (source, target) in enumerate(((k_hbm, k_raw), (v_hbm, v_raw)))
    ]
    for copy in kv_copies:
        copy.start()

    count = jnp.int32(0)
    plan = []
    for k in range(peers):
        found = is_read(reads, base + k, me)
        plan.append((found, count))
        count = count + found.astype(jnp.int32)

    def arriving(k, slot):
        return pltpu.make_async_copy(received.at[k, place], inbox.at[slot], in_sems.at[k])

    def leaving(k, slot):
        return pltpu.make_async_copy(outbox.at[slot], returned.at[k, place], out_sems.at[k])

    for k, (found, slot) in enumerate(plan):

        @pl.when(found)
        def _():
            arriving(k, slot).start()

    for copy in kv_copies:
        copy.wait()
    for raw, pad, turned in ((k_raw, k_pad, k_turned), (v_raw, v_pad, v_turned)):
        pad[0:whole, :] = raw[0:whole, :]
        if whole < tokens:
            last = jnp.zeros((padded - tokens, HD), jnp.bfloat16)
            pad[whole:padded, :] = jnp.concatenate([raw[whole:tokens, :], last], axis=0)
        turned[...] = pad[...].astype(jnp.float32).T.astype(jnp.bfloat16)
    dk_sum[...] = jnp.zeros_like(dk_sum)
    dv_sum[...] = jnp.zeros_like(dv_sum)

    for k, (found, slot) in enumerate(plan):

        @pl.when(found)
        def _():
            arriving(k, slot).wait()

    pieces = [(a, min(a + CHUNK, padded)) for a in range(0, padded, CHUNK)]
    lanes = GROUP * seg_rows
    over_d = (((1,), (1,)), ((), ()))

    def stacked(slot, which):
        return jnp.concatenate(
            [inbox[slot, which, :, h * HD : (h + 1) * HD] for h in range(GROUP)], axis=0
        )

    def store(slot, which, turned_value):
        value = turned_value.T.astype(jnp.bfloat16)
        for h in range(GROUP):
            outbox[slot, which, :, h * HD : (h + 1) * HD] = value[
                h * seg_rows : (h + 1) * seg_rows, :
            ]

    def one_slot(slot, carry):
        q = stacked(slot, 0)
        g = stacked(slot, 1)
        top = jnp.full((1, lanes), LOWEST, jnp.float32)
        for a, b in pieces:
            part = lax.dot_general(k_pad[a:b, :], q, over_d, preferred_element_type=jnp.float32)
            if b > tokens:
                token = lax.broadcasted_iota(jnp.int32, part.shape, 0) + a
                part = jnp.where(token < tokens, part, LOWEST)
            scores[a:b, :] = part
            top = jnp.maximum(top, jnp.max(part, axis=0, keepdims=True))
        total = jnp.zeros((1, lanes), jnp.float32)
        for a, b in pieces:
            part = jnp.exp2((scores[a:b, :] - top) * (SCALE * LOG2E))
            total = total + jnp.sum(part, axis=0, keepdims=True)
            scores[a:b, :] = part
            weights[a:b, :] = part.astype(jnp.bfloat16)
        inverse = 1.0 / total
        out = jnp.dot(v_turned[...], weights[...], preferred_element_type=jnp.float32) * inverse
        store(slot, 0, out)
        g_turned = g.astype(jnp.float32).T * inverse
        g_scaled = g_turned.T.astype(jnp.bfloat16)
        delta = jnp.sum(
            g_turned * out.astype(jnp.bfloat16).astype(jnp.float32), axis=0, keepdims=True
        )
        for a, b in pieces:
            part = lax.dot_general(
                v_pad[a:b, :], g_scaled, over_d, preferred_element_type=jnp.float32
            )
            part = (scores[a:b, :] * (part - delta)).astype(jnp.bfloat16)
            dscores[a:b, :] = part
            dk_sum[a:b, :] += jnp.dot(part, q, preferred_element_type=jnp.float32)
            dv_sum[a:b, :] += jnp.dot(
                weights[a:b, :], g_scaled, preferred_element_type=jnp.float32
            )
        turned_dq = jnp.dot(k_turned[...], dscores[...], preferred_element_type=jnp.float32)
        store(slot, 1, turned_dq * SCALE)
        return carry

    lax.fori_loop(0, count, one_slot, 0)

    for k, (found, slot) in enumerate(plan):

        @pl.when(found)
        def _():
            leaving(k, slot).start()

    grads[0] = (dk_sum[...] * SCALE).astype(jnp.bfloat16)
    grads[1] = dv_sum[...].astype(jnp.bfloat16)

    for k, (found, slot) in enumerate(plan):

        @pl.when(found)
        def _():
            leaving(k, slot).wait()


def xor_permute(array, axis, k):
    if k == 0:
        return array
    size = lax.axis_size(axis)
    return lax.ppermute(array, axis, [(i, i ^ k) for i in range(size)])


def per_device(queries, keys, values, reads, grad_out):
    peers = lax.axis_size("enc")
    n_seq = lax.axis_size("seq")
    n_seg = reads.shape[1]
    seg_rows = queries.shape[0] // n_seg
    slots = min(peers, 3 * n_seg // 2)
    tokens = keys.shape[1]
    padded = (tokens + 15) // 16 * 16
    lanes = GROUP * seg_rows
    bf16, f32 = jnp.bfloat16, jnp.float32
    chunks = [tuple(range(i, i + PER_CHUNK)) for i in range(0, KVH, PER_CHUNK)]
    message = jax.ShapeDtypeStruct((peers, PER_CHUNK, 2, seg_rows, WIDTH), bf16)

    def route(turns):
        return pl.pallas_call(
            functools.partial(route_kernel, turns, n_seg, seg_rows),
            out_shape=message,
            in_specs=[SMEM, ANY, ANY],
            out_specs=ANY,
            scratch_shapes=[
                pltpu.VMEM((PER_CHUNK, 2, n_seg * seg_rows, WIDTH), bf16),
                pltpu.SemaphoreType.DMA((PER_CHUNK, 2)),
                pltpu.SemaphoreType.DMA((n_seg,)),
            ],
            cost_estimate=pl.CostEstimate(flops=0, bytes_accessed=2 << 20, transcendentals=0),
            name=f"route_{turns[0]}",
        )(reads, queries, grad_out)

    def attend(turn, received, returned):
        work = slots * lanes * tokens * HD
        first = returned is None
        return pl.pallas_call(
            functools.partial(
                attend_kernel, turn, turn % PER_CHUNK, peers, seg_rows, tokens
            ),
            out_shape=[message, jax.ShapeDtypeStruct((2, padded, HD), bf16)],
            in_specs=[SMEM] + [ANY] * (3 if first else 4),
            out_specs=[ANY, VMEM],
            input_output_aliases={} if first else {4: 0},
            scratch_shapes=[
                pltpu.VMEM((tokens, HD), bf16),
                pltpu.VMEM((tokens, HD), bf16),
                pltpu.VMEM((padded, HD), bf16),
                pltpu.VMEM((padded, HD), bf16),
                pltpu.VMEM((HD, padded), bf16),
                pltpu.VMEM((HD, padded), bf16),
                pltpu.VMEM((slots, 2, seg_rows, WIDTH), bf16),
                pltpu.VMEM((slots, 2, seg_rows, WIDTH), bf16),
                pltpu.VMEM((padded, lanes), f32),
                pltpu.VMEM((padded, lanes), bf16),
                pltpu.VMEM((padded, lanes), bf16),
                pltpu.VMEM((padded, HD), f32),
                pltpu.VMEM((padded, HD), f32),
                pltpu.SemaphoreType.DMA((2,)),
                pltpu.SemaphoreType.DMA((peers,)),
                pltpu.SemaphoreType.DMA((peers,)),
            ],
            compiler_params=pltpu.CompilerParams(vmem_limit_bytes=40 << 20),
            cost_estimate=pl.CostEstimate(
                flops=24 * work, bytes_accessed=4 << 20, transcendentals=slots * lanes * tokens
            ),
            name=f"attend_{turn}",
        )(reads, keys, values, received, *([] if first else [returned]))

    def collect(returned):
        whole = jax.ShapeDtypeStruct(queries.shape, bf16)
        return pl.pallas_call(
            functools.partial(collect_kernel, chunks, n_seg, seg_rows),
            out_shape=[whole, whole],
            in_specs=[SMEM] + [ANY] * len(chunks),
            out_specs=[VMEM, VMEM],
            scratch_shapes=[pltpu.SemaphoreType.DMA((KVH, n_seg, 2))],
            cost_estimate=pl.CostEstimate(flops=0, bytes_accessed=4 << 20, transcendentals=0),
            name="collect",
        )(reads, *returned)

    def exchange(array):
        return lax.all_to_all(array, "enc", split_axis=0, concat_axis=0, tiled=True)

    received = [exchange(route(turns)) for turns in chunks]
    answers, grads = [], []
    for c, turns in enumerate(chunks):
        returned = None
        arrived = received[c]
        if grads:
            arrived, grads[-1] = lax.optimization_barrier((arrived, grads[-1]))
        for turn in turns:
            returned, grad = attend(turn, arrived, returned)
            grads.append(grad)
        answers.append(exchange(returned))
    attended, grad_queries = collect(answers)

    if n_seq == KVH:
        passed = xor_permute(grads[0], "seq", 1)
        pair = (grads[1].astype(f32) + passed.astype(f32)).astype(bf16)
        pair = xor_permute(pair, "seq", 2)
        near = xor_permute(grads[2], "seq", 1)
        total = grads[3].astype(f32) + near.astype(f32) + pair.astype(f32)
        total = total.astype(bf16)[:, :tokens]
        return attended, grad_queries, total[0][None], total[1][None]
    joined = jnp.concatenate(grads, axis=2)[:, :tokens]
    summed = lax.psum_scatter(joined, "seq", scatter_dimension=2, tiled=True)
    return attended, grad_queries, summed[0][None], summed[1][None]


def solution(mesh):
    placed = (
        P(("seq", "enc"), None),
        P("enc", None, None),
        P("enc", None, None),
        P(),
        P(("seq", "enc"), None),
    )
    return jax.shard_map(
        per_device,
        mesh=mesh,
        in_specs=placed,
        out_specs=(
            P(("seq", "enc"), None),
            P(("seq", "enc"), None),
            P("enc", None, "seq"),
            P("enc", None, "seq"),
        ),
        check_vma=False,
    )
```

```python
import functools

import jax
import jax.numpy as jnp
from jax import lax
from jax.experimental import pallas as pl
from jax.experimental.pallas import tpu as pltpu
from jax.sharding import PartitionSpec as P

HQ = 32
KVH = 4
HD = 128
GROUP = HQ // KVH
WIDTH = GROUP * HD
SCALE = HD ** (-0.5)
LOG2E = 1.4426950408889634
CHUNK = 512
LOWEST = -3.0e38
PER_CHUNK = 2
VMEM_BYTES = 58 << 20
ANY = pl.BlockSpec(memory_space=pl.ANY)
SMEM = pl.BlockSpec(memory_space=pltpu.SMEM)
VMEM = pl.BlockSpec(memory_space=pltpu.VMEM)


def head_at(turn):
    if lax.axis_size("seq") == KVH:
        return lax.axis_index("seq") ^ (KVH - 1 - turn)
    return turn


def route_kernel(turns, n_seg, seg_rows, reads, q_hbm, g_hbm, out, stage, in_sems, out_sems):
    row = lax.axis_index("seq") * lax.axis_size("enc") + lax.axis_index("enc")
    arriving = []
    for i, turn in enumerate(turns):
        column = pl.multiple_of(head_at(turn) * WIDTH, WIDTH)
        for which, source in enumerate((q_hbm, g_hbm)):
            arriving.append(
                pltpu.make_async_copy(
                    source.at[:, pl.ds(column, WIDTH)], stage.at[i, which], in_sems.at[i, which]
                )
            )
    for copy in arriving:
        copy.start()
    for copy in arriving:
        copy.wait()
    leaving = [
        pltpu.make_async_copy(
            stage.at[:, :, r * seg_rows : (r + 1) * seg_rows, :],
            out.at[reads[r, row]],
            out_sems.at[r],
        )
        for r in range(n_seg)
    ]
    for copy in leaving:
        copy.start()
    for copy in leaving:
        copy.wait()


def collect_kernel(chunks, n_seg, seg_rows, reads, *refs):
    returned = refs[: len(chunks)]
    o_out, dq_out, sems = refs[len(chunks) :]
    row = lax.axis_index("seq") * lax.axis_size("enc") + lax.axis_index("enc")
    copies = []
    for c, turns in enumerate(chunks):
        for i, turn in enumerate(turns):
            column = pl.multiple_of(head_at(turn) * WIDTH, WIDTH)
            for r in range(n_seg):
                for which, target in enumerate((o_out, dq_out)):
                    copies.append(
                        pltpu.make_async_copy(
                            returned[c].at[reads[r, row], i, which],
                            target.at[r * seg_rows : (r + 1) * seg_rows, pl.ds(column, WIDTH)],
                            sems.at[turn, r, which],
                        )
                    )
    for copy in copies:
        copy.start()
    for copy in copies:
        copy.wait()


def is_read(reads, row, image):
    found = jnp.int32(0)
    for r in range(reads.shape[0]):
        found = found + (reads[r, row] == image).astype(jnp.int32)
    return found > 0


def prepare_kernel(tokens, k_in, v_in, straight, turned):
    padded = straight.shape[2]
    whole = tokens // 16 * 16
    for which, source in enumerate((k_in, v_in)):
        for head in range(KVH):
            columns = slice(head * HD, (head + 1) * HD)
            straight[head, which, 0:whole, :] = source[0, 0:whole, columns]
            if whole < tokens:
                last = jnp.zeros((padded - tokens, HD), jnp.bfloat16)
                straight[head, which, whole:padded, :] = jnp.concatenate(
                    [source[0, whole:tokens, columns], last], axis=0
                )
            turned[head, which] = (
                straight[head, which].astype(jnp.float32).T.astype(jnp.bfloat16)
            )


def attend_kernel(turn, place, peers, seg_rows, tokens, reads, caches, turned_caches, received, *refs):
    (
        returned,
        grads,
        straight,
        turned,
        inbox,
        outbox,
        scores,
        weights,
        dscores,
        dk_sum,
        dv_sum,
        kv_sems,
        in_sems,
        out_sems,
    ) = refs[-14:]
    me = lax.axis_index("enc")
    base = lax.axis_index("seq") * peers
    padded = straight.shape[1]
    kv_copies = [
        pltpu.make_async_copy(source.at[head_at(turn)], target, kv_sems.at[i])
        for i, (source, target) in enumerate(((caches, straight), (turned_caches, turned)))
    ]
    for copy in kv_copies:
        copy.start()

    count = jnp.int32(0)
    plan = []
    for k in range(peers):
        found = is_read(reads, base + k, me)
        plan.append((found, count))
        count = count + found.astype(jnp.int32)

    def arriving(k, slot):
        return pltpu.make_async_copy(received.at[k, place], inbox.at[slot], in_sems.at[k])

    def leaving(k, slot):
        return pltpu.make_async_copy(outbox.at[slot], returned.at[k, place], out_sems.at[k])

    for k, (found, slot) in enumerate(plan):

        @pl.when(found)
        def _():
            arriving(k, slot).start()

    dk_sum[...] = jnp.zeros_like(dk_sum)
    dv_sum[...] = jnp.zeros_like(dv_sum)

    for k, (found, slot) in enumerate(plan):

        @pl.when(found)
        def _():
            arriving(k, slot).wait()

    for copy in kv_copies:
        copy.wait()
    pieces = [(a, min(a + CHUNK, padded)) for a in range(0, padded, CHUNK)]
    lanes = GROUP * seg_rows
    f32, bf16 = jnp.float32, jnp.bfloat16
    keys, values = straight.at[0], straight.at[1]

    def stacked(slot, which):
        return jnp.concatenate(
            [inbox[slot, which, :, h * HD : (h + 1) * HD] for h in range(GROUP)], axis=0
        )

    def store(slot, which, turned_value):
        value = turned_value.T.astype(bf16)
        for h in range(GROUP):
            outbox[slot, which, :, h * HD : (h + 1) * HD] = value[
                h * seg_rows : (h + 1) * seg_rows, :
            ]

    def masked(part, a, b, other):
        if b <= tokens:
            return part
        token = lax.broadcasted_iota(jnp.int32, part.shape, 0) + a
        return jnp.where(token < tokens, part, other)

    def forward(slot):
        q, g = (stacked(slot, i).astype(f32).T for i in range(2))
        q_turned = q.astype(bf16)
        state = {"top": jnp.full((1, lanes), LOWEST, f32), "total": jnp.zeros((1, lanes), f32)}

        def score(a, b):
            part = jnp.dot(keys[a:b, :], q_turned, preferred_element_type=f32)
            part = masked(part, a, b, LOWEST)
            scores[a:b, :] = part
            state["top"] = jnp.maximum(state["top"], jnp.max(part, axis=0, keepdims=True))

        def weigh(a, b):
            part = jnp.exp2((scores[a:b, :] - state["top"]) * (SCALE * LOG2E))
            state["total"] = state["total"] + jnp.sum(part, axis=0, keepdims=True)
            weights[a:b, :] = part.astype(bf16)

        def finish():
            out = jnp.dot(turned[1], weights[...], preferred_element_type=f32)
            out = out * (1.0 / state["total"])
            store(slot, 0, out)
            delta = jnp.sum(g * out.astype(bf16).astype(f32), axis=0, keepdims=True)
            lse = state["top"] * (SCALE * LOG2E) + jnp.log2(state["total"])
            return lse, delta, q_turned, g.astype(bf16)

        steps = [functools.partial(score, a, b) for a, b in pieces]
        return steps + [functools.partial(weigh, a, b) for a, b in pieces], finish

    def backward(slot, lse, delta, q_turned, g_turned):
        q, g = stacked(slot, 0), stacked(slot, 1)

        def step(a, b):
            part = jnp.dot(keys[a:b, :], q_turned, preferred_element_type=f32)
            prob = masked(jnp.exp2(part * (SCALE * LOG2E) - lse), a, b, 0.0)
            dprob = jnp.dot(values[a:b, :], g_turned, preferred_element_type=f32)
            dscore = (prob * (dprob - delta)).astype(bf16)
            dscores[a:b, :] = dscore
            dk_sum[a:b, :] += jnp.dot(dscore, q, preferred_element_type=f32)
            dv_sum[a:b, :] += jnp.dot(prob.astype(bf16), g, preferred_element_type=f32)

        def finish():
            turned_dq = jnp.dot(turned[0], dscores[...], preferred_element_type=f32)
            store(slot, 1, turned_dq * SCALE)

        return [functools.partial(step, a, b) for a, b in pieces], finish

    def one_slot(slot, carry):
        ahead, ahead_finish = forward(jnp.minimum(slot + 1, count - 1))
        behind, behind_finish = backward(slot, *carry)
        for i, step in enumerate(behind):
            for other in ahead[2 * i : 2 * i + 2]:
                other()
            step()
        behind_finish()
        return ahead_finish()

    @pl.when(count > 0)
    def _():
        first, first_finish = forward(0)
        for step in first:
            step()
        lax.fori_loop(0, count, one_slot, first_finish())

    for k, (found, slot) in enumerate(plan):

        @pl.when(found)
        def _():
            leaving(k, slot).start()

    grads[0] = (dk_sum[...] * SCALE).astype(jnp.bfloat16)
    grads[1] = dv_sum[...].astype(jnp.bfloat16)

    for k, (found, slot) in enumerate(plan):

        @pl.when(found)
        def _():
            leaving(k, slot).wait()


def xor_permute(array, axis, k):
    if k == 0:
        return array
    size = lax.axis_size(axis)
    return lax.ppermute(array, axis, [(i, i ^ k) for i in range(size)])


def per_device(queries, keys, values, reads, grad_out):
    peers = lax.axis_size("enc")
    n_seq = lax.axis_size("seq")
    n_seg = reads.shape[1]
    by_segment = reads.T
    seg_rows = queries.shape[0] // n_seg
    slots = min(peers, 3 * n_seg // 2)
    tokens = keys.shape[1]
    padded = (tokens + 15) // 16 * 16
    lanes = GROUP * seg_rows
    bf16, f32 = jnp.bfloat16, jnp.float32
    chunks = [tuple(range(i, i + PER_CHUNK)) for i in range(0, KVH, PER_CHUNK)]
    message = jax.ShapeDtypeStruct((peers, PER_CHUNK, 2, seg_rows, WIDTH), bf16)

    def route(turns):
        return pl.pallas_call(
            functools.partial(route_kernel, turns, n_seg, seg_rows),
            out_shape=message,
            in_specs=[SMEM, ANY, ANY],
            out_specs=ANY,
            scratch_shapes=[
                pltpu.VMEM((PER_CHUNK, 2, n_seg * seg_rows, WIDTH), bf16),
                pltpu.SemaphoreType.DMA((PER_CHUNK, 2)),
                pltpu.SemaphoreType.DMA((n_seg,)),
            ],
            compiler_params=pltpu.CompilerParams(vmem_limit_bytes=VMEM_BYTES),
            cost_estimate=pl.CostEstimate(flops=0, bytes_accessed=2 << 20, transcendentals=0),
            name=f"route_{turns[0]}",
        )(by_segment, queries, grad_out)

    prepared = pl.pallas_call(
        functools.partial(prepare_kernel, tokens),
        out_shape=[
            jax.ShapeDtypeStruct((KVH, 2, padded, HD), bf16),
            jax.ShapeDtypeStruct((KVH, 2, HD, padded), bf16),
        ],
        in_specs=[VMEM, VMEM],
        out_specs=[VMEM, VMEM],
        compiler_params=pltpu.CompilerParams(vmem_limit_bytes=VMEM_BYTES),
        cost_estimate=pl.CostEstimate(flops=0, bytes_accessed=16 << 20, transcendentals=0),
        name="prepare",
    )(keys, values)

    def attend(turn, received, returned):
        work = slots * lanes * tokens * HD
        first = returned is None
        return pl.pallas_call(
            functools.partial(
                attend_kernel, turn, turn % PER_CHUNK, peers, seg_rows, tokens
            ),
            out_shape=[message, jax.ShapeDtypeStruct((2, padded, HD), bf16)],
            in_specs=[SMEM] + [ANY] * (3 if first else 4),
            out_specs=[ANY, VMEM],
            input_output_aliases={} if first else {4: 0},
            scratch_shapes=[
                pltpu.VMEM((2, padded, HD), bf16),
                pltpu.VMEM((2, HD, padded), bf16),
                pltpu.VMEM((slots, 2, seg_rows, WIDTH), bf16),
                pltpu.VMEM((slots, 2, seg_rows, WIDTH), bf16),
                pltpu.VMEM((padded, lanes), f32),
                pltpu.VMEM((padded, lanes), bf16),
                pltpu.VMEM((padded, lanes), bf16),
                pltpu.VMEM((padded, HD), f32),
                pltpu.VMEM((padded, HD), f32),
                pltpu.SemaphoreType.DMA((2,)),
                pltpu.SemaphoreType.DMA((peers,)),
                pltpu.SemaphoreType.DMA((peers,)),
            ],
            compiler_params=pltpu.CompilerParams(vmem_limit_bytes=VMEM_BYTES),
            cost_estimate=pl.CostEstimate(
                flops=24 * work, bytes_accessed=4 << 20, transcendentals=slots * lanes * tokens
            ),
            name=f"attend_{turn}",
        )(by_segment, *prepared, received, *([] if first else [returned]))

    def collect(returned):
        whole = jax.ShapeDtypeStruct(queries.shape, bf16)
        return pl.pallas_call(
            functools.partial(collect_kernel, chunks, n_seg, seg_rows),
            out_shape=[whole, whole],
            in_specs=[SMEM] + [ANY] * len(chunks),
            out_specs=[VMEM, VMEM],
            scratch_shapes=[pltpu.SemaphoreType.DMA((KVH, n_seg, 2))],
            compiler_params=pltpu.CompilerParams(vmem_limit_bytes=VMEM_BYTES),
            cost_estimate=pl.CostEstimate(flops=0, bytes_accessed=4 << 20, transcendentals=0),
            name="collect",
        )(by_segment, *returned)

    def exchange(array):
        return lax.all_to_all(array, "enc", split_axis=0, concat_axis=0, tiled=True)

    received = [exchange(route(turns)) for turns in chunks]
    answers, grads = [], []
    for c, turns in enumerate(chunks):
        returned = None
        arrived = received[c]
        if grads:
            arrived, grads[-1] = lax.optimization_barrier((arrived, grads[-1]))
        for turn in turns:
            returned, grad = attend(turn, arrived, returned)
            grads.append(grad)
        answers.append(exchange(returned))
    attended, grad_queries = collect(answers)

    if n_seq == KVH:
        passed = xor_permute(grads[0], "seq", 1)
        pair = (grads[1].astype(f32) + passed.astype(f32)).astype(bf16)
        pair = xor_permute(pair, "seq", 2)
        near = xor_permute(grads[2], "seq", 1)
        total = grads[3].astype(f32) + near.astype(f32) + pair.astype(f32)
        total = total.astype(bf16)[:, :tokens]
        return attended, grad_queries, total[0][None], total[1][None]
    joined = jnp.concatenate(grads, axis=2)[:, :tokens]
    summed = lax.psum_scatter(joined, "seq", scatter_dimension=2, tiled=True)
    return attended, grad_queries, summed[0][None], summed[1][None]


def solution(mesh):
    placed = (
        P(("seq", "enc"), None),
        P("enc", None, None),
        P("enc", None, None),
        P(),
        P(("seq", "enc"), None),
    )
    return jax.shard_map(
        per_device,
        mesh=mesh,
        in_specs=placed,
        out_specs=(
            P(("seq", "enc"), None),
            P(("seq", "enc"), None),
            P("enc", None, "seq"),
            P("enc", None, "seq"),
        ),
        check_vma=False,
    )
```

```python
import functools

import jax
import jax.numpy as jnp
from jax import lax
from jax.experimental import pallas as pl
from jax.experimental.pallas import tpu as pltpu
from jax.sharding import PartitionSpec as P

HQ = 32
KVH = 4
HD = 128
GROUP = HQ // KVH
WIDTH = GROUP * HD
SCALE = HD ** (-0.5)
LOG2E = 1.4426950408889634
CHUNK = 2048
LOWEST = -3.0e38
PER_CHUNK = 2
VMEM_BYTES = 58 << 20
ANY = pl.BlockSpec(memory_space=pl.ANY)
SMEM = pl.BlockSpec(memory_space=pltpu.SMEM)
VMEM = pl.BlockSpec(memory_space=pltpu.VMEM)
HBM = pl.BlockSpec(memory_space=pltpu.HBM)


def head_at(turn):
    if lax.axis_size("seq") == KVH:
        return lax.axis_index("seq") ^ (KVH - 1 - turn)
    return turn


def route_kernel(turns, n_seg, seg_rows, tokens, reads, q_hbm, g_hbm, *refs):
    caches, (out, *prepared, stage, in_sems, out_sems) = refs[:-6], refs[-6:]
    if not caches:
        out, stage, in_sems, out_sems = refs
        prepared = ()
    row = lax.axis_index("seq") * lax.axis_size("enc") + lax.axis_index("enc")
    arriving = [[] for _ in range(n_seg)]
    for r in range(n_seg):
        rows = slice(r * seg_rows, (r + 1) * seg_rows)
        for i, turn in enumerate(turns):
            columns = pl.ds(pl.multiple_of(head_at(turn) * WIDTH, WIDTH), WIDTH)
            for which, source in enumerate((q_hbm, g_hbm)):
                arriving[r].append(
                    pltpu.make_async_copy(
                        source.at[rows, columns],
                        stage.at[r, i, which],
                        in_sems.at[r, i, which],
                    )
                )
    leaving = [
        pltpu.make_async_copy(stage.at[r], out.at[reads[r, row]], out_sems.at[r])
        for r in range(n_seg)
    ]
    for copies in arriving:
        for copy in copies:
            copy.start()
    for r, copies in enumerate(arriving):
        for copy in copies:
            copy.wait()
        leaving[r].start()
    if caches:
        prepare(tokens, *caches, *prepared)
    for copy in leaving:
        copy.wait()


def collect_kernel(chunks, n_seg, seg_rows, reads, *refs):
    returned = refs[: len(chunks)]
    o_out, dq_out, sems = refs[len(chunks) :]
    row = lax.axis_index("seq") * lax.axis_size("enc") + lax.axis_index("enc")
    copies = []
    for c, turns in enumerate(chunks):
        for i, turn in enumerate(turns):
            column = pl.multiple_of(head_at(turn) * WIDTH, WIDTH)
            for r in range(n_seg):
                for which, target in enumerate((o_out, dq_out)):
                    copies.append(
                        pltpu.make_async_copy(
                            returned[c].at[reads[r, row], i, which],
                            target.at[r * seg_rows : (r + 1) * seg_rows, pl.ds(column, WIDTH)],
                            sems.at[turn, r, which],
                        )
                    )
    for copy in copies:
        copy.start()
    for copy in copies:
        copy.wait()


def is_read(reads, row, image):
    found = jnp.int32(0)
    for r in range(reads.shape[0]):
        found = found + (reads[r, row] == image).astype(jnp.int32)
    return found > 0


def prepare(tokens, k_in, v_in, straight, turned):
    padded = straight.shape[2]
    whole = tokens // 16 * 16
    for which, source in enumerate((k_in, v_in)):
        for head in range(KVH):
            columns = slice(head * HD, (head + 1) * HD)
            straight[head, which, 0:whole, :] = source[0, 0:whole, columns]
            if whole < tokens:
                last = jnp.zeros((padded - tokens, HD), jnp.bfloat16)
                straight[head, which, whole:padded, :] = jnp.concatenate(
                    [source[0, whole:tokens, columns], last], axis=0
                )
            turned[head, which] = (
                straight[head, which].astype(jnp.float32).T.astype(jnp.bfloat16)
            )


def attend_kernel(turns, peers, seg_rows, tokens, reads, caches, turned_caches, received, *refs):
    returned, grads = refs[0], refs[1 : 1 + len(turns)]
    (
        straight,
        turned,
        inbox,
        outbox,
        scores,
        weights,
        dscores,
        sums,
        staged,
        owners,
        kv_sems,
        in_sems,
        out_sems,
        grad_sems,
    ) = refs[1 + len(turns) :]
    me = lax.axis_index("enc")
    base = lax.axis_index("seq") * peers
    slots = inbox.shape[1]
    padded = straight.shape[2]
    pieces = [(a, min(a + CHUNK, padded)) for a in range(0, padded, CHUNK)]
    lanes = GROUP * seg_rows
    f32, bf16 = jnp.float32, jnp.bfloat16

    kv_copies = [
        [
            pltpu.make_async_copy(source.at[head_at(turn)], target.at[i], kv_sems.at[i, j])
            for j, (source, target) in enumerate(((caches, straight), (turned_caches, turned)))
        ]
        for i, turn in enumerate(turns)
    ]

    def arriving(i, slot, owner):
        return pltpu.make_async_copy(
            received.at[owner, i], inbox.at[i, slot], in_sems.at[i, slot]
        )

    def leaving(i, slot, owner):
        return pltpu.make_async_copy(
            outbox.at[i, slot], returned.at[owner, i], out_sems.at[i, slot]
        )

    def handing(i):
        return pltpu.make_async_copy(staged.at[i], grads[i], grad_sems.at[i])

    for copy in kv_copies[0]:
        copy.start()
    count = jnp.int32(0)
    for k in range(peers):
        found = is_read(reads, base + k, me)

        @pl.when(found)
        def _():
            owners[count] = jnp.int32(k)
            arriving(0, count, k).start()

        count = count + found.astype(jnp.int32)
    for i in range(1, len(turns)):
        for copy in kv_copies[i]:
            copy.start()
        for slot in range(slots):

            @pl.when(slot < count)
            def _():
                arriving(i, slot, owners[slot]).start()

    sums[...] = jnp.zeros_like(sums)
    steps = count * len(turns)

    def place(step):
        return lax.div(step, count), lax.rem(step, count)

    def stacked(i, slot, which):
        return jnp.concatenate(
            [inbox[i, slot, which, :, h * HD : (h + 1) * HD] for h in range(GROUP)], axis=0
        )

    def store(i, slot, which, turned_value):
        value = turned_value.T.astype(bf16)
        for h in range(GROUP):
            outbox[i, slot, which, :, h * HD : (h + 1) * HD] = value[
                h * seg_rows : (h + 1) * seg_rows, :
            ]

    def masked(part, a, b, other):
        if b <= tokens:
            return part
        token = lax.broadcasted_iota(jnp.int32, part.shape, 0) + a
        return jnp.where(token < tokens, part, other)

    def await_step(step):
        i, slot = place(step)
        for head in range(len(turns)):

            @pl.when(step == head * count)
            def _():
                for copy in kv_copies[head]:
                    copy.wait()

        arriving(i, slot, 0).wait()

    def forward(i, slot):
        q, g = (stacked(i, slot, which).astype(f32).T for which in range(2))
        q_turned = q.astype(bf16)
        state = {"top": jnp.full((1, lanes), LOWEST, f32), "total": jnp.zeros((1, lanes), f32)}

        def score(a, b):
            part = jnp.dot(straight[i, 0, a:b, :], q_turned, preferred_element_type=f32)
            part = masked(part, a, b, LOWEST)
            scores[a:b, :] = part
            state["top"] = jnp.maximum(state["top"], jnp.max(part, axis=0, keepdims=True))

        def weigh(a, b):
            part = jnp.exp2((scores[a:b, :] - state["top"]) * (SCALE * LOG2E))
            state["total"] = state["total"] + jnp.sum(part, axis=0, keepdims=True)
            weights[a:b, :] = part.astype(bf16)

        def finish():
            out = jnp.dot(turned[i, 1], weights[...], preferred_element_type=f32)
            out = out * (1.0 / state["total"])
            store(i, slot, 0, out)
            delta = jnp.sum(g * out.astype(bf16).astype(f32), axis=0, keepdims=True)
            lse = state["top"] * (SCALE * LOG2E) + jnp.log2(state["total"])
            return lse, delta, q_turned, g.astype(bf16)

        parts = [functools.partial(score, a, b) for a, b in pieces]
        return parts + [functools.partial(weigh, a, b) for a, b in pieces], finish

    def backward(i, slot, lse, delta, q_turned, g_turned):
        q, g = stacked(i, slot, 0), stacked(i, slot, 1)

        def part(a, b):
            score = jnp.dot(straight[i, 0, a:b, :], q_turned, preferred_element_type=f32)
            prob = masked(jnp.exp2(score * (SCALE * LOG2E) - lse), a, b, 0.0)
            dprob = jnp.dot(straight[i, 1, a:b, :], g_turned, preferred_element_type=f32)
            dscore = (prob * (dprob - delta)).astype(bf16)
            dscores[a:b, :] = dscore
            sums[i, 0, a:b, :] += jnp.dot(dscore, q, preferred_element_type=f32)
            sums[i, 1, a:b, :] += jnp.dot(prob.astype(bf16), g, preferred_element_type=f32)

        def finish():
            turned_dq = jnp.dot(turned[i, 0], dscores[...], preferred_element_type=f32)
            store(i, slot, 1, turned_dq * SCALE)

        return [functools.partial(part, a, b) for a, b in pieces], finish

    def one_step(step, carry):
        i, slot = place(step)
        later = jnp.minimum(step + 1, steps - 1)

        @pl.when(step + 1 < steps)
        def _():
            await_step(step + 1)

        ahead, ahead_finish = forward(*place(later))
        behind, behind_finish = backward(i, slot, *carry)
        for j, part in enumerate(behind):
            for other in ahead[2 * j : 2 * j + 2]:
                other()
            part()
        behind_finish()
        carry = ahead_finish()
        leaving(i, slot, owners[slot]).start()

        @pl.when(slot == count - 1)
        def _():
            staged[i, 0] = (sums[i, 0] * SCALE).astype(bf16)
            staged[i, 1] = sums[i, 1].astype(bf16)
            for head in range(len(turns)):

                @pl.when(i == head)
                def _():
                    handing(head).start()

        return carry

    @pl.when(count > 0)
    def _():
        await_step(jnp.int32(0))
        first, first_finish = forward(0, 0)
        for part in first:
            part()
        lax.fori_loop(0, steps, one_step, first_finish())

    @pl.when(count == 0)
    def _():
        staged[...] = jnp.zeros_like(staged)
        for i in range(len(turns)):
            for copy in kv_copies[i]:
                copy.wait()
            handing(i).start()

    for i in range(len(turns)):
        for slot in range(slots):

            @pl.when(slot < count)
            def _():
                leaving(i, slot, 0).wait()

        handing(i).wait()


def xor_permute(array, axis, k):
    if k == 0:
        return array
    size = lax.axis_size(axis)
    return lax.ppermute(array, axis, [(i, i ^ k) for i in range(size)])


def per_device(queries, keys, values, reads, grad_out):
    peers = lax.axis_size("enc")
    n_seq = lax.axis_size("seq")
    n_seg = reads.shape[1]
    by_segment = reads.T
    seg_rows = queries.shape[0] // n_seg
    slots = min(peers, 3 * n_seg // 2)
    tokens = keys.shape[1]
    padded = (tokens + 15) // 16 * 16
    lanes = GROUP * seg_rows
    bf16, f32 = jnp.bfloat16, jnp.float32
    chunks = [tuple(range(i, i + PER_CHUNK)) for i in range(0, KVH, PER_CHUNK)]
    message = jax.ShapeDtypeStruct((peers, PER_CHUNK, 2, seg_rows, WIDTH), bf16)

    caches = [
        jax.ShapeDtypeStruct((KVH, 2, padded, HD), bf16),
        jax.ShapeDtypeStruct((KVH, 2, HD, padded), bf16),
    ]

    def route(turns, prepares):
        return pl.pallas_call(
            functools.partial(route_kernel, turns, n_seg, seg_rows, tokens),
            out_shape=[message] + caches * prepares,
            in_specs=[SMEM, HBM, HBM] + [VMEM] * 2 * prepares,
            out_specs=[ANY] + [VMEM] * 2 * prepares,
            scratch_shapes=[
                pltpu.VMEM((n_seg, PER_CHUNK, 2, seg_rows, WIDTH), bf16),
                pltpu.SemaphoreType.DMA((n_seg, PER_CHUNK, 2)),
                pltpu.SemaphoreType.DMA((n_seg,)),
            ],
            compiler_params=pltpu.CompilerParams(vmem_limit_bytes=VMEM_BYTES),
            cost_estimate=pl.CostEstimate(
                flops=0, bytes_accessed=(2 + 10 * prepares) << 20, transcendentals=0
            ),
            name=f"route_{turns[0]}",
        )(by_segment, queries, grad_out, *[keys, values] * prepares)

    def attend(turns, received):
        work = slots * lanes * tokens * HD * len(turns)
        results = pl.pallas_call(
            functools.partial(attend_kernel, turns, peers, seg_rows, tokens),
            out_shape=[message] + [jax.ShapeDtypeStruct((2, padded, HD), bf16)] * len(turns),
            in_specs=[SMEM] + [ANY] * 3,
            out_specs=[ANY] * (1 + len(turns)),
            scratch_shapes=[
                pltpu.VMEM((len(turns), 2, padded, HD), bf16),
                pltpu.VMEM((len(turns), 2, HD, padded), bf16),
                pltpu.VMEM((len(turns), slots, 2, seg_rows, WIDTH), bf16),
                pltpu.VMEM((len(turns), slots, 2, seg_rows, WIDTH), bf16),
                pltpu.VMEM((padded, lanes), f32),
                pltpu.VMEM((padded, lanes), bf16),
                pltpu.VMEM((padded, lanes), bf16),
                pltpu.VMEM((len(turns), 2, padded, HD), f32),
                pltpu.VMEM((len(turns), 2, padded, HD), bf16),
                pltpu.SMEM((slots,), jnp.int32),
                pltpu.SemaphoreType.DMA((len(turns), 2)),
                pltpu.SemaphoreType.DMA((len(turns), slots)),
                pltpu.SemaphoreType.DMA((len(turns), slots)),
                pltpu.SemaphoreType.DMA((len(turns),)),
            ],
            compiler_params=pltpu.CompilerParams(vmem_limit_bytes=VMEM_BYTES),
            cost_estimate=pl.CostEstimate(
                flops=24 * work, bytes_accessed=8 << 20, transcendentals=slots * lanes * tokens
            ),
            name=f"attend_{turns[0]}",
        )(by_segment, *prepared, received)
        return results[0], list(results[1:])

    def collect(returned):
        whole = jax.ShapeDtypeStruct(queries.shape, bf16)
        return pl.pallas_call(
            functools.partial(collect_kernel, chunks, n_seg, seg_rows),
            out_shape=[whole, whole],
            in_specs=[SMEM] + [ANY] * len(chunks),
            out_specs=[VMEM, VMEM],
            scratch_shapes=[pltpu.SemaphoreType.DMA((KVH, n_seg, 2))],
            compiler_params=pltpu.CompilerParams(vmem_limit_bytes=VMEM_BYTES),
            cost_estimate=pl.CostEstimate(flops=0, bytes_accessed=4 << 20, transcendentals=0),
            name="collect",
        )(by_segment, *returned)

    def exchange(array):
        return lax.all_to_all(array, "enc", split_axis=0, concat_axis=0, tiled=True)

    first, second = chunks
    routed, = route(first, 0)
    received = exchange(routed)
    routed, *prepared = route(second, 1)
    received, routed = lax.optimization_barrier((received, routed))
    received_later = exchange(routed)
    returned, grads = attend(first, received)
    answer = exchange(returned)
    passed = xor_permute(grads[0], "seq", 1)
    received_later, grads[1] = lax.optimization_barrier((received_later, grads[1]))
    returned, more = attend(second, received_later)
    grads += more
    if n_seq == KVH:
        pair = (grads[1].astype(f32) + passed.astype(f32)).astype(bf16)
        answer, returned, pair = lax.optimization_barrier((answer, returned, pair))
        pair = xor_permute(pair, "seq", 2)
        near = xor_permute(grads[2], "seq", 1)
    answers = [answer, exchange(returned)]
    attended, grad_queries = collect(answers)

    if n_seq == KVH:
        total = grads[3].astype(f32) + near.astype(f32) + pair.astype(f32)
        total = total.astype(bf16)[:, :tokens]
        return attended, grad_queries, total[0][None], total[1][None]
    joined = jnp.concatenate(grads, axis=2)[:, :tokens]
    summed = lax.psum_scatter(joined, "seq", scatter_dimension=2, tiled=True)
    return attended, grad_queries, summed[0][None], summed[1][None]


def solution(mesh):
    placed = (
        P(("seq", "enc"), None),
        P("enc", None, None),
        P("enc", None, None),
        P(),
        P(("seq", "enc"), None),
    )
    return jax.shard_map(
        per_device,
        mesh=mesh,
        in_specs=placed,
        out_specs=(
            P(("seq", "enc"), None),
            P(("seq", "enc"), None),
            P("enc", None, "seq"),
            P("enc", None, "seq"),
        ),
        check_vma=False,
    )
```

```python
import functools

import jax
import jax.numpy as jnp
from jax import lax
from jax.experimental import pallas as pl
from jax.experimental.pallas import tpu as pltpu
from jax.sharding import PartitionSpec as P

HQ = 32
KVH = 4
HD = 128
GROUP = HQ // KVH
WIDTH = GROUP * HD
SCALE = HD ** (-0.5)
LOG2E = 1.4426950408889634
CHUNK = 512
SLICE = 128
LOWEST = -3.0e38
PER_CHUNK = 2
VMEM_BYTES = 58 << 20
ANY = pl.BlockSpec(memory_space=pl.ANY)
SMEM = pl.BlockSpec(memory_space=pltpu.SMEM)
VMEM = pl.BlockSpec(memory_space=pltpu.VMEM)
HBM = pl.BlockSpec(memory_space=pltpu.HBM)


def head_at(turn):
    if lax.axis_size("seq") == KVH:
        return lax.axis_index("seq") ^ (KVH - 1 - turn)
    return turn


def route_kernel(turns, n_seg, seg_rows, tokens, reads, q_hbm, g_hbm, *refs):
    caches, (out, *prepared, stage, in_sems, out_sems) = refs[:-6], refs[-6:]
    if not caches:
        out, stage, in_sems, out_sems = refs
        prepared = ()
    row = lax.axis_index("seq") * lax.axis_size("enc") + lax.axis_index("enc")
    arriving = [[] for _ in range(n_seg)]
    for r in range(n_seg):
        rows = slice(r * seg_rows, (r + 1) * seg_rows)
        for i, turn in enumerate(turns):
            columns = pl.ds(pl.multiple_of(head_at(turn) * WIDTH, WIDTH), WIDTH)
            for which, source in enumerate((q_hbm, g_hbm)):
                arriving[r].append(
                    pltpu.make_async_copy(
                        source.at[rows, columns],
                        stage.at[r, i, which],
                        in_sems.at[r, i, which],
                    )
                )
    leaving = [
        pltpu.make_async_copy(stage.at[r], out.at[reads[r, row]], out_sems.at[r])
        for r in range(n_seg)
    ]
    for copies in arriving:
        for copy in copies:
            copy.start()
    for r, copies in enumerate(arriving):
        for copy in copies:
            copy.wait()
        leaving[r].start()
    if caches:
        prepare(tokens, *caches, *prepared)
    for copy in leaving:
        copy.wait()


def collect_kernel(turns, n_seg, seg_rows, reads, returned, *refs):
    o_hbm, dq_hbm, stage, in_sems, out_sems = refs[-5:]
    row = lax.axis_index("seq") * lax.axis_size("enc") + lax.axis_index("enc")
    arriving, leaving = [], []
    for i, turn in enumerate(turns):
        columns = pl.ds(pl.multiple_of(head_at(turn) * WIDTH, WIDTH), WIDTH)
        for which, target in enumerate((o_hbm, dq_hbm)):
            arriving.append(
                [
                    pltpu.make_async_copy(
                        returned.at[reads[r, row], i, which],
                        stage.at[i, which, r * seg_rows : (r + 1) * seg_rows, :],
                        in_sems.at[i, which, r],
                    )
                    for r in range(n_seg)
                ]
            )
            leaving.append(
                pltpu.make_async_copy(
                    stage.at[i, which], target.at[:, columns], out_sems.at[i, which]
                )
            )
    for copies in arriving:
        for copy in copies:
            copy.start()
    for copies, out in zip(arriving, leaving):
        for copy in copies:
            copy.wait()
        out.start()
    for out in leaving:
        out.wait()


def is_read(reads, row, image):
    found = jnp.int32(0)
    for r in range(reads.shape[0]):
        found = found + (reads[r, row] == image).astype(jnp.int32)
    return found > 0


def prepare(tokens, k_in, v_in, straight, turned):
    padded = straight.shape[2]
    whole = tokens // 16 * 16
    for which, source in enumerate((k_in, v_in)):
        for head in range(KVH):
            columns = slice(head * HD, (head + 1) * HD)
            straight[head, which, 0:whole, :] = source[0, 0:whole, columns]
            if whole < tokens:
                last = jnp.zeros((padded - tokens, HD), jnp.bfloat16)
                straight[head, which, whole:padded, :] = jnp.concatenate(
                    [source[0, whole:tokens, columns], last], axis=0
                )
            turned[head, which] = (
                straight[head, which].astype(jnp.float32).T.astype(jnp.bfloat16)
            )


def attend_kernel(turns, peers, seg_rows, tokens, reads, caches, turned_caches, received, *refs):
    returned, grads = refs[0], refs[1 : 1 + len(turns)]
    (
        straight,
        turned,
        inbox,
        outbox,
        scores,
        even,
        odd,
        dscores,
        sums,
        staged,
        owners,
        kv_sems,
        in_sems,
        out_sems,
        grad_sems,
    ) = refs[1 + len(turns) :]
    me = lax.axis_index("enc")
    base = lax.axis_index("seq") * peers
    slots = inbox.shape[1]
    padded = straight.shape[2]
    pieces = [(a, min(a + CHUNK, padded)) for a in range(0, padded, CHUNK)]
    lanes = GROUP * seg_rows
    f32, bf16 = jnp.float32, jnp.bfloat16

    kv_copies = [
        [
            pltpu.make_async_copy(source.at[head_at(turn)], target.at[i], kv_sems.at[i, j])
            for j, (source, target) in enumerate(((caches, straight), (turned_caches, turned)))
        ]
        for i, turn in enumerate(turns)
    ]

    def arriving(i, slot, owner):
        return pltpu.make_async_copy(
            received.at[owner, i], inbox.at[i, slot], in_sems.at[i, slot]
        )

    def leaving(i, slot, owner):
        return pltpu.make_async_copy(
            outbox.at[i, slot], returned.at[owner, i], out_sems.at[i, slot]
        )

    def handing(i):
        return pltpu.make_async_copy(staged.at[i], grads[i], grad_sems.at[i])

    for copy in kv_copies[0]:
        copy.start()
    count = jnp.int32(0)
    for k in range(peers):
        found = is_read(reads, base + k, me)

        @pl.when(found)
        def _():
            owners[count] = jnp.int32(k)
            arriving(0, count, k).start()

        count = count + found.astype(jnp.int32)
    for i in range(1, len(turns)):
        for copy in kv_copies[i]:
            copy.start()
        for slot in range(slots):

            @pl.when(slot < count)
            def _():
                arriving(i, slot, owners[slot]).start()

    sums[...] = jnp.zeros_like(sums)
    steps = count * len(turns)

    def place(step):
        return lax.div(step, count), lax.rem(step, count)

    def stacked(i, slot, which):
        return jnp.concatenate(
            [inbox[i, slot, which, :, h * HD : (h + 1) * HD] for h in range(GROUP)], axis=0
        )

    def store(i, slot, which, turned_value):
        value = turned_value.T.astype(bf16)
        for h in range(GROUP):
            outbox[i, slot, which, :, h * HD : (h + 1) * HD] = value[
                h * seg_rows : (h + 1) * seg_rows, :
            ]

    def await_step(step):
        i, slot = place(step)
        for head in range(len(turns)):

            @pl.when(step == head * count)
            def _():
                for copy in kv_copies[head]:
                    copy.wait()

        arriving(i, slot, 0).wait()

    def slices(a, b):
        return [(c, min(c + SLICE, b)) for c in range(a, b, SLICE)]

    def folded(value, reduce):
        return reduce(value.reshape(-1, 8, lanes), axis=0)

    def forward(i, slot, weights):
        q_turned = stacked(i, slot, 0).astype(f32).T.astype(bf16)
        tops, totals = [], []

        def score(a, b):
            part = jnp.dot(straight[i, 0, a:b, :], q_turned, preferred_element_type=f32)
            for c, d in slices(a, b):
                piece = part[c - a : d - a, :]
                if d > tokens:
                    token = lax.broadcasted_iota(jnp.int32, piece.shape, 0) + c
                    piece = jnp.where(token < tokens, piece, LOWEST)
                scores[c:d, :] = piece
                tops.append(folded(piece, jnp.max))

        def weigh(a, b):
            if a == 0:
                tops[:] = [jnp.max(functools.reduce(jnp.maximum, tops), axis=0, keepdims=True)]
            for c, d in slices(a, b):
                piece = jnp.exp2((scores[c:d, :] - tops[0]) * (SCALE * LOG2E))
                totals.append(folded(piece, jnp.sum))
                weights[c:d, :] = piece.astype(bf16)

        def finish():
            total = jnp.sum(functools.reduce(jnp.add, totals), axis=0, keepdims=True)
            inverse = 1.0 / total
            out = jnp.dot(turned[i, 1], weights[...], preferred_element_type=f32) * inverse
            store(i, slot, 0, out)
            g = (stacked(i, slot, 1).astype(f32).T * inverse).astype(bf16)
            exact = g.astype(f32)
            delta = jnp.sum(exact * out.astype(bf16).astype(f32), axis=0, keepdims=True)
            return delta, g, exact.T.astype(bf16)

        parts = [functools.partial(score, a, b) for a, b in pieces]
        return parts + [functools.partial(weigh, a, b) for a, b in pieces], finish

    def backward(i, slot, weights, delta, g_turned, g):
        q = stacked(i, slot, 0)

        def part(a, b):
            dprob = jnp.dot(straight[i, 1, a:b, :], g_turned, preferred_element_type=f32)
            for c, d in slices(a, b):
                piece = weights[c:d, :].astype(f32) * (dprob[c - a : d - a, :] - delta)
                dscores[c:d, :] = piece.astype(bf16)
            sums[i, 0, a:b, :] += jnp.dot(dscores[a:b, :], q, preferred_element_type=f32)
            sums[i, 1, a:b, :] += jnp.dot(weights[a:b, :], g, preferred_element_type=f32)

        def finish():
            turned_dq = jnp.dot(turned[i, 0], dscores[...], preferred_element_type=f32)
            store(i, slot, 1, turned_dq * SCALE)

        return [functools.partial(part, a, b) for a, b in pieces], finish

    def one_step(step, carry, weights, next_weights):
        i, slot = place(step)
        later = jnp.minimum(step + 1, steps - 1)

        @pl.when(step + 1 < steps)
        def _():
            await_step(step + 1)

        ahead, ahead_finish = forward(*place(later), next_weights)
        behind, behind_finish = backward(i, slot, weights, *carry)
        for j, part in enumerate(behind):
            for other in ahead[2 * j : 2 * j + 2]:
                other()
            part()
        behind_finish()
        carry = ahead_finish()
        leaving(i, slot, owners[slot]).start()

        @pl.when(slot == count - 1)
        def _():
            staged[i, 0] = (sums[i, 0] * SCALE).astype(bf16)
            staged[i, 1] = sums[i, 1].astype(bf16)
            for head in range(len(turns)):

                @pl.when(i == head)
                def _():
                    handing(head).start()

        return carry

    def two_steps(pair, carry):
        carry = one_step(2 * pair, carry, even, odd)
        return one_step(2 * pair + 1, carry, odd, even)

    @pl.when(count > 0)
    def _():
        await_step(jnp.int32(0))
        first, first_finish = forward(0, 0, even)
        for part in first:
            part()
        lax.fori_loop(0, steps // 2, two_steps, first_finish())

    @pl.when(count == 0)
    def _():
        staged[...] = jnp.zeros_like(staged)
        for i in range(len(turns)):
            for copy in kv_copies[i]:
                copy.wait()
            handing(i).start()

    for i in range(len(turns)):
        for slot in range(slots):

            @pl.when(slot < count)
            def _():
                leaving(i, slot, 0).wait()

        handing(i).wait()


def xor_permute(array, axis, k):
    if k == 0:
        return array
    size = lax.axis_size(axis)
    return lax.ppermute(array, axis, [(i, i ^ k) for i in range(size)])


def per_device(queries, keys, values, reads, grad_out):
    peers = lax.axis_size("enc")
    n_seq = lax.axis_size("seq")
    n_seg = reads.shape[1]
    by_segment = reads.T
    seg_rows = queries.shape[0] // n_seg
    slots = min(peers, 3 * n_seg // 2)
    tokens = keys.shape[1]
    padded = (tokens + 15) // 16 * 16
    lanes = GROUP * seg_rows
    bf16, f32 = jnp.bfloat16, jnp.float32
    chunks = [tuple(range(i, i + PER_CHUNK)) for i in range(0, KVH, PER_CHUNK)]
    message = jax.ShapeDtypeStruct((peers, PER_CHUNK, 2, seg_rows, WIDTH), bf16)

    caches = [
        jax.ShapeDtypeStruct((KVH, 2, padded, HD), bf16),
        jax.ShapeDtypeStruct((KVH, 2, HD, padded), bf16),
    ]

    def route(turns, prepares):
        return pl.pallas_call(
            functools.partial(route_kernel, turns, n_seg, seg_rows, tokens),
            out_shape=[message] + caches * prepares,
            in_specs=[SMEM, HBM, HBM] + [VMEM] * 2 * prepares,
            out_specs=[ANY] + [VMEM] * 2 * prepares,
            scratch_shapes=[
                pltpu.VMEM((n_seg, PER_CHUNK, 2, seg_rows, WIDTH), bf16),
                pltpu.SemaphoreType.DMA((n_seg, PER_CHUNK, 2)),
                pltpu.SemaphoreType.DMA((n_seg,)),
            ],
            compiler_params=pltpu.CompilerParams(vmem_limit_bytes=VMEM_BYTES),
            cost_estimate=pl.CostEstimate(
                flops=0, bytes_accessed=(2 + 10 * prepares) << 20, transcendentals=0
            ),
            name=f"route_{turns[0]}",
        )(by_segment, queries, grad_out, *[keys, values] * prepares)

    def attend(turns, received):
        work = slots * lanes * tokens * HD * len(turns)
        results = pl.pallas_call(
            functools.partial(attend_kernel, turns, peers, seg_rows, tokens),
            out_shape=[message] + [jax.ShapeDtypeStruct((2, padded, HD), bf16)] * len(turns),
            in_specs=[SMEM] + [ANY] * 3,
            out_specs=[ANY] * (1 + len(turns)),
            scratch_shapes=[
                pltpu.VMEM((len(turns), 2, padded, HD), bf16),
                pltpu.VMEM((len(turns), 2, HD, padded), bf16),
                pltpu.VMEM((len(turns), slots, 2, seg_rows, WIDTH), bf16),
                pltpu.VMEM((len(turns), slots, 2, seg_rows, WIDTH), bf16),
                pltpu.VMEM((padded, lanes), f32),
                pltpu.VMEM((padded, lanes), bf16),
                pltpu.VMEM((padded, lanes), bf16),
                pltpu.VMEM((padded, lanes), bf16),
                pltpu.VMEM((len(turns), 2, padded, HD), f32),
                pltpu.VMEM((len(turns), 2, padded, HD), bf16),
                pltpu.SMEM((slots,), jnp.int32),
                pltpu.SemaphoreType.DMA((len(turns), 2)),
                pltpu.SemaphoreType.DMA((len(turns), slots)),
                pltpu.SemaphoreType.DMA((len(turns), slots)),
                pltpu.SemaphoreType.DMA((len(turns),)),
            ],
            compiler_params=pltpu.CompilerParams(vmem_limit_bytes=VMEM_BYTES),
            cost_estimate=pl.CostEstimate(
                flops=12 * work, bytes_accessed=8 << 20, transcendentals=slots * lanes * tokens
            ),
            name=f"attend_{turns[0]}",
        )(by_segment, *prepared, received)
        return results[0], list(results[1:])

    def collect(turns, returned, before):
        whole = jax.ShapeDtypeStruct(queries.shape, bf16)
        return pl.pallas_call(
            functools.partial(collect_kernel, turns, n_seg, seg_rows),
            out_shape=[whole, whole],
            in_specs=[SMEM, ANY] + [ANY] * len(before),
            out_specs=[ANY, ANY],
            input_output_aliases={2: 0, 3: 1} if before else {},
            scratch_shapes=[
                pltpu.VMEM((PER_CHUNK, 2, n_seg * seg_rows, WIDTH), bf16),
                pltpu.SemaphoreType.DMA((PER_CHUNK, 2, n_seg)),
                pltpu.SemaphoreType.DMA((PER_CHUNK, 2)),
            ],
            compiler_params=pltpu.CompilerParams(vmem_limit_bytes=VMEM_BYTES),
            cost_estimate=pl.CostEstimate(flops=0, bytes_accessed=4 << 20, transcendentals=0),
            name=f"collect_{turns[0]}",
        )(by_segment, returned, *before)

    def exchange(array):
        return lax.all_to_all(array, "enc", split_axis=0, concat_axis=0, tiled=True)

    first, second = chunks
    routed, = route(first, 0)
    received = exchange(routed)
    routed, *prepared = route(second, 1)
    received, routed = lax.optimization_barrier((received, routed))
    received_later = exchange(routed)
    returned, grads = attend(first, received)
    answer = exchange(returned)
    passed = xor_permute(grads[0], "seq", 1)
    received_later, grads[1] = lax.optimization_barrier((received_later, grads[1]))
    returned, more = attend(second, received_later)
    grads += more
    answer, returned = lax.optimization_barrier((answer, returned))
    answer_later = exchange(returned)
    if n_seq == KVH:
        passed, grads[1], grads[2] = lax.optimization_barrier((passed, grads[1], grads[2]))
        pair = (grads[1].astype(f32) + passed.astype(f32)).astype(bf16)
        pair = xor_permute(pair, "seq", 2)
        near = xor_permute(grads[2], "seq", 1)
    half = collect(first, answer, [])
    attended, grad_queries = collect(second, answer_later, half)

    if n_seq == KVH:
        total = grads[3].astype(f32) + near.astype(f32) + pair.astype(f32)
        total = total.astype(bf16)[:, :tokens]
        return attended, grad_queries, total[0][None], total[1][None]
    joined = jnp.concatenate(grads, axis=2)[:, :tokens]
    summed = lax.psum_scatter(joined, "seq", scatter_dimension=2, tiled=True)
    return attended, grad_queries, summed[0][None], summed[1][None]


def solution(mesh):
    placed = (
        P(("seq", "enc"), None),
        P("enc", None, None),
        P("enc", None, None),
        P(),
        P(("seq", "enc"), None),
    )
    return jax.shard_map(
        per_device,
        mesh=mesh,
        in_specs=placed,
        out_specs=(
            P(("seq", "enc"), None),
            P(("seq", "enc"), None),
            P("enc", None, "seq"),
            P("enc", None, "seq"),
        ),
        check_vma=False,
    )
```

```python
import functools

import jax
import jax.numpy as jnp
from jax import lax
from jax.experimental import pallas as pl
from jax.experimental.pallas import tpu as pltpu
from jax.sharding import PartitionSpec as P

HQ = 32
KVH = 4
HD = 128
GROUP = HQ // KVH
WIDTH = GROUP * HD
SCALE = HD ** (-0.5)
LOG2E = 1.4426950408889634
CHUNK = 512
SLICE = 128
LOWEST = -3.0e38
PER_CHUNK = 2
VMEM_BYTES = 58 << 20
ANY = pl.BlockSpec(memory_space=pl.ANY)
SMEM = pl.BlockSpec(memory_space=pltpu.SMEM)
VMEM = pl.BlockSpec(memory_space=pltpu.VMEM)
HBM = pl.BlockSpec(memory_space=pltpu.HBM)


def head_at(turn):
    if lax.axis_size("seq") == KVH:
        return lax.axis_index("seq") ^ (KVH - 1 - turn)
    return turn


def route_kernel(turns, n_seg, seg_rows, tokens, reads, q_hbm, g_hbm, *refs):
    caches, (out, *prepared, stage, in_sems, out_sems) = refs[:-6], refs[-6:]
    if not caches:
        out, stage, in_sems, out_sems = refs
        prepared = ()
    row = lax.axis_index("seq") * lax.axis_size("enc") + lax.axis_index("enc")
    arriving = [[] for _ in range(n_seg)]
    for r in range(n_seg):
        rows = slice(r * seg_rows, (r + 1) * seg_rows)
        for i, turn in enumerate(turns):
            columns = pl.ds(pl.multiple_of(head_at(turn) * WIDTH, WIDTH), WIDTH)
            for which, source in enumerate((q_hbm, g_hbm)):
                arriving[r].append(
                    pltpu.make_async_copy(
                        source.at[rows, columns],
                        stage.at[r, i, which],
                        in_sems.at[r, i, which],
                    )
                )
    leaving = [
        pltpu.make_async_copy(stage.at[r], out.at[reads[r, row]], out_sems.at[r])
        for r in range(n_seg)
    ]
    for copies in arriving:
        for copy in copies:
            copy.start()
    for r, copies in enumerate(arriving):
        for copy in copies:
            copy.wait()
        leaving[r].start()
    if caches:
        prepare(tokens, *caches, *prepared)
    for copy in leaving:
        copy.wait()


def collect_kernel(turns, n_seg, seg_rows, reads, returned, *refs):
    o_hbm, dq_hbm, stage, in_sems, out_sems = refs[-5:]
    row = lax.axis_index("seq") * lax.axis_size("enc") + lax.axis_index("enc")
    arriving, leaving = [], []
    for i, turn in enumerate(turns):
        columns = pl.ds(pl.multiple_of(head_at(turn) * WIDTH, WIDTH), WIDTH)
        for which, target in enumerate((o_hbm, dq_hbm)):
            arriving.append(
                [
                    pltpu.make_async_copy(
                        returned.at[reads[r, row], i, which],
                        stage.at[i, which, r * seg_rows : (r + 1) * seg_rows, :],
                        in_sems.at[i, which, r],
                    )
                    for r in range(n_seg)
                ]
            )
            leaving.append(
                pltpu.make_async_copy(
                    stage.at[i, which], target.at[:, columns], out_sems.at[i, which]
                )
            )
    for copies in arriving:
        for copy in copies:
            copy.start()
    for copies, out in zip(arriving, leaving):
        for copy in copies:
            copy.wait()
        out.start()
    for out in leaving:
        out.wait()


def is_read(reads, row, image):
    found = jnp.int32(0)
    for r in range(reads.shape[0]):
        found = found + (reads[r, row] == image).astype(jnp.int32)
    return found > 0


def prepare(tokens, k_in, v_in, straight, turned):
    padded = straight.shape[2]
    whole = tokens // 16 * 16
    for which, source in enumerate((k_in, v_in)):
        for head in range(KVH):
            columns = slice(head * HD, (head + 1) * HD)
            straight[head, which, 0:whole, :] = source[0, 0:whole, columns]
            if whole < tokens:
                last = jnp.zeros((padded - tokens, HD), jnp.bfloat16)
                straight[head, which, whole:padded, :] = jnp.concatenate(
                    [source[0, whole:tokens, columns], last], axis=0
                )
            turned[head, which] = (
                straight[head, which].astype(jnp.float32).T.astype(jnp.bfloat16)
            )


def attend_kernel(turns, peers, seg_rows, tokens, reads, caches, turned_caches, received, *refs):
    returned, grads = refs[0], refs[1 : 1 + len(turns)]
    (
        straight,
        turned,
        inbox,
        outbox,
        scores,
        even_odd,
        dscores,
        sums,
        staged,
        owners,
        kv_sems,
        in_sems,
        out_sems,
        grad_sems,
    ) = refs[1 + len(turns) :]
    me = lax.axis_index("enc")
    base = lax.axis_index("seq") * peers
    slots = inbox.shape[1]
    padded = straight.shape[2]
    pieces = [(a, min(a + CHUNK, padded)) for a in range(0, padded, CHUNK)]
    lanes = GROUP * seg_rows
    f32, bf16 = jnp.float32, jnp.bfloat16

    kv_copies = [
        [
            pltpu.make_async_copy(source.at[head_at(turn)], target.at[i], kv_sems.at[i, j])
            for j, (source, target) in enumerate(((caches, straight), (turned_caches, turned)))
        ]
        for i, turn in enumerate(turns)
    ]

    def arriving(i, slot, owner):
        return pltpu.make_async_copy(
            received.at[owner, i], inbox.at[i, slot], in_sems.at[i, slot]
        )

    def leaving(i, slot, owner):
        return pltpu.make_async_copy(
            outbox.at[i, slot], returned.at[owner, i], out_sems.at[i, slot]
        )

    def handing(i):
        return pltpu.make_async_copy(staged.at[i], grads[i], grad_sems.at[i])

    for j in range(2):
        for copies in kv_copies:
            copies[j].start()
    count = jnp.int32(0)
    for k in range(peers):
        found = is_read(reads, base + k, me)

        @pl.when(found)
        def _():
            owners[count] = jnp.int32(k)
            for i in range(len(turns)):
                arriving(i, count, k).start()

        count = count + found.astype(jnp.int32)

    sums[...] = jnp.zeros_like(sums)

    def stacked(i, slot, which):
        return jnp.concatenate(
            [inbox[i, slot, which, :, h * HD : (h + 1) * HD] for h in range(GROUP)], axis=0
        )

    def store(i, slot, which, turned_value):
        value = turned_value.T.astype(bf16)
        for h in range(GROUP):
            outbox[i, slot, which, :, h * HD : (h + 1) * HD] = value[
                h * seg_rows : (h + 1) * seg_rows, :
            ]

    def slices(a, b):
        return [(c, min(c + SLICE, b)) for c in range(a, b, SLICE)]

    def folded(value, reduce):
        return reduce(value.reshape(-1, 8, lanes), axis=0)

    def forward(i, slot, weights):
        q_turned = stacked(i, slot, 0).astype(f32).T.astype(bf16)
        tops, totals, outs = [], [], []

        def score(a, b):
            part = jnp.dot(straight[i, 0, a:b, :], q_turned, preferred_element_type=f32)
            for c, d in slices(a, b):
                piece = part[c - a : d - a, :]
                if d > tokens:
                    token = lax.broadcasted_iota(jnp.int32, piece.shape, 0) + c
                    piece = jnp.where(token < tokens, piece, LOWEST)
                scores[i, c:d, :] = piece
                tops.append(folded(piece, jnp.max))

        def weigh(a, b):
            if a == 0:
                tops[:] = [jnp.max(functools.reduce(jnp.maximum, tops), axis=0, keepdims=True)]
            for c, d in slices(a, b):
                piece = jnp.exp2((scores[i, c:d, :] - tops[0]) * (SCALE * LOG2E))
                totals.append(folded(piece, jnp.sum))
                weights[i, c:d, :] = piece.astype(bf16)
            outs.append(
                jnp.dot(turned[i, 1, :, a:b], weights[i, a:b, :], preferred_element_type=f32)
            )

        def finish():
            total = jnp.sum(functools.reduce(jnp.add, totals), axis=0, keepdims=True)
            inverse = 1.0 / total
            out = functools.reduce(jnp.add, outs) * inverse
            store(i, slot, 0, out)
            g = (stacked(i, slot, 1).astype(f32).T * inverse).astype(bf16)
            exact = g.astype(f32)
            delta = jnp.sum(exact * out.astype(bf16).astype(f32), axis=0, keepdims=True)
            return delta, g, exact.T.astype(bf16)

        return score, weigh, finish

    def backward(i, slot, weights, delta, g_turned, g):
        q = stacked(i, slot, 0)
        turned_dq = []

        def values_part(a, b):
            dprob = jnp.dot(straight[i, 1, a:b, :], g_turned, preferred_element_type=f32)
            for c, d in slices(a, b):
                piece = weights[i, c:d, :].astype(f32) * (dprob[c - a : d - a, :] - delta)
                dscores[i, c:d, :] = piece.astype(bf16)
            sums[i, 1, a:b, :] += jnp.dot(weights[i, a:b, :], g, preferred_element_type=f32)

        def keys_part(a, b):
            sums[i, 0, a:b, :] += jnp.dot(dscores[i, a:b, :], q, preferred_element_type=f32)
            turned_dq.append(
                jnp.dot(turned[i, 0, :, a:b], dscores[i, a:b, :], preferred_element_type=f32)
            )

        def finish():
            store(i, slot, 1, functools.reduce(jnp.add, turned_dq) * SCALE)

        return values_part, keys_part, finish

    heads = range(len(turns))

    def one_slot(slot, carry):
        later = jnp.minimum(slot + 1, count - 1)

        @pl.when(slot + 1 < count)
        def _():
            for i in heads:
                arriving(i, later, 0).wait()

        weights, next_weights = even_odd.at[slot & 1], even_odd.at[(slot + 1) & 1]
        ahead = [forward(i, later, next_weights) for i in heads]
        behind = [backward(i, slot, weights, *carry[i]) for i in heads]
        for phase in range(2):
            for a, b in pieces:
                for i in heads:
                    ahead[i][phase](a, b)
                    behind[i][phase](a, b)
        for i in heads:
            behind[i][2]()
        carry = [ahead[i][2]() for i in heads]
        for i in heads:
            leaving(i, slot, owners[slot]).start()
        return carry

    @pl.when(count > 0)
    def _():
        for i in heads:
            arriving(i, 0, 0).wait()
            kv_copies[i][0].wait()
        first = [forward(i, 0, even_odd.at[0]) for i in heads]
        for phase in range(2):
            if phase == 1:
                for i in heads:
                    kv_copies[i][1].wait()
            for a, b in pieces:
                for i in heads:
                    first[i][phase](a, b)
        lax.fori_loop(0, count, one_slot, [first[i][2]() for i in heads])
        for i in heads:
            staged[i, 0] = (sums[i, 0] * SCALE).astype(bf16)
            staged[i, 1] = sums[i, 1].astype(bf16)
            handing(i).start()

    @pl.when(count == 0)
    def _():
        staged[...] = jnp.zeros_like(staged)
        for i in range(len(turns)):
            for copy in kv_copies[i]:
                copy.wait()
            handing(i).start()

    for i in range(len(turns)):
        for slot in range(slots):

            @pl.when(slot < count)
            def _():
                leaving(i, slot, 0).wait()

        handing(i).wait()


def xor_permute(array, axis, k):
    if k == 0:
        return array
    size = lax.axis_size(axis)
    return lax.ppermute(array, axis, [(i, i ^ k) for i in range(size)])


def per_device(queries, keys, values, reads, grad_out):
    peers = lax.axis_size("enc")
    n_seq = lax.axis_size("seq")
    n_seg = reads.shape[1]
    by_segment = reads.T
    seg_rows = queries.shape[0] // n_seg
    slots = min(peers, 3 * n_seg // 2)
    tokens = keys.shape[1]
    padded = (tokens + 15) // 16 * 16
    lanes = GROUP * seg_rows
    bf16, f32 = jnp.bfloat16, jnp.float32
    chunks = [tuple(range(i, i + PER_CHUNK)) for i in range(0, KVH, PER_CHUNK)]
    message = jax.ShapeDtypeStruct((peers, PER_CHUNK, 2, seg_rows, WIDTH), bf16)

    caches = [
        jax.ShapeDtypeStruct((KVH, 2, padded, HD), bf16),
        jax.ShapeDtypeStruct((KVH, 2, HD, padded), bf16),
    ]

    def route(turns, prepares):
        return pl.pallas_call(
            functools.partial(route_kernel, turns, n_seg, seg_rows, tokens),
            out_shape=[message] + caches * prepares,
            in_specs=[SMEM, HBM, HBM] + [VMEM] * 2 * prepares,
            out_specs=[ANY] + [VMEM] * 2 * prepares,
            scratch_shapes=[
                pltpu.VMEM((n_seg, PER_CHUNK, 2, seg_rows, WIDTH), bf16),
                pltpu.SemaphoreType.DMA((n_seg, PER_CHUNK, 2)),
                pltpu.SemaphoreType.DMA((n_seg,)),
            ],
            compiler_params=pltpu.CompilerParams(vmem_limit_bytes=VMEM_BYTES),
            cost_estimate=pl.CostEstimate(
                flops=0, bytes_accessed=(2 + 10 * prepares) << 20, transcendentals=0
            ),
            name=f"route_{turns[0]}",
        )(by_segment, queries, grad_out, *[keys, values] * prepares)

    def attend(turns, received):
        work = slots * lanes * tokens * HD * len(turns)
        results = pl.pallas_call(
            functools.partial(attend_kernel, turns, peers, seg_rows, tokens),
            out_shape=[message] + [jax.ShapeDtypeStruct((2, padded, HD), bf16)] * len(turns),
            in_specs=[SMEM] + [ANY] * 3,
            out_specs=[ANY] * (1 + len(turns)),
            scratch_shapes=[
                pltpu.VMEM((len(turns), 2, padded, HD), bf16),
                pltpu.VMEM((len(turns), 2, HD, padded), bf16),
                pltpu.VMEM((len(turns), slots, 2, seg_rows, WIDTH), bf16),
                pltpu.VMEM((len(turns), slots, 2, seg_rows, WIDTH), bf16),
                pltpu.VMEM((len(turns), padded, lanes), f32),
                pltpu.VMEM((2, len(turns), padded, lanes), bf16),
                pltpu.VMEM((len(turns), padded, lanes), bf16),
                pltpu.VMEM((len(turns), 2, padded, HD), f32),
                pltpu.VMEM((len(turns), 2, padded, HD), bf16),
                pltpu.SMEM((slots,), jnp.int32),
                pltpu.SemaphoreType.DMA((len(turns), 2)),
                pltpu.SemaphoreType.DMA((len(turns), slots)),
                pltpu.SemaphoreType.DMA((len(turns), slots)),
                pltpu.SemaphoreType.DMA((len(turns),)),
            ],
            compiler_params=pltpu.CompilerParams(vmem_limit_bytes=VMEM_BYTES),
            cost_estimate=pl.CostEstimate(
                flops=12 * work, bytes_accessed=8 << 20, transcendentals=slots * lanes * tokens
            ),
            name=f"attend_{turns[0]}",
        )(by_segment, *prepared, received)
        return results[0], list(results[1:])

    def collect(turns, returned, before):
        whole = jax.ShapeDtypeStruct(queries.shape, bf16)
        return pl.pallas_call(
            functools.partial(collect_kernel, turns, n_seg, seg_rows),
            out_shape=[whole, whole],
            in_specs=[SMEM, ANY] + [ANY] * len(before),
            out_specs=[ANY, ANY],
            input_output_aliases={2: 0, 3: 1} if before else {},
            scratch_shapes=[
                pltpu.VMEM((PER_CHUNK, 2, n_seg * seg_rows, WIDTH), bf16),
                pltpu.SemaphoreType.DMA((PER_CHUNK, 2, n_seg)),
                pltpu.SemaphoreType.DMA((PER_CHUNK, 2)),
            ],
            compiler_params=pltpu.CompilerParams(vmem_limit_bytes=VMEM_BYTES),
            cost_estimate=pl.CostEstimate(flops=0, bytes_accessed=4 << 20, transcendentals=0),
            name=f"collect_{turns[0]}",
        )(by_segment, returned, *before)

    def exchange(array):
        return lax.all_to_all(array, "enc", split_axis=0, concat_axis=0, tiled=True)

    first, second = chunks
    routed, = route(first, 0)
    received = exchange(routed)
    routed, *prepared = route(second, 1)
    received, routed = lax.optimization_barrier((received, routed))
    received_later = exchange(routed)
    returned, grads = attend(first, received)
    answer = exchange(returned)
    passed = xor_permute(grads[0], "seq", 1)
    received_later, grads[1] = lax.optimization_barrier((received_later, grads[1]))
    returned, more = attend(second, received_later)
    grads += more
    answer, returned = lax.optimization_barrier((answer, returned))
    answer_later = exchange(returned)
    if n_seq == KVH:
        passed, grads[1], grads[2] = lax.optimization_barrier((passed, grads[1], grads[2]))
        pair = (grads[1].astype(f32) + passed.astype(f32)).astype(bf16)
        pair = xor_permute(pair, "seq", 2)
        near = xor_permute(grads[2], "seq", 1)
    half = collect(first, answer, [])
    attended, grad_queries = collect(second, answer_later, half)

    if n_seq == KVH:
        total = grads[3].astype(f32) + near.astype(f32) + pair.astype(f32)
        total = total.astype(bf16)[:, :tokens]
        return attended, grad_queries, total[0][None], total[1][None]
    joined = jnp.concatenate(grads, axis=2)[:, :tokens]
    summed = lax.psum_scatter(joined, "seq", scatter_dimension=2, tiled=True)
    return attended, grad_queries, summed[0][None], summed[1][None]


def solution(mesh):
    placed = (
        P(("seq", "enc"), None),
        P("enc", None, None),
        P("enc", None, None),
        P(),
        P(("seq", "enc"), None),
    )
    return jax.shard_map(
        per_device,
        mesh=mesh,
        in_specs=placed,
        out_specs=(
            P(("seq", "enc"), None),
            P(("seq", "enc"), None),
            P("enc", None, "seq"),
            P("enc", None, "seq"),
        ),
        check_vma=False,
    )
```

```python
import functools

import jax
import jax.numpy as jnp
from jax import lax
from jax.experimental import pallas as pl
from jax.experimental.pallas import tpu as pltpu
from jax.sharding import PartitionSpec as P

HQ = 32
KVH = 4
HD = 128
GROUP = HQ // KVH
WIDTH = GROUP * HD
SCALE = HD ** (-0.5)
LOG2E = 1.4426950408889634
CHUNK = 512
SLICE = 128
LOWEST = -3.0e38
PER_CHUNK = 2
VMEM_BYTES = 58 << 20
ANY = pl.BlockSpec(memory_space=pl.ANY)
SMEM = pl.BlockSpec(memory_space=pltpu.SMEM)
VMEM = pl.BlockSpec(memory_space=pltpu.VMEM)
HBM = pl.BlockSpec(memory_space=pltpu.HBM)


def head_at(turn):
    if lax.axis_size("seq") == KVH:
        return lax.axis_index("seq") ^ (KVH - 1 - turn)
    return turn


def route_kernel(turns, n_seg, seg_rows, tokens, reads, q_hbm, g_hbm, *refs):
    caches, (out, *prepared, stage, in_sems, out_sems) = refs[:-6], refs[-6:]
    if not caches:
        out, stage, in_sems, out_sems = refs
        prepared = ()
    row = lax.axis_index("seq") * lax.axis_size("enc") + lax.axis_index("enc")
    arriving = [[] for _ in range(n_seg)]
    for r in range(n_seg):
        rows = slice(r * seg_rows, (r + 1) * seg_rows)
        for i, turn in enumerate(turns):
            columns = pl.ds(pl.multiple_of(head_at(turn) * WIDTH, WIDTH), WIDTH)
            for which, source in enumerate((q_hbm, g_hbm)):
                arriving[r].append(
                    pltpu.make_async_copy(
                        source.at[rows, columns],
                        stage.at[r, i, which],
                        in_sems.at[r, i, which],
                    )
                )
    leaving = [
        pltpu.make_async_copy(stage.at[r], out.at[reads[r, row]], out_sems.at[r])
        for r in range(n_seg)
    ]
    for copies in arriving:
        for copy in copies:
            copy.start()
    for r, copies in enumerate(arriving):
        for copy in copies:
            copy.wait()
        leaving[r].start()
    if caches:
        prepare(tokens, *caches, *prepared)
    for copy in leaving:
        copy.wait()


def collect_kernel(turns, n_seg, seg_rows, reads, returned, *refs):
    o_hbm, dq_hbm, stage, in_sems, out_sems = refs[-5:]
    row = lax.axis_index("seq") * lax.axis_size("enc") + lax.axis_index("enc")
    arriving, leaving = [], []
    for i, turn in enumerate(turns):
        columns = pl.ds(pl.multiple_of(head_at(turn) * WIDTH, WIDTH), WIDTH)
        for which, target in enumerate((o_hbm, dq_hbm)):
            arriving.append(
                [
                    pltpu.make_async_copy(
                        returned.at[reads[r, row], i, which],
                        stage.at[i, which, r * seg_rows : (r + 1) * seg_rows, :],
                        in_sems.at[i, which, r],
                    )
                    for r in range(n_seg)
                ]
            )
            leaving.append(
                pltpu.make_async_copy(
                    stage.at[i, which], target.at[:, columns], out_sems.at[i, which]
                )
            )
    for copies in arriving:
        for copy in copies:
            copy.start()
    for copies, out in zip(arriving, leaving):
        for copy in copies:
            copy.wait()
        out.start()
    for out in leaving:
        out.wait()


def is_read(reads, row, image):
    found = jnp.int32(0)
    for r in range(reads.shape[0]):
        found = found + (reads[r, row] == image).astype(jnp.int32)
    return found > 0


def prepare(tokens, k_in, v_in, straight, turned):
    padded = straight.shape[2]
    whole = tokens // 16 * 16
    for which, source in enumerate((k_in, v_in)):
        for head in range(KVH):
            columns = slice(head * HD, (head + 1) * HD)
            straight[head, which, 0:whole, :] = source[0, 0:whole, columns]
            if whole < tokens:
                last = jnp.zeros((padded - tokens, HD), jnp.bfloat16)
                straight[head, which, whole:padded, :] = jnp.concatenate(
                    [source[0, whole:tokens, columns], last], axis=0
                )
            turned[head, which] = (
                straight[head, which].astype(jnp.float32).T.astype(jnp.bfloat16)
            )


def attend_kernel(turns, peers, seg_rows, tokens, reads, caches, turned_caches, received, *refs):
    returned, grads = refs[0], refs[1 : 1 + len(turns)]
    (
        straight,
        turned,
        inbox,
        outbox,
        scores,
        even_odd,
        dscores,
        sums,
        staged,
        owners,
        kv_sems,
        in_sems,
        out_sems,
        grad_sems,
    ) = refs[1 + len(turns) :]
    me = lax.axis_index("enc")
    base = lax.axis_index("seq") * peers
    slots = inbox.shape[1]
    padded = straight.shape[2]
    pieces = [(a, min(a + CHUNK, padded)) for a in range(0, padded, CHUNK)]
    lanes = GROUP * seg_rows
    f32, bf16 = jnp.float32, jnp.bfloat16

    kv_copies = [
        [
            pltpu.make_async_copy(
                source.at[head_at(turn), which], target.at[i, which], kv_sems.at[i, j]
            )
            for j, (source, target, which) in enumerate(
                (
                    (caches, straight, 0),
                    (turned_caches, turned, 1),
                    (caches, straight, 1),
                    (turned_caches, turned, 0),
                )
            )
        ]
        for i, turn in enumerate(turns)
    ]

    def arriving(i, slot, owner):
        return pltpu.make_async_copy(
            received.at[owner, i], inbox.at[i, slot], in_sems.at[i, slot]
        )

    def leaving(i, slot, owner):
        return pltpu.make_async_copy(
            outbox.at[i, slot], returned.at[owner, i], out_sems.at[i, slot]
        )

    def handing(i):
        return pltpu.make_async_copy(staged.at[i], grads[i], grad_sems.at[i])

    for copies in kv_copies:
        copies[0].start()
    count = jnp.int32(0)
    for k in range(peers):
        found = is_read(reads, base + k, me)

        @pl.when(found)
        def _():
            owners[count] = jnp.int32(k)
            for i in range(len(turns)):
                arriving(i, count, k).start()

        count = count + found.astype(jnp.int32)
    for j in range(1, 4):
        for copies in kv_copies:
            copies[j].start()

    sums[...] = jnp.zeros_like(sums)

    def stacked(i, slot, which):
        return jnp.concatenate(
            [inbox[i, slot, which, :, h * HD : (h + 1) * HD] for h in range(GROUP)], axis=0
        )

    def store(i, slot, which, turned_value):
        value = turned_value.T.astype(bf16)
        for h in range(GROUP):
            outbox[i, slot, which, :, h * HD : (h + 1) * HD] = value[
                h * seg_rows : (h + 1) * seg_rows, :
            ]

    def slices(a, b):
        return [(c, min(c + SLICE, b)) for c in range(a, b, SLICE)]

    def folded(value, reduce):
        return reduce(value.reshape(-1, 8, lanes), axis=0)

    def forward(i, slot, weights):
        q_turned = stacked(i, slot, 0).astype(f32).T.astype(bf16)
        tops, totals, outs = [], [], []

        def score():
            part = jnp.dot(straight[i, 0], q_turned, preferred_element_type=f32)
            for c, d in slices(0, padded):
                piece = part[c:d, :]
                if d > tokens:
                    token = lax.broadcasted_iota(jnp.int32, piece.shape, 0) + c
                    piece = jnp.where(token < tokens, piece, LOWEST)
                scores[i, c:d, :] = piece
                tops.append(folded(piece, jnp.max))

        def weigh(a, b):
            if a == 0:
                tops[:] = [jnp.max(functools.reduce(jnp.maximum, tops), axis=0, keepdims=True)]
            for c, d in slices(a, b):
                piece = jnp.exp2((scores[i, c:d, :] - tops[0]) * (SCALE * LOG2E))
                totals.append(folded(piece, jnp.sum))
                weights[i, c:d, :] = piece.astype(bf16)
            outs.append(
                jnp.dot(turned[i, 1, :, a:b], weights[i, a:b, :], preferred_element_type=f32)
            )

        def finish():
            total = jnp.sum(functools.reduce(jnp.add, totals), axis=0, keepdims=True)
            inverse = 1.0 / total
            out = functools.reduce(jnp.add, outs) * inverse
            store(i, slot, 0, out)
            g = (stacked(i, slot, 1).astype(f32).T * inverse).astype(bf16)
            exact = g.astype(f32)
            delta = jnp.sum(exact * out.astype(bf16).astype(f32), axis=0, keepdims=True)
            return delta, g, exact.T.astype(bf16)

        return score, weigh, finish

    def backward(i, slot, weights, delta, g_turned, g):
        q = stacked(i, slot, 0)
        turned_dq = []

        def values_part(a, b):
            dprob = jnp.dot(straight[i, 1, a:b, :], g_turned, preferred_element_type=f32)
            for c, d in slices(a, b):
                piece = weights[i, c:d, :].astype(f32) * (dprob[c - a : d - a, :] - delta)
                dscores[i, c:d, :] = piece.astype(bf16)

        def values_sum():
            sums[i, 1] += jnp.dot(weights[i], g, preferred_element_type=f32)

        def keys_sum():
            sums[i, 0] += jnp.dot(dscores[i], q, preferred_element_type=f32)

        def queries_part(a, b):
            turned_dq.append(
                jnp.dot(turned[i, 0, :, a:b], dscores[i, a:b, :], preferred_element_type=f32)
            )

        def finish():
            store(i, slot, 1, functools.reduce(jnp.add, turned_dq) * SCALE)

        return values_part, values_sum, keys_sum, queries_part, finish

    heads = range(len(turns))

    def one_slot(slot, carry, last=False):
        weights, next_weights = even_odd.at[slot & 1], even_odd.at[(slot + 1) & 1]
        behind = [backward(i, slot, weights, *carry[i]) for i in heads]
        ahead = []
        if not last:
            for i in heads:
                arriving(i, slot + 1, 0).wait()
            ahead = [forward(i, slot + 1, next_weights) for i in heads]

        for score, _, _ in ahead:
            score()
        for a, b in pieces:
            for values_part, *_ in behind:
                values_part(a, b)
        for _, values_sum, keys_sum, _, _ in behind:
            values_sum()
            keys_sum()
        for a, b in pieces:
            for _, weigh, _ in ahead:
                weigh(a, b)
            for _, _, _, queries_part, _ in behind:
                queries_part(a, b)
        for *_, finish in behind:
            finish()
        carry = [finish() for _, _, finish in ahead]
        for i in heads:
            leaving(i, slot, owners[slot]).start()
        return carry

    @pl.when(count > 0)
    def _():
        for i in heads:
            arriving(i, 0, 0).wait()
            kv_copies[i][0].wait()
        first = [forward(i, 0, even_odd.at[0]) for i in heads]
        for score, _, _ in first:
            score()
        for i in heads:
            kv_copies[i][1].wait()
        for a, b in pieces:
            for _, weigh, _ in first:
                weigh(a, b)
        carry = [finish() for _, _, finish in first]
        for i in heads:
            kv_copies[i][2].wait()
            kv_copies[i][3].wait()
        carry = lax.fori_loop(0, count - 1, one_slot, carry)
        one_slot(count - 1, carry, last=True)
        for i in heads:
            staged[i, 0] = (sums[i, 0] * SCALE).astype(bf16)
            staged[i, 1] = sums[i, 1].astype(bf16)
            handing(i).start()

    @pl.when(count == 0)
    def _():
        staged[...] = jnp.zeros_like(staged)
        for i in range(len(turns)):
            for copy in kv_copies[i]:
                copy.wait()
            handing(i).start()

    for i in range(len(turns)):
        for slot in range(slots):

            @pl.when(slot < count)
            def _():
                leaving(i, slot, 0).wait()

        handing(i).wait()


def xor_permute(array, axis, k):
    if k == 0:
        return array
    size = lax.axis_size(axis)
    return lax.ppermute(array, axis, [(i, i ^ k) for i in range(size)])


def per_device(queries, keys, values, reads, grad_out):
    peers = lax.axis_size("enc")
    n_seq = lax.axis_size("seq")
    n_seg = reads.shape[1]
    by_segment = reads.T
    seg_rows = queries.shape[0] // n_seg
    slots = min(peers, 3 * n_seg // 2)
    tokens = keys.shape[1]
    padded = (tokens + 15) // 16 * 16
    lanes = GROUP * seg_rows
    bf16, f32 = jnp.bfloat16, jnp.float32
    chunks = [tuple(range(i, i + PER_CHUNK)) for i in range(0, KVH, PER_CHUNK)]
    message = jax.ShapeDtypeStruct((peers, PER_CHUNK, 2, seg_rows, WIDTH), bf16)

    caches = [
        jax.ShapeDtypeStruct((KVH, 2, padded, HD), bf16),
        jax.ShapeDtypeStruct((KVH, 2, HD, padded), bf16),
    ]

    def route(turns, prepares):
        return pl.pallas_call(
            functools.partial(route_kernel, turns, n_seg, seg_rows, tokens),
            out_shape=[message] + caches * prepares,
            in_specs=[SMEM, HBM, HBM] + [VMEM] * 2 * prepares,
            out_specs=[ANY] + [VMEM] * 2 * prepares,
            scratch_shapes=[
                pltpu.VMEM((n_seg, PER_CHUNK, 2, seg_rows, WIDTH), bf16),
                pltpu.SemaphoreType.DMA((n_seg, PER_CHUNK, 2)),
                pltpu.SemaphoreType.DMA((n_seg,)),
            ],
            compiler_params=pltpu.CompilerParams(vmem_limit_bytes=VMEM_BYTES),
            cost_estimate=pl.CostEstimate(
                flops=0, bytes_accessed=(2 + 10 * prepares) << 20, transcendentals=0
            ),
            name=f"route_{turns[0]}",
        )(by_segment, queries, grad_out, *[keys, values] * prepares)

    def attend(turns, received):
        work = slots * lanes * tokens * HD * len(turns)
        results = pl.pallas_call(
            functools.partial(attend_kernel, turns, peers, seg_rows, tokens),
            out_shape=[message] + [jax.ShapeDtypeStruct((2, padded, HD), bf16)] * len(turns),
            in_specs=[SMEM] + [ANY] * 3,
            out_specs=[ANY] * (1 + len(turns)),
            scratch_shapes=[
                pltpu.VMEM((len(turns), 2, padded, HD), bf16),
                pltpu.VMEM((len(turns), 2, HD, padded), bf16),
                pltpu.VMEM((len(turns), slots, 2, seg_rows, WIDTH), bf16),
                pltpu.VMEM((len(turns), slots, 2, seg_rows, WIDTH), bf16),
                pltpu.VMEM((len(turns), padded, lanes), f32),
                pltpu.VMEM((2, len(turns), padded, lanes), bf16),
                pltpu.VMEM((len(turns), padded, lanes), bf16),
                pltpu.VMEM((len(turns), 2, padded, HD), f32),
                pltpu.VMEM((len(turns), 2, padded, HD), bf16),
                pltpu.SMEM((slots,), jnp.int32),
                pltpu.SemaphoreType.DMA((len(turns), 4)),
                pltpu.SemaphoreType.DMA((len(turns), slots)),
                pltpu.SemaphoreType.DMA((len(turns), slots)),
                pltpu.SemaphoreType.DMA((len(turns),)),
            ],
            compiler_params=pltpu.CompilerParams(vmem_limit_bytes=VMEM_BYTES),
            cost_estimate=pl.CostEstimate(
                flops=12 * work, bytes_accessed=8 << 20, transcendentals=slots * lanes * tokens
            ),
            name=f"attend_{turns[0]}",
        )(by_segment, *prepared, received)
        return results[0], list(results[1:])

    def collect(turns, returned, before):
        whole = jax.ShapeDtypeStruct(queries.shape, bf16)
        return pl.pallas_call(
            functools.partial(collect_kernel, turns, n_seg, seg_rows),
            out_shape=[whole, whole],
            in_specs=[SMEM, ANY] + [ANY] * len(before),
            out_specs=[ANY, ANY],
            input_output_aliases={2: 0, 3: 1} if before else {},
            scratch_shapes=[
                pltpu.VMEM((PER_CHUNK, 2, n_seg * seg_rows, WIDTH), bf16),
                pltpu.SemaphoreType.DMA((PER_CHUNK, 2, n_seg)),
                pltpu.SemaphoreType.DMA((PER_CHUNK, 2)),
            ],
            compiler_params=pltpu.CompilerParams(vmem_limit_bytes=VMEM_BYTES),
            cost_estimate=pl.CostEstimate(flops=0, bytes_accessed=4 << 20, transcendentals=0),
            name=f"collect_{turns[0]}",
        )(by_segment, returned, *before)

    def exchange(array):
        return lax.all_to_all(array, "enc", split_axis=0, concat_axis=0, tiled=True)

    first, second = chunks
    routed, = route(first, 0)
    received = exchange(routed)
    routed, *prepared = route(second, 1)
    received, routed = lax.optimization_barrier((received, routed))
    received_later = exchange(routed)
    returned, grads = attend(first, received)
    answer = exchange(returned)
    passed = xor_permute(grads[0], "seq", 1)
    received_later, grads[1] = lax.optimization_barrier((received_later, grads[1]))
    returned, more = attend(second, received_later)
    grads += more
    answer, returned = lax.optimization_barrier((answer, returned))
    answer_later = exchange(returned)
    if n_seq == KVH:
        passed, grads[1], grads[2] = lax.optimization_barrier((passed, grads[1], grads[2]))
        pair = (grads[1].astype(f32) + passed.astype(f32)).astype(bf16)
        pair = xor_permute(pair, "seq", 2)
        near = xor_permute(grads[2], "seq", 1)
    half = collect(first, answer, [])
    attended, grad_queries = collect(second, answer_later, half)

    if n_seq == KVH:
        total = grads[3].astype(f32) + near.astype(f32) + pair.astype(f32)
        total = total.astype(bf16)[:, :tokens]
        return attended, grad_queries, total[0][None], total[1][None]
    joined = jnp.concatenate(grads, axis=2)[:, :tokens]
    summed = lax.psum_scatter(joined, "seq", scatter_dimension=2, tiled=True)
    return attended, grad_queries, summed[0][None], summed[1][None]


def solution(mesh):
    placed = (
        P(("seq", "enc"), None),
        P("enc", None, None),
        P("enc", None, None),
        P(),
        P(("seq", "enc"), None),
    )
    return jax.shard_map(
        per_device,
        mesh=mesh,
        in_specs=placed,
        out_specs=(
            P(("seq", "enc"), None),
            P(("seq", "enc"), None),
            P("enc", None, "seq"),
            P("enc", None, "seq"),
        ),
        check_vma=False,
    )
```

```python
import functools

import jax
import jax.numpy as jnp
from jax import lax
from jax.experimental import pallas as pl
from jax.experimental.pallas import tpu as pltpu
from jax.sharding import PartitionSpec as P

HQ = 32
KVH = 4
HD = 128
GROUP = HQ // KVH
WIDTH = GROUP * HD
SCALE = HD ** (-0.5)
LOG2E = 1.4426950408889634
CHUNK = 512
SLICE = 128
LOWEST = -3.0e38
PER_CHUNK = 2
VMEM_BYTES = 54 << 20
ANY = pl.BlockSpec(memory_space=pl.ANY)
SMEM = pl.BlockSpec(memory_space=pltpu.SMEM)
VMEM = pl.BlockSpec(memory_space=pltpu.VMEM)


def head_at(turn):
    if lax.axis_size("seq") == KVH:
        return lax.axis_index("seq") ^ (KVH - 1 - turn)
    return turn


def route_kernel(turns, n_seg, seg_rows, tokens, reads, q_hbm, g_hbm, *refs):
    stage, in_sems, out_sems = refs[-3:]
    apart = len(refs) > 8
    me = lax.axis_index("enc")
    row = lax.axis_index("seq") * lax.axis_size("enc") + me
    arriving = [[] for _ in range(n_seg)]
    for r in range(n_seg):
        rows = slice(r * seg_rows, (r + 1) * seg_rows)
        for i, turn in enumerate(turns):
            columns = pl.ds(pl.multiple_of(head_at(turn) * WIDTH, WIDTH), WIDTH)
            for which, source in enumerate((q_hbm, g_hbm)):
                arriving[r].append(
                    pltpu.make_async_copy(
                        source.at[rows, columns],
                        stage.at[r, i, which],
                        in_sems.at[r, i, which],
                    )
                )

    def leaving(r, target):
        return pltpu.make_async_copy(stage.at[r], target, out_sems.at[r])

    for copies in arriving:
        for copy in copies:
            copy.start()
    for r, copies in enumerate(arriving):
        for copy in copies:
            copy.wait()
        if apart:
            for k, out in enumerate(refs[:-3]):

                @pl.when(reads[r, row] == me ^ k)
                def _():
                    leaving(r, out).start()

        else:
            leaving(r, refs[2].at[reads[r, row]]).start()
    if not apart:
        k_in, v_in, _, straight, turned = refs[:5]
        prepare(tokens, k_in, v_in, straight, turned)
    for r in range(n_seg):
        leaving(r, refs[0] if apart else refs[2].at[0]).wait()


def collect_kernel(turns, n_seg, seg_rows, reads, returned, *refs):
    o_hbm, dq_hbm, stage, in_sems, out_sems = refs[-5:]
    row = lax.axis_index("seq") * lax.axis_size("enc") + lax.axis_index("enc")
    arriving, leaving = [], []
    for i, turn in enumerate(turns):
        columns = pl.ds(pl.multiple_of(head_at(turn) * WIDTH, WIDTH), WIDTH)
        for which, target in enumerate((o_hbm, dq_hbm)):
            arriving.append(
                [
                    pltpu.make_async_copy(
                        returned.at[reads[r, row], i, which],
                        stage.at[i, which, r * seg_rows : (r + 1) * seg_rows, :],
                        in_sems.at[i, which, r],
                    )
                    for r in range(n_seg)
                ]
            )
            leaving.append(
                pltpu.make_async_copy(
                    stage.at[i, which], target.at[:, columns], out_sems.at[i, which]
                )
            )
    for copies in arriving:
        for copy in copies:
            copy.start()
    for copies, out in zip(arriving, leaving):
        for copy in copies:
            copy.wait()
        out.start()
    for out in leaving:
        out.wait()


def is_read(reads, row, image):
    found = jnp.int32(0)
    for r in range(reads.shape[0]):
        found = found + (reads[r, row] == image).astype(jnp.int32)
    return found > 0


def prepare(tokens, k_in, v_in, straight, turned):
    padded = straight.shape[2]
    whole = tokens // 16 * 16
    for which, source in enumerate((k_in, v_in)):
        for head in range(KVH):
            columns = slice(head * HD, (head + 1) * HD)
            straight[head, which, 0:whole, :] = source[0, 0:whole, columns]
            if whole < tokens:
                last = jnp.zeros((padded - tokens, HD), jnp.bfloat16)
                straight[head, which, whole:padded, :] = jnp.concatenate(
                    [source[0, whole:tokens, columns], last], axis=0
                )
            turned[head, which] = (
                straight[head, which].astype(jnp.float32).T.astype(jnp.bfloat16)
            )


def attend_kernel(turns, peers, seg_rows, tokens, reads, caches, turned_caches, *refs):
    received, refs = refs[: len(refs) - 15 - len(turns)], refs[len(refs) - 15 - len(turns) :]
    returned, grads = refs[0], refs[1 : 1 + len(turns)]
    (
        straight,
        turned,
        inbox,
        outbox,
        scores,
        even_odd,
        dscores,
        sums,
        staged,
        owners,
        kv_sems,
        in_sems,
        out_sems,
        grad_sems,
    ) = refs[1 + len(turns) :]
    me = lax.axis_index("enc")
    base = lax.axis_index("seq") * peers
    slots = inbox.shape[1]
    padded = straight.shape[2]
    pieces = [(a, min(a + CHUNK, padded)) for a in range(0, padded, CHUNK)]
    lanes = GROUP * seg_rows
    f32, bf16 = jnp.float32, jnp.bfloat16

    kv_copies = [
        [
            pltpu.make_async_copy(
                source.at[head_at(turn), which], target.at[i, which], kv_sems.at[i, j]
            )
            for j, (source, target, which) in enumerate(
                (
                    (caches, straight, 0),
                    (turned_caches, turned, 1),
                    (caches, straight, 1),
                    (turned_caches, turned, 0),
                )
            )
        ]
        for i, turn in enumerate(turns)
    ]

    def arriving(i, slot, k):
        source = received[k] if len(received) > 1 else received[0].at[me ^ k]
        return pltpu.make_async_copy(source.at[i], inbox.at[i, slot], in_sems.at[i, slot])

    def leaving(i, slot, owner):
        return pltpu.make_async_copy(
            outbox.at[i, slot], returned.at[owner, i], out_sems.at[i, slot]
        )

    def handing(i):
        return pltpu.make_async_copy(staged.at[i], grads[i], grad_sems.at[i])

    for copies in kv_copies:
        copies[0].start()
    count = jnp.int32(0)
    for k in range(peers):
        found = is_read(reads, base + (me ^ k), me)

        @pl.when(found)
        def _():
            owners[count] = me ^ k
            for i in range(len(turns)):
                arriving(i, count, k).start()

        count = count + found.astype(jnp.int32)
    for j in range(1, 4):
        for copies in kv_copies:
            copies[j].start()

    sums[...] = jnp.zeros_like(sums)

    def stacked(i, slot, which):
        return jnp.concatenate(
            [inbox[i, slot, which, :, h * HD : (h + 1) * HD] for h in range(GROUP)], axis=0
        )

    def store(i, slot, which, turned_value):
        value = turned_value.T.astype(bf16)
        for h in range(GROUP):
            outbox[i, slot, which, :, h * HD : (h + 1) * HD] = value[
                h * seg_rows : (h + 1) * seg_rows, :
            ]

    def slices(a, b):
        return [(c, min(c + SLICE, b)) for c in range(a, b, SLICE)]

    def folded(value, reduce):
        return reduce(value.reshape(-1, 8, lanes), axis=0)

    def forward(i, slot, weights):
        q_turned = stacked(i, slot, 0).astype(f32).T.astype(bf16)
        tops, totals, outs = [], [], []

        def score():
            part = jnp.dot(straight[i, 0], q_turned, preferred_element_type=f32)
            for c, d in slices(0, padded):
                piece = part[c:d, :]
                if d > tokens:
                    token = lax.broadcasted_iota(jnp.int32, piece.shape, 0) + c
                    piece = jnp.where(token < tokens, piece, LOWEST)
                scores[i, c:d, :] = piece
                tops.append(folded(piece, jnp.max))

        def weigh(a, b):
            if a == 0:
                tops[:] = [jnp.max(functools.reduce(jnp.maximum, tops), axis=0, keepdims=True)]
            for c, d in slices(a, b):
                piece = jnp.exp2((scores[i, c:d, :] - tops[0]) * (SCALE * LOG2E))
                totals.append(folded(piece, jnp.sum))
                weights[i, c:d, :] = piece.astype(bf16)
            outs.append(
                jnp.dot(turned[i, 1, :, a:b], weights[i, a:b, :], preferred_element_type=f32)
            )

        def finish():
            total = jnp.sum(functools.reduce(jnp.add, totals), axis=0, keepdims=True)
            inverse = 1.0 / total
            out = functools.reduce(jnp.add, outs) * inverse
            store(i, slot, 0, out)
            g = (stacked(i, slot, 1).astype(f32).T * inverse).astype(bf16)
            exact = g.astype(f32)
            delta = jnp.sum(exact * out.astype(bf16).astype(f32), axis=0, keepdims=True)
            return delta, g, exact.T.astype(bf16)

        return score, weigh, finish

    def backward(i, slot, weights, delta, g_turned, g):
        q = stacked(i, slot, 0)
        turned_dq = []

        def values_part(a, b):
            dprob = jnp.dot(straight[i, 1, a:b, :], g_turned, preferred_element_type=f32)
            for c, d in slices(a, b):
                piece = weights[i, c:d, :].astype(f32) * (dprob[c - a : d - a, :] - delta)
                dscores[i, c:d, :] = piece.astype(bf16)

        def values_sum():
            sums[i, 1] += jnp.dot(weights[i], g, preferred_element_type=f32)

        def keys_sum():
            sums[i, 0] += jnp.dot(dscores[i], q, preferred_element_type=f32)

        def queries_part(a, b):
            turned_dq.append(
                jnp.dot(turned[i, 0, :, a:b], dscores[i, a:b, :], preferred_element_type=f32)
            )

        def finish():
            store(i, slot, 1, functools.reduce(jnp.add, turned_dq) * SCALE)

        return values_part, values_sum, keys_sum, queries_part, finish

    heads = range(len(turns))

    def one_slot(slot, carry, last=False):
        weights, next_weights = even_odd.at[slot & 1], even_odd.at[(slot + 1) & 1]
        behind = [backward(i, slot, weights, *carry[i]) for i in heads]
        ahead = []
        if not last:
            for i in heads:
                arriving(i, slot + 1, 0).wait()
            ahead = [forward(i, slot + 1, next_weights) for i in heads]

        for score, _, _ in ahead:
            score()
        for a, b in pieces:
            for values_part, *_ in behind:
                values_part(a, b)
        for _, values_sum, keys_sum, _, _ in behind:
            values_sum()
            keys_sum()
        for a, b in pieces:
            for _, weigh, _ in ahead:
                weigh(a, b)
            for _, _, _, queries_part, _ in behind:
                queries_part(a, b)
        for *_, finish in behind:
            finish()
        carry = [finish() for _, _, finish in ahead]
        for i in heads:
            leaving(i, slot, owners[slot]).start()
        return carry

    @pl.when(count > 0)
    def _():
        for i in heads:
            arriving(i, 0, 0).wait()
            kv_copies[i][0].wait()
        first = [forward(i, 0, even_odd.at[0]) for i in heads]
        for score, _, _ in first:
            score()
        for i in heads:
            kv_copies[i][1].wait()
        for a, b in pieces:
            for _, weigh, _ in first:
                weigh(a, b)
        carry = [finish() for _, _, finish in first]
        for i in heads:
            kv_copies[i][2].wait()
            kv_copies[i][3].wait()
        carry = lax.fori_loop(0, count - 1, one_slot, carry)
        one_slot(count - 1, carry, last=True)
        for i in heads:
            staged[i, 0] = (sums[i, 0] * SCALE).astype(bf16)
            staged[i, 1] = sums[i, 1].astype(bf16)
            handing(i).start()

    @pl.when(count == 0)
    def _():
        staged[...] = jnp.zeros_like(staged)
        for i in range(len(turns)):
            for copy in kv_copies[i]:
                copy.wait()
            handing(i).start()

    for i in range(len(turns)):
        for slot in range(slots):

            @pl.when(slot < count)
            def _():
                leaving(i, slot, 0).wait()

        handing(i).wait()


def xor_permute(array, axis, k):
    if k == 0:
        return array
    size = lax.axis_size(axis)
    return lax.ppermute(array, axis, [(i, i ^ k) for i in range(size)])


def per_device(queries, keys, values, reads, grad_out):
    peers = lax.axis_size("enc")
    n_seq = lax.axis_size("seq")
    n_seg = reads.shape[1]
    by_segment = reads.T
    seg_rows = queries.shape[0] // n_seg
    slots = min(peers, 3 * n_seg // 2)
    tokens = keys.shape[1]
    padded = (tokens + 15) // 16 * 16
    lanes = GROUP * seg_rows
    bf16, f32 = jnp.bfloat16, jnp.float32
    chunks = [tuple(range(i, i + PER_CHUNK)) for i in range(0, KVH, PER_CHUNK)]
    message = jax.ShapeDtypeStruct((peers, PER_CHUNK, 2, seg_rows, WIDTH), bf16)
    part = jax.ShapeDtypeStruct((PER_CHUNK, 2, seg_rows, WIDTH), bf16)

    caches = [
        jax.ShapeDtypeStruct((KVH, 2, padded, HD), bf16),
        jax.ShapeDtypeStruct((KVH, 2, HD, padded), bf16),
    ]

    def route(turns, prepares):
        outputs = [message] + caches if prepares else [part] * peers
        return pl.pallas_call(
            functools.partial(route_kernel, turns, n_seg, seg_rows, tokens),
            out_shape=outputs,
            in_specs=[SMEM, ANY, ANY] + [VMEM] * 2 * prepares,
            out_specs=[ANY, VMEM, VMEM] if prepares else [ANY] * peers,
            scratch_shapes=[
                pltpu.VMEM((n_seg, PER_CHUNK, 2, seg_rows, WIDTH), bf16),
                pltpu.SemaphoreType.DMA((n_seg, PER_CHUNK, 2)),
                pltpu.SemaphoreType.DMA((n_seg,)),
            ],
            compiler_params=pltpu.CompilerParams(vmem_limit_bytes=VMEM_BYTES),
            cost_estimate=pl.CostEstimate(
                flops=0, bytes_accessed=(2 + 10 * prepares) << 20, transcendentals=0
            ),
            name=f"route_{turns[0]}",
        )(by_segment, queries, grad_out, *[keys, values] * prepares)

    def attend(turns, received):
        work = slots * lanes * tokens * HD * len(turns)
        results = pl.pallas_call(
            functools.partial(attend_kernel, turns, peers, seg_rows, tokens),
            out_shape=[message] + [jax.ShapeDtypeStruct((2, padded, HD), bf16)] * len(turns),
            in_specs=[SMEM] + [ANY] * (2 + len(received)),
            out_specs=[ANY] * (1 + len(turns)),
            scratch_shapes=[
                pltpu.VMEM((len(turns), 2, padded, HD), bf16),
                pltpu.VMEM((len(turns), 2, HD, padded), bf16),
                pltpu.VMEM((len(turns), slots, 2, seg_rows, WIDTH), bf16),
                pltpu.VMEM((len(turns), slots, 2, seg_rows, WIDTH), bf16),
                pltpu.VMEM((len(turns), padded, lanes), f32),
                pltpu.VMEM((2, len(turns), padded, lanes), bf16),
                pltpu.VMEM((len(turns), padded, lanes), bf16),
                pltpu.VMEM((len(turns), 2, padded, HD), f32),
                pltpu.VMEM((len(turns), 2, padded, HD), bf16),
                pltpu.SMEM((slots,), jnp.int32),
                pltpu.SemaphoreType.DMA((len(turns), 4)),
                pltpu.SemaphoreType.DMA((len(turns), slots)),
                pltpu.SemaphoreType.DMA((len(turns), slots)),
                pltpu.SemaphoreType.DMA((len(turns),)),
            ],
            compiler_params=pltpu.CompilerParams(vmem_limit_bytes=VMEM_BYTES),
            cost_estimate=pl.CostEstimate(
                flops=12 * work, bytes_accessed=8 << 20, transcendentals=slots * lanes * tokens
            ),
            name=f"attend_{turns[0]}",
        )(by_segment, *prepared, *received)
        return results[0], list(results[1:])

    def collect(turns, returned, before):
        whole = jax.ShapeDtypeStruct(queries.shape, bf16)
        return pl.pallas_call(
            functools.partial(collect_kernel, turns, n_seg, seg_rows),
            out_shape=[whole, whole],
            in_specs=[SMEM, ANY] + [ANY] * len(before),
            out_specs=[ANY, ANY],
            input_output_aliases={2: 0, 3: 1} if before else {},
            scratch_shapes=[
                pltpu.VMEM((PER_CHUNK, 2, n_seg * seg_rows, WIDTH), bf16),
                pltpu.SemaphoreType.DMA((PER_CHUNK, 2, n_seg)),
                pltpu.SemaphoreType.DMA((PER_CHUNK, 2)),
            ],
            compiler_params=pltpu.CompilerParams(vmem_limit_bytes=VMEM_BYTES),
            cost_estimate=pl.CostEstimate(flops=0, bytes_accessed=4 << 20, transcendentals=0),
            name=f"collect_{turns[0]}",
        )(by_segment, returned, *before)

    def exchange(array):
        return lax.all_to_all(array, "enc", split_axis=0, concat_axis=0, tiled=True)

    first, second = chunks
    received = [xor_permute(array, "enc", k) for k, array in enumerate(route(first, 0))]
    routed, *prepared = route(second, 1)
    *received, routed = lax.optimization_barrier((*received, routed))
    received_later = exchange(routed)
    returned, grads = attend(first, received)
    answer = exchange(returned)
    if n_seq == KVH:
        far = [xor_permute(grads[0], "seq", 3), xor_permute(grads[1], "seq", 2)]
    received_later, grads[1] = lax.optimization_barrier((received_later, grads[1]))
    returned, more = attend(second, [received_later])
    answer, returned = lax.optimization_barrier((answer, returned))
    answer_later = exchange(returned)
    if n_seq == KVH:
        near = xor_permute(more[0], "seq", 1)
    half = collect(first, answer, [])
    attended, grad_queries = collect(second, answer_later, half)

    if n_seq == KVH:
        total = more[1].astype(f32) + near.astype(f32) + far[0].astype(f32) + far[1].astype(f32)
        total = total.astype(bf16)[:, :tokens]
        return attended, grad_queries, total[0][None], total[1][None]
    grads += more
    joined = jnp.concatenate(grads, axis=2)[:, :tokens]
    summed = lax.psum_scatter(joined, "seq", scatter_dimension=2, tiled=True)
    return attended, grad_queries, summed[0][None], summed[1][None]


def solution(mesh):
    placed = (
        P(("seq", "enc"), None),
        P("enc", None, None),
        P("enc", None, None),
        P(),
        P(("seq", "enc"), None),
    )
    return jax.shard_map(
        per_device,
        mesh=mesh,
        in_specs=placed,
        out_specs=(
            P(("seq", "enc"), None),
            P(("seq", "enc"), None),
            P("enc", None, "seq"),
            P("enc", None, "seq"),
        ),
        check_vma=False,
    )
```

```python
import functools

import jax
import jax.numpy as jnp
from jax import lax
from jax.experimental import pallas as pl
from jax.experimental.pallas import tpu as pltpu
from jax.sharding import PartitionSpec as P

HQ = 32
KVH = 4
HD = 128
GROUP = HQ // KVH
WIDTH = GROUP * HD
SCALE = HD ** (-0.5)
LOG2E = 1.4426950408889634
CHUNK = 512
SLICE = 128
LOWEST = -3.0e38
PER_CHUNK = 2
VMEM_BYTES = 58 << 20
ANY = pl.BlockSpec(memory_space=pl.ANY)
SMEM = pl.BlockSpec(memory_space=pltpu.SMEM)
VMEM = pl.BlockSpec(memory_space=pltpu.VMEM)


def head_at(turn):
    if lax.axis_size("seq") == KVH:
        return lax.axis_index("seq") ^ (KVH - 1 - turn)
    return turn


def route_kernel(turns, n_seg, seg_rows, tokens, reads, q_hbm, g_hbm, *refs):
    stage, in_sems, out_sems = refs[-3:]
    apart = len(refs) > 8
    me = lax.axis_index("enc")
    row = lax.axis_index("seq") * lax.axis_size("enc") + me
    arriving = [[] for _ in range(n_seg)]
    for r in range(n_seg):
        rows = slice(r * seg_rows, (r + 1) * seg_rows)
        for i, turn in enumerate(turns):
            columns = pl.ds(pl.multiple_of(head_at(turn) * WIDTH, WIDTH), WIDTH)
            for which, source in enumerate((q_hbm, g_hbm)):
                arriving[r].append(
                    pltpu.make_async_copy(
                        source.at[rows, columns],
                        stage.at[r, i, which],
                        in_sems.at[r, i, which],
                    )
                )

    def leaving(r, target):
        return pltpu.make_async_copy(stage.at[r], target, out_sems.at[r])

    for copies in arriving:
        for copy in copies:
            copy.start()
    for r, copies in enumerate(arriving):
        for copy in copies:
            copy.wait()
        if apart:
            for k, out in enumerate(refs[:-3]):

                @pl.when(reads[r, row] == me ^ k)
                def _():
                    leaving(r, out).start()

        else:
            leaving(r, refs[2].at[reads[r, row]]).start()
    if not apart:
        k_in, v_in, _, straight, turned = refs[:5]
        prepare(tokens, k_in, v_in, straight, turned)
    for r in range(n_seg):
        leaving(r, refs[0] if apart else refs[2].at[0]).wait()


def collect_kernel(turns, n_seg, seg_rows, reads, returned, *refs):
    o_hbm, dq_hbm, stage, in_sems, out_sems = refs[-5:]
    row = lax.axis_index("seq") * lax.axis_size("enc") + lax.axis_index("enc")
    arriving, leaving = [], []
    for i, turn in enumerate(turns):
        columns = pl.ds(pl.multiple_of(head_at(turn) * WIDTH, WIDTH), WIDTH)
        for which, target in enumerate((o_hbm, dq_hbm)):
            arriving.append(
                [
                    pltpu.make_async_copy(
                        returned.at[reads[r, row], i, which],
                        stage.at[i, which, r * seg_rows : (r + 1) * seg_rows, :],
                        in_sems.at[i, which, r],
                    )
                    for r in range(n_seg)
                ]
            )
            leaving.append(
                pltpu.make_async_copy(
                    stage.at[i, which], target.at[:, columns], out_sems.at[i, which]
                )
            )
    for copies in arriving:
        for copy in copies:
            copy.start()
    for copies, out in zip(arriving, leaving):
        for copy in copies:
            copy.wait()
        out.start()
    for out in leaving:
        out.wait()


def is_read(reads, row, image):
    found = jnp.int32(0)
    for r in range(reads.shape[0]):
        found = found + (reads[r, row] == image).astype(jnp.int32)
    return found > 0


def prepare(tokens, k_in, v_in, straight, turned):
    padded = straight.shape[2]
    whole = tokens // 16 * 16
    for which, source in enumerate((k_in, v_in)):
        for head in range(KVH):
            columns = slice(head * HD, (head + 1) * HD)
            straight[head, which, 0:whole, :] = source[0, 0:whole, columns]
            if whole < tokens:
                last = jnp.zeros((padded - tokens, HD), jnp.bfloat16)
                straight[head, which, whole:padded, :] = jnp.concatenate(
                    [source[0, whole:tokens, columns], last], axis=0
                )
            turned[head, which] = (
                straight[head, which].astype(jnp.float32).T.astype(jnp.bfloat16)
            )


def attend_kernel(turns, hands, peers, seg_rows, tokens, reads, caches, turned_caches, *refs):
    outs = 1 + hands * len(turns)
    received, refs = refs[: len(refs) - 14 - outs], refs[len(refs) - 14 - outs :]
    returned, grads = refs[0], refs[1:outs]
    (
        straight,
        turned,
        inbox,
        outbox,
        scores,
        even_odd,
        dscores,
        sums,
        staged,
        owners,
        kv_sems,
        in_sems,
        out_sems,
        grad_sems,
    ) = refs[outs:]
    me = lax.axis_index("enc")
    base = lax.axis_index("seq") * peers
    slots = inbox.shape[1]
    padded = straight.shape[2]
    pieces = [(a, min(a + CHUNK, padded)) for a in range(0, padded, CHUNK)]
    lanes = GROUP * seg_rows
    f32, bf16 = jnp.float32, jnp.bfloat16

    kv_copies = [
        [
            pltpu.make_async_copy(
                source.at[head_at(turn), which], target.at[i, which], kv_sems.at[i, j]
            )
            for j, (source, target, which) in enumerate(
                (
                    (caches, straight, 0),
                    (turned_caches, turned, 1),
                    (caches, straight, 1),
                    (turned_caches, turned, 0),
                )
            )
        ]
        for i, turn in enumerate(turns)
    ]

    def arriving(i, slot, k):
        source = received[k] if len(received) > 1 else received[0].at[me ^ k]
        return pltpu.make_async_copy(source.at[i], inbox.at[i, slot], in_sems.at[i, slot])

    def leaving(i, slot, owner):
        return pltpu.make_async_copy(
            outbox.at[i, slot], returned.at[owner, i], out_sems.at[i, slot]
        )

    def handing(i):
        pairs = [(staged.at[i], grads[i])]
        if hands == 2:
            pairs = [(staged.at[i, j], grads[2 * i + j]) for j in range(2)]
        return [
            pltpu.make_async_copy(source, target, grad_sems.at[i, j])
            for j, (source, target) in enumerate(pairs)
        ]

    for copies in kv_copies:
        copies[0].start()
    count = jnp.int32(0)
    for k in range(peers):
        found = is_read(reads, base + (me ^ k), me)

        @pl.when(found)
        def _():
            owners[count] = me ^ k
            for i in range(len(turns)):
                arriving(i, count, k).start()

        count = count + found.astype(jnp.int32)
    for j in range(1, 4):
        for copies in kv_copies:
            copies[j].start()

    sums[...] = jnp.zeros_like(sums)

    def stacked(i, slot, which):
        return jnp.concatenate(
            [inbox[i, slot, which, :, h * HD : (h + 1) * HD] for h in range(GROUP)], axis=0
        )

    def store(i, slot, which, turned_value):
        value = turned_value.T.astype(bf16)
        for h in range(GROUP):
            outbox[i, slot, which, :, h * HD : (h + 1) * HD] = value[
                h * seg_rows : (h + 1) * seg_rows, :
            ]

    def slices(a, b):
        return [(c, min(c + SLICE, b)) for c in range(a, b, SLICE)]

    def folded(value, reduce):
        return reduce(value.reshape(-1, 8, lanes), axis=0)

    def forward(i, slot, weights):
        q_turned = stacked(i, slot, 0).astype(f32).T.astype(bf16)
        tops, totals, outs = [], [], []

        def score():
            part = jnp.dot(straight[i, 0], q_turned, preferred_element_type=f32)
            for c, d in slices(0, padded):
                piece = part[c:d, :]
                if d > tokens:
                    token = lax.broadcasted_iota(jnp.int32, piece.shape, 0) + c
                    piece = jnp.where(token < tokens, piece, LOWEST)
                scores[i, c:d, :] = piece
                tops.append(folded(piece, jnp.max))

        def weigh(a, b):
            if a == 0:
                tops[:] = [jnp.max(functools.reduce(jnp.maximum, tops), axis=0, keepdims=True)]
            for c, d in slices(a, b):
                piece = jnp.exp2((scores[i, c:d, :] - tops[0]) * (SCALE * LOG2E))
                totals.append(folded(piece, jnp.sum))
                weights[i, c:d, :] = piece.astype(bf16)
            outs.append(
                jnp.dot(turned[i, 1, :, a:b], weights[i, a:b, :], preferred_element_type=f32)
            )

        def finish():
            total = jnp.sum(functools.reduce(jnp.add, totals), axis=0, keepdims=True)
            inverse = 1.0 / total
            out = functools.reduce(jnp.add, outs) * inverse
            store(i, slot, 0, out)
            g = (stacked(i, slot, 1).astype(f32).T * inverse).astype(bf16)
            exact = g.astype(f32)
            delta = jnp.sum(exact * out.astype(bf16).astype(f32), axis=0, keepdims=True)
            return delta, g, exact.T.astype(bf16)

        return score, weigh, finish

    def backward(i, slot, weights, delta, g_turned, g):
        q = stacked(i, slot, 0)
        turned_dq = []

        def values_part(a, b):
            dprob = jnp.dot(straight[i, 1, a:b, :], g_turned, preferred_element_type=f32)
            for c, d in slices(a, b):
                piece = weights[i, c:d, :].astype(f32) * (dprob[c - a : d - a, :] - delta)
                dscores[i, c:d, :] = piece.astype(bf16)

        def values_sum():
            sums[i, 1] += jnp.dot(weights[i], g, preferred_element_type=f32)

        def keys_sum():
            sums[i, 0] += jnp.dot(dscores[i], q, preferred_element_type=f32)

        def queries_part(a, b):
            turned_dq.append(
                jnp.dot(turned[i, 0, :, a:b], dscores[i, a:b, :], preferred_element_type=f32)
            )

        def finish():
            store(i, slot, 1, functools.reduce(jnp.add, turned_dq) * SCALE)

        return values_part, values_sum, keys_sum, queries_part, finish

    heads = range(len(turns))

    def one_slot(slot, carry, last=False):
        weights, next_weights = even_odd.at[slot & 1], even_odd.at[(slot + 1) & 1]
        behind = [backward(i, slot, weights, *carry[i]) for i in heads]
        ahead = []
        if not last:
            for i in heads:
                arriving(i, slot + 1, 0).wait()
            ahead = [forward(i, slot + 1, next_weights) for i in heads]

        for score, _, _ in ahead:
            score()
        for a, b in pieces:
            for values_part, *_ in behind:
                values_part(a, b)
        for _, values_sum, keys_sum, _, _ in behind:
            values_sum()
            keys_sum()
        for a, b in pieces:
            for _, weigh, _ in ahead:
                weigh(a, b)
            for _, _, _, queries_part, _ in behind:
                queries_part(a, b)
        for *_, finish in behind:
            finish()
        carry = [finish() for _, _, finish in ahead]
        for i in heads:
            leaving(i, slot, owners[slot]).start()
        return carry

    @pl.when(count > 0)
    def _():
        for i in heads:
            arriving(i, 0, 0).wait()
            kv_copies[i][0].wait()
        first = [forward(i, 0, even_odd.at[0]) for i in heads]
        for score, _, _ in first:
            score()
        for i in heads:
            kv_copies[i][1].wait()
        for a, b in pieces:
            for _, weigh, _ in first:
                weigh(a, b)
        carry = [finish() for _, _, finish in first]
        for i in heads:
            kv_copies[i][2].wait()
            kv_copies[i][3].wait()
        carry = lax.fori_loop(0, count - 1, one_slot, carry)
        one_slot(count - 1, carry, last=True)
        for i in heads:
            staged[i, 0] = (sums[i, 0] * SCALE).astype(bf16)
            staged[i, 1] = sums[i, 1].astype(bf16)
            for copy in handing(i):
                copy.start()

    @pl.when(count == 0)
    def _():
        staged[...] = jnp.zeros_like(staged)
        for i in range(len(turns)):
            for copy in kv_copies[i]:
                copy.wait()
            for copy in handing(i):
                copy.start()

    for i in range(len(turns)):
        for slot in range(slots):

            @pl.when(slot < count)
            def _():
                leaving(i, slot, 0).wait()

        for copy in handing(i):
            copy.wait()


def xor_permute(array, axis, k):
    if k == 0:
        return array
    size = lax.axis_size(axis)
    return lax.ppermute(array, axis, [(i, i ^ k) for i in range(size)])


def per_device(queries, keys, values, reads, grad_out):
    peers = lax.axis_size("enc")
    n_seq = lax.axis_size("seq")
    n_seg = reads.shape[1]
    by_segment = reads.T
    seg_rows = queries.shape[0] // n_seg
    slots = min(peers, 3 * n_seg // 2)
    tokens = keys.shape[1]
    padded = (tokens + 15) // 16 * 16
    lanes = GROUP * seg_rows
    bf16, f32 = jnp.bfloat16, jnp.float32
    chunks = [tuple(range(i, i + PER_CHUNK)) for i in range(0, KVH, PER_CHUNK)]
    message = jax.ShapeDtypeStruct((peers, PER_CHUNK, 2, seg_rows, WIDTH), bf16)
    part = jax.ShapeDtypeStruct((PER_CHUNK, 2, seg_rows, WIDTH), bf16)

    caches = [
        jax.ShapeDtypeStruct((KVH, 2, padded, HD), bf16),
        jax.ShapeDtypeStruct((KVH, 2, HD, padded), bf16),
    ]

    def route(turns, prepares):
        outputs = [message] + caches if prepares else [part] * peers
        return pl.pallas_call(
            functools.partial(route_kernel, turns, n_seg, seg_rows, tokens),
            out_shape=outputs,
            in_specs=[SMEM, ANY, ANY] + [VMEM] * 2 * prepares,
            out_specs=[ANY, VMEM, VMEM] if prepares else [ANY] * peers,
            scratch_shapes=[
                pltpu.VMEM((n_seg, PER_CHUNK, 2, seg_rows, WIDTH), bf16),
                pltpu.SemaphoreType.DMA((n_seg, PER_CHUNK, 2)),
                pltpu.SemaphoreType.DMA((n_seg,)),
            ],
            compiler_params=pltpu.CompilerParams(vmem_limit_bytes=VMEM_BYTES),
            cost_estimate=pl.CostEstimate(
                flops=0, bytes_accessed=(2 + 10 * prepares) << 20, transcendentals=0
            ),
            name=f"route_{turns[0]}",
        )(by_segment, queries, grad_out, *[keys, values] * prepares)

    def attend(turns, hands, received):
        work = slots * lanes * tokens * HD * len(turns)
        grad = jax.ShapeDtypeStruct((2, padded, HD)[hands - 1 :], bf16)
        results = pl.pallas_call(
            functools.partial(attend_kernel, turns, hands, peers, seg_rows, tokens),
            out_shape=[message] + [grad] * hands * len(turns),
            in_specs=[SMEM] + [ANY] * (2 + len(received)),
            out_specs=[ANY] * (1 + hands * len(turns)),
            scratch_shapes=[
                pltpu.VMEM((len(turns), 2, padded, HD), bf16),
                pltpu.VMEM((len(turns), 2, HD, padded), bf16),
                pltpu.VMEM((len(turns), slots, 2, seg_rows, WIDTH), bf16),
                pltpu.VMEM((len(turns), slots, 2, seg_rows, WIDTH), bf16),
                pltpu.VMEM((len(turns), padded, lanes), f32),
                pltpu.VMEM((2, len(turns), padded, lanes), bf16),
                pltpu.VMEM((len(turns), padded, lanes), bf16),
                pltpu.VMEM((len(turns), 2, padded, HD), f32),
                pltpu.VMEM((len(turns), 2, padded, HD), bf16),
                pltpu.SMEM((slots,), jnp.int32),
                pltpu.SemaphoreType.DMA((len(turns), 4)),
                pltpu.SemaphoreType.DMA((len(turns), slots)),
                pltpu.SemaphoreType.DMA((len(turns), slots)),
                pltpu.SemaphoreType.DMA((len(turns), 2)),
            ],
            compiler_params=pltpu.CompilerParams(vmem_limit_bytes=VMEM_BYTES),
            cost_estimate=pl.CostEstimate(
                flops=12 * work, bytes_accessed=8 << 20, transcendentals=slots * lanes * tokens
            ),
            name=f"attend_{turns[0]}",
        )(by_segment, *prepared, *received)
        return results

    def collect(turns, returned, before):
        whole = jax.ShapeDtypeStruct(queries.shape, bf16)
        return pl.pallas_call(
            functools.partial(collect_kernel, turns, n_seg, seg_rows),
            out_shape=[whole, whole],
            in_specs=[SMEM, ANY] + [ANY] * len(before),
            out_specs=[ANY, ANY],
            input_output_aliases={2: 0, 3: 1} if before else {},
            scratch_shapes=[
                pltpu.VMEM((PER_CHUNK, 2, n_seg * seg_rows, WIDTH), bf16),
                pltpu.SemaphoreType.DMA((PER_CHUNK, 2, n_seg)),
                pltpu.SemaphoreType.DMA((PER_CHUNK, 2)),
            ],
            compiler_params=pltpu.CompilerParams(vmem_limit_bytes=VMEM_BYTES),
            cost_estimate=pl.CostEstimate(flops=0, bytes_accessed=4 << 20, transcendentals=0),
            name=f"collect_{turns[0]}",
        )(by_segment, returned, *before)

    def exchange(array):
        return lax.all_to_all(array, "enc", split_axis=0, concat_axis=0, tiled=True)

    first, second = chunks
    received = [xor_permute(array, "enc", k) for k, array in enumerate(route(first, 0))]
    routed, *prepared = route(second, 1)
    most = len(received) // 2 + 1
    *received[:most], routed = lax.optimization_barrier((*received[:most], routed))
    received_later = exchange(routed)
    butterfly = n_seq == KVH
    returned, *grads = attend(first, 1 + butterfly, received)
    answer = exchange(returned)
    if butterfly:
        passed = xor_permute(grads[0], "seq", 1)
        far = [xor_permute(grads[1], "seq", 3), xor_permute(grads[3], "seq", 2)]
    received_later, grads[-1] = lax.optimization_barrier((received_later, grads[-1]))
    returned, *more = attend(second, 1, [received_later])
    if butterfly:
        passed, grads[2], more[0] = lax.optimization_barrier((passed, grads[2], more[0]))
        pair = (grads[2].astype(f32) + passed.astype(f32)).astype(bf16)
        returned, pair = lax.optimization_barrier((returned, pair))
        pair = xor_permute(pair, "seq", 2)
        near = xor_permute(more[0], "seq", 1)
    answer, returned = lax.optimization_barrier((answer, returned))
    answer_later = exchange(returned)
    half = collect(first, answer, [])
    attended, grad_queries = collect(second, answer_later, half)

    if butterfly:
        terms = [[more[1][0], near[0], pair], [more[1][1], near[1], *far]]
        summed = [sum(term.astype(f32) for term in ones)[:tokens].astype(bf16) for ones in terms]
        return attended, grad_queries, summed[0][None], summed[1][None]
    joined = jnp.concatenate(grads + more, axis=2)[:, :tokens]
    summed = lax.psum_scatter(joined, "seq", scatter_dimension=2, tiled=True)
    return attended, grad_queries, summed[0][None], summed[1][None]


def solution(mesh):
    placed = (
        P(("seq", "enc"), None),
        P("enc", None, None),
        P("enc", None, None),
        P(),
        P(("seq", "enc"), None),
    )
    return jax.shard_map(
        per_device,
        mesh=mesh,
        in_specs=placed,
        out_specs=(
            P(("seq", "enc"), None),
            P(("seq", "enc"), None),
            P("enc", None, "seq"),
            P("enc", None, "seq"),
        ),
        check_vma=False,
    )
```

```python
import functools

import jax
import jax.numpy as jnp
from jax import lax
from jax.experimental import pallas as pl
from jax.experimental.pallas import tpu as pltpu
from jax.sharding import PartitionSpec as P

HQ = 32
KVH = 4
HD = 128
GROUP = HQ // KVH
WIDTH = GROUP * HD
SCALE = HD ** (-0.5)
LOG2E = 1.4426950408889634
CHUNK = 512
SLICE = 128
LOWEST = -3.0e38
PER_CHUNK = 2
VMEM_BYTES = 58 << 20
ANY = pl.BlockSpec(memory_space=pl.ANY)
SMEM = pl.BlockSpec(memory_space=pltpu.SMEM)
VMEM = pl.BlockSpec(memory_space=pltpu.VMEM)


def head_at(turn):
    if lax.axis_size("seq") == KVH:
        return lax.axis_index("seq") ^ (KVH - 1 - turn)
    return turn


def route_kernel(turns, n_seg, seg_rows, tokens, reads, q_hbm, g_hbm, *refs):
    stage, in_sems, out_sems = refs[-3:]
    apart = len(refs) > 8
    me = lax.axis_index("enc")
    row = lax.axis_index("seq") * lax.axis_size("enc") + me
    arriving = [[] for _ in range(n_seg)]
    for r in range(n_seg):
        rows = slice(r * seg_rows, (r + 1) * seg_rows)
        for i, turn in enumerate(turns):
            columns = pl.ds(pl.multiple_of(head_at(turn) * WIDTH, WIDTH), WIDTH)
            for which, source in enumerate((q_hbm, g_hbm)):
                arriving[r].append(
                    pltpu.make_async_copy(
                        source.at[rows, columns],
                        stage.at[r, i, which],
                        in_sems.at[r, i, which],
                    )
                )

    def leaving(r, target):
        return pltpu.make_async_copy(stage.at[r], target, out_sems.at[r])

    for copies in arriving:
        for copy in copies:
            copy.start()
    for r, copies in enumerate(arriving):
        for copy in copies:
            copy.wait()
        if apart:
            for k, out in enumerate(refs[:-3]):

                @pl.when(reads[r, row] == me ^ k)
                def _():
                    leaving(r, out).start()

        else:
            leaving(r, refs[2].at[reads[r, row]]).start()
    if not apart:
        k_in, v_in, _, straight, turned = refs[:5]
        prepare(tokens, k_in, v_in, straight, turned)
    for r in range(n_seg):
        leaving(r, refs[0] if apart else refs[2].at[0]).wait()


def collect_kernel(turns, n_seg, seg_rows, reads, returned, *refs):
    o_hbm, dq_hbm, stage, in_sems, out_sems = refs[-5:]
    row = lax.axis_index("seq") * lax.axis_size("enc") + lax.axis_index("enc")
    arriving, leaving = [], []
    for i, turn in enumerate(turns):
        columns = pl.ds(pl.multiple_of(head_at(turn) * WIDTH, WIDTH), WIDTH)
        for which, target in enumerate((o_hbm, dq_hbm)):
            arriving.append(
                [
                    pltpu.make_async_copy(
                        returned.at[reads[r, row], i, which],
                        stage.at[i, which, r * seg_rows : (r + 1) * seg_rows, :],
                        in_sems.at[i, which, r],
                    )
                    for r in range(n_seg)
                ]
            )
            leaving.append(
                pltpu.make_async_copy(
                    stage.at[i, which], target.at[:, columns], out_sems.at[i, which]
                )
            )
    for copies in arriving:
        for copy in copies:
            copy.start()
    for copies, out in zip(arriving, leaving):
        for copy in copies:
            copy.wait()
        out.start()
    for out in leaving:
        out.wait()


def is_read(reads, row, image):
    found = jnp.int32(0)
    for r in range(reads.shape[0]):
        found = found + (reads[r, row] == image).astype(jnp.int32)
    return found > 0


def prepare(tokens, k_in, v_in, straight, turned):
    padded = straight.shape[2]
    whole = tokens // 16 * 16
    for which, source in enumerate((k_in, v_in)):
        for head in range(KVH):
            columns = slice(head * HD, (head + 1) * HD)
            straight[head, which, 0:whole, :] = source[0, 0:whole, columns]
            if whole < tokens:
                last = jnp.zeros((padded - tokens, HD), jnp.bfloat16)
                straight[head, which, whole:padded, :] = jnp.concatenate(
                    [source[0, whole:tokens, columns], last], axis=0
                )
            turned[head, which] = (
                straight[head, which].astype(jnp.float32).T.astype(jnp.bfloat16)
            )


def attend_kernel(turns, hands, peers, seg_rows, tokens, reads, caches, turned_caches, *refs):
    outs = 1 + hands * len(turns)
    received, refs = refs[: len(refs) - 14 - outs], refs[len(refs) - 14 - outs :]
    returned, grads = refs[0], refs[1:outs]
    (
        straight,
        turned,
        inbox,
        outbox,
        scores,
        even_odd,
        dscores,
        sums,
        staged,
        owners,
        kv_sems,
        in_sems,
        out_sems,
        grad_sems,
    ) = refs[outs:]
    me = lax.axis_index("enc")
    base = lax.axis_index("seq") * peers
    slots = inbox.shape[1]
    padded = straight.shape[2]
    pieces = [(a, min(a + CHUNK, padded)) for a in range(0, padded, CHUNK)]
    lanes = GROUP * seg_rows
    f32, bf16 = jnp.float32, jnp.bfloat16

    kv_copies = [
        [
            pltpu.make_async_copy(
                source.at[head_at(turn), which], target.at[i, which], kv_sems.at[i, j]
            )
            for j, (source, target, which) in enumerate(
                (
                    (caches, straight, 0),
                    (turned_caches, turned, 1),
                    (caches, straight, 1),
                    (turned_caches, turned, 0),
                )
            )
        ]
        for i, turn in enumerate(turns)
    ]

    def arriving(i, slot, k):
        source = received[k] if len(received) > 1 else received[0].at[me ^ k]
        return pltpu.make_async_copy(source.at[i], inbox.at[i, slot], in_sems.at[i, slot])

    def leaving(i, slot, owner):
        return pltpu.make_async_copy(
            outbox.at[i, slot], returned.at[owner, i], out_sems.at[i, slot]
        )

    def handing(i):
        pairs = [(staged.at[i], grads[i])]
        if hands == 2:
            pairs = [(staged.at[i, j], grads[2 * i + j]) for j in range(2)]
        return [
            pltpu.make_async_copy(source, target, grad_sems.at[i, j])
            for j, (source, target) in enumerate(pairs)
        ]

    for copies in kv_copies:
        copies[0].start()
    count = jnp.int32(0)
    for k in range(peers):
        found = is_read(reads, base + (me ^ k), me)

        @pl.when(found)
        def _():
            owners[count] = me ^ k
            for i in range(len(turns)):
                arriving(i, count, k).start()

        count = count + found.astype(jnp.int32)
    for j in range(1, 4):
        for copies in kv_copies:
            copies[j].start()

    sums[...] = jnp.zeros_like(sums)

    def stacked(i, slot, which):
        return jnp.concatenate(
            [inbox[i, slot, which, :, h * HD : (h + 1) * HD] for h in range(GROUP)], axis=0
        )

    def store(i, slot, which, turned_value):
        value = turned_value.T.astype(bf16)
        for h in range(GROUP):
            outbox[i, slot, which, :, h * HD : (h + 1) * HD] = value[
                h * seg_rows : (h + 1) * seg_rows, :
            ]

    def slices(a, b):
        return [(c, min(c + SLICE, b)) for c in range(a, b, SLICE)]

    def folded(value, reduce):
        return reduce(value.reshape(-1, 8, lanes), axis=0)

    def forward(i, slot, weights):
        q_turned = stacked(i, slot, 0).astype(f32).T.astype(bf16)
        tops, totals, outs = [], [], []

        def score():
            part = jnp.dot(straight[i, 0], q_turned, preferred_element_type=f32)
            for c, d in slices(0, padded):
                piece = part[c:d, :]
                if d > tokens:
                    token = lax.broadcasted_iota(jnp.int32, piece.shape, 0) + c
                    piece = jnp.where(token < tokens, piece, LOWEST)
                scores[i, c:d, :] = piece
                tops.append(folded(piece, jnp.max))

        def weigh(a, b):
            if a == 0:
                tops[:] = [jnp.max(functools.reduce(jnp.maximum, tops), axis=0, keepdims=True)]
            for c, d in slices(a, b):
                piece = jnp.exp2((scores[i, c:d, :] - tops[0]) * (SCALE * LOG2E))
                totals.append(folded(piece, jnp.sum))
                weights[i, c:d, :] = piece.astype(bf16)
            outs.append(
                jnp.dot(turned[i, 1, :, a:b], weights[i, a:b, :], preferred_element_type=f32)
            )

        def finish():
            total = jnp.sum(functools.reduce(jnp.add, totals), axis=0, keepdims=True)
            inverse = 1.0 / total
            out = functools.reduce(jnp.add, outs) * inverse
            store(i, slot, 0, out)
            g = (stacked(i, slot, 1).astype(f32).T * inverse).astype(bf16)
            exact = g.astype(f32)
            delta = jnp.sum(exact * out.astype(bf16).astype(f32), axis=0, keepdims=True)
            return delta, g, exact.T.astype(bf16)

        return score, weigh, finish

    def backward(i, slot, weights, delta, g_turned, g):
        q = stacked(i, slot, 0)
        turned_dq = []

        def values_part(a, b):
            dprob = jnp.dot(straight[i, 1, a:b, :], g_turned, preferred_element_type=f32)
            for c, d in slices(a, b):
                piece = weights[i, c:d, :].astype(f32) * (dprob[c - a : d - a, :] - delta)
                dscores[i, c:d, :] = piece.astype(bf16)

        def values_sum():
            sums[i, 1] += jnp.dot(weights[i], g, preferred_element_type=f32)

        def keys_sum():
            sums[i, 0] += jnp.dot(dscores[i], q, preferred_element_type=f32)

        def queries_part(a, b):
            turned_dq.append(
                jnp.dot(turned[i, 0, :, a:b], dscores[i, a:b, :], preferred_element_type=f32)
            )

        def finish():
            store(i, slot, 1, functools.reduce(jnp.add, turned_dq) * SCALE)

        return values_part, values_sum, keys_sum, queries_part, finish

    heads = range(len(turns))

    def one_slot(slot, carry, last=False):
        weights, next_weights = even_odd.at[slot & 1], even_odd.at[(slot + 1) & 1]
        behind = [backward(i, slot, weights, *carry[i]) for i in heads]
        ahead = []
        if not last:
            for i in heads:
                arriving(i, slot + 1, 0).wait()
            ahead = [forward(i, slot + 1, next_weights) for i in heads]

        for score, _, _ in ahead:
            score()
        for a, b in pieces:
            for values_part, *_ in behind:
                values_part(a, b)
        for _, values_sum, keys_sum, _, _ in behind:
            values_sum()
            keys_sum()
        for a, b in pieces:
            for _, weigh, _ in ahead:
                weigh(a, b)
            for _, _, _, queries_part, _ in behind:
                queries_part(a, b)
        for *_, finish in behind:
            finish()
        carry = [finish() for _, _, finish in ahead]
        for i in heads:
            leaving(i, slot, owners[slot]).start()
        return carry

    @pl.when(count > 0)
    def _():
        for i in heads:
            arriving(i, 0, 0).wait()
            kv_copies[i][0].wait()
        first = [forward(i, 0, even_odd.at[0]) for i in heads]
        for score, _, _ in first:
            score()
        for i in heads:
            kv_copies[i][1].wait()
        for a, b in pieces:
            for _, weigh, _ in first:
                weigh(a, b)
        carry = [finish() for _, _, finish in first]
        for i in heads:
            kv_copies[i][2].wait()
            kv_copies[i][3].wait()
        carry = lax.fori_loop(0, count - 1, one_slot, carry)
        one_slot(count - 1, carry, last=True)
        for i in heads:
            staged[i, 0] = (sums[i, 0] * SCALE).astype(bf16)
            staged[i, 1] = sums[i, 1].astype(bf16)
            for copy in handing(i):
                copy.start()

    @pl.when(count == 0)
    def _():
        staged[...] = jnp.zeros_like(staged)
        for i in range(len(turns)):
            for copy in kv_copies[i]:
                copy.wait()
            for copy in handing(i):
                copy.start()

    for i in range(len(turns)):
        for slot in range(slots):

            @pl.when(slot < count)
            def _():
                leaving(i, slot, 0).wait()

        for copy in handing(i):
            copy.wait()


def xor_permute(array, axis, k):
    if k == 0:
        return array
    size = lax.axis_size(axis)
    return lax.ppermute(array, axis, [(i, i ^ k) for i in range(size)])


def per_device(queries, keys, values, reads, grad_out):
    peers = lax.axis_size("enc")
    n_seq = lax.axis_size("seq")
    n_seg = reads.shape[1]
    by_segment = reads.T
    seg_rows = queries.shape[0] // n_seg
    slots = min(peers, 3 * n_seg // 2)
    tokens = keys.shape[1]
    padded = (tokens + 15) // 16 * 16
    lanes = GROUP * seg_rows
    bf16, f32 = jnp.bfloat16, jnp.float32
    chunks = [tuple(range(i, i + PER_CHUNK)) for i in range(0, KVH, PER_CHUNK)]
    message = jax.ShapeDtypeStruct((peers, PER_CHUNK, 2, seg_rows, WIDTH), bf16)
    part = jax.ShapeDtypeStruct((PER_CHUNK, 2, seg_rows, WIDTH), bf16)

    caches = [
        jax.ShapeDtypeStruct((KVH, 2, padded, HD), bf16),
        jax.ShapeDtypeStruct((KVH, 2, HD, padded), bf16),
    ]

    def route(turns, prepares):
        outputs = [message] + caches if prepares else [part] * peers
        return pl.pallas_call(
            functools.partial(route_kernel, turns, n_seg, seg_rows, tokens),
            out_shape=outputs,
            in_specs=[SMEM, ANY, ANY] + [VMEM] * 2 * prepares,
            out_specs=[ANY, VMEM, VMEM] if prepares else [ANY] * peers,
            scratch_shapes=[
                pltpu.VMEM((n_seg, PER_CHUNK, 2, seg_rows, WIDTH), bf16),
                pltpu.SemaphoreType.DMA((n_seg, PER_CHUNK, 2)),
                pltpu.SemaphoreType.DMA((n_seg,)),
            ],
            compiler_params=pltpu.CompilerParams(vmem_limit_bytes=VMEM_BYTES),
            cost_estimate=pl.CostEstimate(
                flops=0, bytes_accessed=(2 + 10 * prepares) << 20, transcendentals=0
            ),
            name=f"route_{turns[0]}",
        )(by_segment, queries, grad_out, *[keys, values] * prepares)

    def attend(turns, hands, received):
        work = slots * lanes * tokens * HD * len(turns)
        grad = jax.ShapeDtypeStruct((2, padded, HD)[hands - 1 :], bf16)
        results = pl.pallas_call(
            functools.partial(attend_kernel, turns, hands, peers, seg_rows, tokens),
            out_shape=[message] + [grad] * hands * len(turns),
            in_specs=[SMEM] + [ANY] * (2 + len(received)),
            out_specs=[ANY] * (1 + hands * len(turns)),
            scratch_shapes=[
                pltpu.VMEM((len(turns), 2, padded, HD), bf16),
                pltpu.VMEM((len(turns), 2, HD, padded), bf16),
                pltpu.VMEM((len(turns), slots, 2, seg_rows, WIDTH), bf16),
                pltpu.VMEM((len(turns), slots, 2, seg_rows, WIDTH), bf16),
                pltpu.VMEM((len(turns), padded, lanes), f32),
                pltpu.VMEM((2, len(turns), padded, lanes), bf16),
                pltpu.VMEM((len(turns), padded, lanes), bf16),
                pltpu.VMEM((len(turns), 2, padded, HD), f32),
                pltpu.VMEM((len(turns), 2, padded, HD), bf16),
                pltpu.SMEM((slots,), jnp.int32),
                pltpu.SemaphoreType.DMA((len(turns), 4)),
                pltpu.SemaphoreType.DMA((len(turns), slots)),
                pltpu.SemaphoreType.DMA((len(turns), slots)),
                pltpu.SemaphoreType.DMA((len(turns), 2)),
            ],
            compiler_params=pltpu.CompilerParams(vmem_limit_bytes=VMEM_BYTES),
            cost_estimate=pl.CostEstimate(
                flops=12 * work, bytes_accessed=8 << 20, transcendentals=slots * lanes * tokens
            ),
            name=f"attend_{turns[0]}",
        )(by_segment, *prepared, *received)
        return results

    def collect(turns, returned, before):
        whole = jax.ShapeDtypeStruct(queries.shape, bf16)
        return pl.pallas_call(
            functools.partial(collect_kernel, turns, n_seg, seg_rows),
            out_shape=[whole, whole],
            in_specs=[SMEM, ANY] + [ANY] * len(before),
            out_specs=[ANY, ANY],
            input_output_aliases={2: 0, 3: 1} if before else {},
            scratch_shapes=[
                pltpu.VMEM((PER_CHUNK, 2, n_seg * seg_rows, WIDTH), bf16),
                pltpu.SemaphoreType.DMA((PER_CHUNK, 2, n_seg)),
                pltpu.SemaphoreType.DMA((PER_CHUNK, 2)),
            ],
            compiler_params=pltpu.CompilerParams(vmem_limit_bytes=VMEM_BYTES),
            cost_estimate=pl.CostEstimate(flops=0, bytes_accessed=4 << 20, transcendentals=0),
            name=f"collect_{turns[0]}",
        )(by_segment, returned, *before)

    def exchange(array):
        return lax.all_to_all(array, "enc", split_axis=0, concat_axis=0, tiled=True)

    first, second = chunks
    received = [xor_permute(array, "enc", k) for k, array in enumerate(route(first, 0))]
    routed, *prepared = route(second, 1)
    *received, routed = lax.optimization_barrier((*received, routed))
    received_later = exchange(routed)
    butterfly = n_seq == KVH
    returned, *grads = attend(first, 1 + butterfly, received)
    answer = exchange(returned)
    if butterfly:
        passed = xor_permute(grads[0], "seq", 1)
        far = [xor_permute(grads[1], "seq", 3), xor_permute(grads[3], "seq", 2)]
    received_later, grads[-1] = lax.optimization_barrier((received_later, grads[-1]))
    returned, *more = attend(second, 1, [received_later])
    if butterfly:
        passed, grads[2], more[0] = lax.optimization_barrier((passed, grads[2], more[0]))
        pair = (grads[2].astype(f32) + passed.astype(f32)).astype(bf16)
        returned, pair = lax.optimization_barrier((returned, pair))
        pair = xor_permute(pair, "seq", 2)
        near = xor_permute(more[0], "seq", 1)
    answer, returned = lax.optimization_barrier((answer, returned))
    answer_later = exchange(returned)
    if butterfly:
        answer, *far = lax.optimization_barrier((answer, *far))
    half = collect(first, answer, [])
    attended, grad_queries = collect(second, answer_later, half)

    if butterfly:
        terms = [[more[1][0], near[0], pair], [more[1][1], near[1], *far]]
        summed = [sum(term.astype(f32) for term in ones)[:tokens].astype(bf16) for ones in terms]
        return attended, grad_queries, summed[0][None], summed[1][None]
    joined = jnp.concatenate(grads + more, axis=2)[:, :tokens]
    summed = lax.psum_scatter(joined, "seq", scatter_dimension=2, tiled=True)
    return attended, grad_queries, summed[0][None], summed[1][None]


def solution(mesh):
    placed = (
        P(("seq", "enc"), None),
        P("enc", None, None),
        P("enc", None, None),
        P(),
        P(("seq", "enc"), None),
    )
    return jax.shard_map(
        per_device,
        mesh=mesh,
        in_specs=placed,
        out_specs=(
            P(("seq", "enc"), None),
            P(("seq", "enc"), None),
            P("enc", None, "seq"),
            P("enc", None, "seq"),
        ),
        check_vma=False,
    )
```

```python
import functools

import jax
import jax.numpy as jnp
from jax import lax
from jax.experimental import pallas as pl
from jax.experimental.pallas import tpu as pltpu
from jax.sharding import PartitionSpec as P

HQ = 32
KVH = 4
HD = 128
GROUP = HQ // KVH
WIDTH = GROUP * HD
SCALE = HD ** (-0.5)
LOG2E = 1.4426950408889634
CHUNK = 512
SLICE = 128
LOWEST = -3.0e38
PER_CHUNK = 2
VMEM_BYTES = 58 << 20
KERNEL_BYTES = 40 << 20
SPARE = 8
ANY = pl.BlockSpec(memory_space=pl.ANY)
SMEM = pl.BlockSpec(memory_space=pltpu.SMEM)
VMEM = pl.BlockSpec(memory_space=pltpu.VMEM)


def head_at(turn):
    if lax.axis_size("seq") == KVH:
        return lax.axis_index("seq") ^ (KVH - 1 - turn)
    return turn


def route_kernel(turns, apart, n_seg, seg_rows, tokens, reads, q_hbm, g_hbm, *refs):
    stage, in_sems, out_sems, *more = refs[-3:] if apart else refs[-6:]
    me = lax.axis_index("enc")
    row = lax.axis_index("seq") * lax.axis_size("enc") + me
    arriving = [[] for _ in range(n_seg)]
    for r in range(n_seg):
        rows = slice(r * seg_rows, (r + 1) * seg_rows)
        for i, turn in enumerate(turns):
            columns = pl.ds(pl.multiple_of(head_at(turn) * WIDTH, WIDTH), WIDTH)
            for which, source in enumerate((q_hbm, g_hbm)):
                arriving[r].append(
                    pltpu.make_async_copy(
                        source.at[rows, columns],
                        stage.at[r, i, which],
                        in_sems.at[r, i, which],
                    )
                )

    def leaving(r, target):
        return pltpu.make_async_copy(stage.at[r], target, out_sems.at[r])

    for copies in arriving:
        for copy in copies:
            copy.start()
    for r, copies in enumerate(arriving):
        for copy in copies:
            copy.wait()
        if apart:
            for k, out in enumerate(refs[:-3]):

                @pl.when(reads[r, row] == me ^ k)
                def _():
                    leaving(r, out).start()

        else:
            leaving(r, refs[2].at[reads[r, row]]).start()
    if not apart:
        k_in, v_in, _, *targets = refs[:5]
        straight, turned, cache_sems = more
        prepare(tokens, k_in, v_in, straight, turned)
        copies = [
            pltpu.make_async_copy(source, target.at[pl.ds(0, KVH)], cache_sems.at[i])
            for i, (source, target) in enumerate(((straight, targets[0]), (turned, targets[1])))
        ]
        for copy in copies:
            copy.start()
        for copy in copies:
            copy.wait()
    for r in range(n_seg):
        leaving(r, refs[0] if apart else refs[2].at[0]).wait()


def collect_kernel(turns, n_seg, seg_rows, reads, returned, *refs):
    o_hbm, dq_hbm, stage, in_sems, out_sems = refs[-5:]
    row = lax.axis_index("seq") * lax.axis_size("enc") + lax.axis_index("enc")
    arriving, leaving = [], []
    for i, turn in enumerate(turns):
        columns = pl.ds(pl.multiple_of(head_at(turn) * WIDTH, WIDTH), WIDTH)
        for which, target in enumerate((o_hbm, dq_hbm)):
            arriving.append(
                [
                    pltpu.make_async_copy(
                        returned.at[reads[r, row], i, which],
                        stage.at[i, which, r * seg_rows : (r + 1) * seg_rows, :],
                        in_sems.at[i, which, r],
                    )
                    for r in range(n_seg)
                ]
            )
            leaving.append(
                pltpu.make_async_copy(
                    stage.at[i, which], target.at[:, columns], out_sems.at[i, which]
                )
            )
    for copies in arriving:
        for copy in copies:
            copy.start()
    for copies, out in zip(arriving, leaving):
        for copy in copies:
            copy.wait()
        out.start()
    for out in leaving:
        out.wait()


def is_read(reads, row, image):
    found = jnp.int32(0)
    for r in range(reads.shape[0]):
        found = found + (reads[r, row] == image).astype(jnp.int32)
    return found > 0


def prepare(tokens, k_in, v_in, straight, turned):
    padded = straight.shape[2]
    whole = tokens // 16 * 16
    for which, source in enumerate((k_in, v_in)):
        for head in range(KVH):
            columns = slice(head * HD, (head + 1) * HD)
            straight[head, which, 0:whole, :] = source[0, 0:whole, columns]
            if whole < tokens:
                last = jnp.zeros((padded - tokens, HD), jnp.bfloat16)
                straight[head, which, whole:padded, :] = jnp.concatenate(
                    [source[0, whole:tokens, columns], last], axis=0
                )
            turned[head, which] = (
                straight[head, which].astype(jnp.float32).T.astype(jnp.bfloat16)
            )


def attend_kernel(turns, hands, peers, seg_rows, tokens, reads, caches, turned_caches, *refs):
    outs = 1 + hands * len(turns)
    received, refs = refs[: len(refs) - 14 - outs], refs[len(refs) - 14 - outs :]
    returned, grads = refs[0], refs[1:outs]
    (
        straight,
        turned,
        inbox,
        outbox,
        scores,
        even_odd,
        dscores,
        sums,
        staged,
        owners,
        kv_sems,
        in_sems,
        out_sems,
        grad_sems,
    ) = refs[outs:]
    me = lax.axis_index("enc")
    base = lax.axis_index("seq") * peers
    slots = inbox.shape[1]
    padded = straight.shape[2]
    pieces = [(a, min(a + CHUNK, padded)) for a in range(0, padded, CHUNK)]
    lanes = GROUP * seg_rows
    f32, bf16 = jnp.float32, jnp.bfloat16

    kv_copies = [
        [
            pltpu.make_async_copy(
                source.at[head_at(turn), which], target.at[i, which], kv_sems.at[i, j]
            )
            for j, (source, target, which) in enumerate(
                (
                    (caches, straight, 0),
                    (turned_caches, turned, 1),
                    (caches, straight, 1),
                    (turned_caches, turned, 0),
                )
            )
        ]
        for i, turn in enumerate(turns)
    ]

    def arriving(i, slot, k):
        source = received[k] if len(received) > 1 else received[0].at[me ^ k]
        return pltpu.make_async_copy(source.at[i], inbox.at[i, slot], in_sems.at[i, slot])

    def leaving(i, slot, owner):
        return pltpu.make_async_copy(
            outbox.at[i, slot], returned.at[owner, i], out_sems.at[i, slot]
        )

    def handing(i):
        pairs = [(staged.at[i], grads[i])]
        if hands == 2:
            pairs = [(staged.at[i, j], grads[2 * i + j]) for j in range(2)]
        return [
            pltpu.make_async_copy(source, target, grad_sems.at[i, j])
            for j, (source, target) in enumerate(pairs)
        ]

    for copies in kv_copies:
        copies[0].start()
    count = jnp.int32(0)
    for k in range(peers):
        found = is_read(reads, base + (me ^ k), me)

        @pl.when(found)
        def _():
            owners[count] = me ^ k
            for i in range(len(turns)):
                arriving(i, count, k).start()

        count = count + found.astype(jnp.int32)
    for j in range(1, 4):
        for copies in kv_copies:
            copies[j].start()

    sums[...] = jnp.zeros_like(sums)

    def stacked(i, slot, which):
        return jnp.concatenate(
            [inbox[i, slot, which, :, h * HD : (h + 1) * HD] for h in range(GROUP)], axis=0
        )

    def store(i, slot, which, turned_value):
        value = turned_value.T.astype(bf16)
        for h in range(GROUP):
            outbox[i, slot, which, :, h * HD : (h + 1) * HD] = value[
                h * seg_rows : (h + 1) * seg_rows, :
            ]

    def slices(a, b):
        return [(c, min(c + SLICE, b)) for c in range(a, b, SLICE)]

    def folded(value, reduce):
        return reduce(value.reshape(-1, 8, lanes), axis=0)

    def forward(i, slot, weights):
        q_turned = stacked(i, slot, 0).astype(f32).T.astype(bf16)
        tops, totals, outs = [], [], []

        def score():
            part = jnp.dot(straight[i, 0], q_turned, preferred_element_type=f32)
            for c, d in slices(0, padded):
                piece = part[c:d, :]
                if d > tokens:
                    token = lax.broadcasted_iota(jnp.int32, piece.shape, 0) + c
                    piece = jnp.where(token < tokens, piece, LOWEST)
                scores[i, c:d, :] = piece
                tops.append(folded(piece, jnp.max))

        def weigh(a, b):
            if a == 0:
                tops[:] = [jnp.max(functools.reduce(jnp.maximum, tops), axis=0, keepdims=True)]
            for c, d in slices(a, b):
                piece = jnp.exp2((scores[i, c:d, :] - tops[0]) * (SCALE * LOG2E))
                totals.append(folded(piece, jnp.sum))
                weights[i, c:d, :] = piece.astype(bf16)
            outs.append(
                jnp.dot(turned[i, 1, :, a:b], weights[i, a:b, :], preferred_element_type=f32)
            )

        def finish():
            total = jnp.sum(functools.reduce(jnp.add, totals), axis=0, keepdims=True)
            inverse = 1.0 / total
            out = functools.reduce(jnp.add, outs) * inverse
            store(i, slot, 0, out)
            g = (stacked(i, slot, 1).astype(f32).T * inverse).astype(bf16)
            exact = g.astype(f32)
            delta = jnp.sum(exact * out.astype(bf16).astype(f32), axis=0, keepdims=True)
            return delta, g, exact.T.astype(bf16)

        return score, weigh, finish

    def backward(i, slot, weights, delta, g_turned, g):
        q = stacked(i, slot, 0)
        turned_dq = []

        def values_part(a, b):
            dprob = jnp.dot(straight[i, 1, a:b, :], g_turned, preferred_element_type=f32)
            for c, d in slices(a, b):
                piece = weights[i, c:d, :].astype(f32) * (dprob[c - a : d - a, :] - delta)
                dscores[i, c:d, :] = piece.astype(bf16)

        def values_sum():
            sums[i, 1] += jnp.dot(weights[i], g, preferred_element_type=f32)

        def keys_sum():
            sums[i, 0] += jnp.dot(dscores[i], q, preferred_element_type=f32)

        def queries_part(a, b):
            turned_dq.append(
                jnp.dot(turned[i, 0, :, a:b], dscores[i, a:b, :], preferred_element_type=f32)
            )

        def finish():
            store(i, slot, 1, functools.reduce(jnp.add, turned_dq) * SCALE)

        return values_part, values_sum, keys_sum, queries_part, finish

    heads = range(len(turns))

    def one_slot(slot, carry, last=False):
        weights, next_weights = even_odd.at[slot & 1], even_odd.at[(slot + 1) & 1]
        behind = [backward(i, slot, weights, *carry[i]) for i in heads]
        ahead = []
        if not last:
            for i in heads:
                arriving(i, slot + 1, 0).wait()
            ahead = [forward(i, slot + 1, next_weights) for i in heads]

        for score, _, _ in ahead:
            score()
        for a, b in pieces:
            for values_part, *_ in behind:
                values_part(a, b)
        for _, values_sum, keys_sum, _, _ in behind:
            values_sum()
            keys_sum()
        for a, b in pieces:
            for _, weigh, _ in ahead:
                weigh(a, b)
            for _, _, _, queries_part, _ in behind:
                queries_part(a, b)
        for *_, finish in behind:
            finish()
        carry = [finish() for _, _, finish in ahead]
        for i in heads:
            leaving(i, slot, owners[slot]).start()
        return carry

    @pl.when(count > 0)
    def _():
        for i in heads:
            arriving(i, 0, 0).wait()
            kv_copies[i][0].wait()
        first = [forward(i, 0, even_odd.at[0]) for i in heads]
        for score, _, _ in first:
            score()
        for i in heads:
            kv_copies[i][1].wait()
        for a, b in pieces:
            for _, weigh, _ in first:
                weigh(a, b)
        carry = [finish() for _, _, finish in first]
        for i in heads:
            kv_copies[i][2].wait()
            kv_copies[i][3].wait()
        carry = lax.fori_loop(0, count - 1, one_slot, carry)
        one_slot(count - 1, carry, last=True)
        for i in heads:
            staged[i, 0] = (sums[i, 0] * SCALE).astype(bf16)
            staged[i, 1] = sums[i, 1].astype(bf16)
            for copy in handing(i):
                copy.start()

    @pl.when(count == 0)
    def _():
        staged[...] = jnp.zeros_like(staged)
        for i in range(len(turns)):
            for copy in kv_copies[i]:
                copy.wait()
            for copy in handing(i):
                copy.start()

    for i in range(len(turns)):
        for slot in range(slots):

            @pl.when(slot < count)
            def _():
                leaving(i, slot, 0).wait()

        for copy in handing(i):
            copy.wait()


def xor_permute(array, axis, k):
    if k == 0:
        return array
    size = lax.axis_size(axis)
    return lax.ppermute(array, axis, [(i, i ^ k) for i in range(size)])


def per_device(queries, keys, values, reads, grad_out):
    peers = lax.axis_size("enc")
    n_seq = lax.axis_size("seq")
    n_seg = reads.shape[1]
    by_segment = reads.T
    seg_rows = queries.shape[0] // n_seg
    slots = min(peers, 3 * n_seg // 2)
    tokens = keys.shape[1]
    padded = (tokens + 15) // 16 * 16
    lanes = GROUP * seg_rows
    bf16, f32 = jnp.bfloat16, jnp.float32
    chunks = [tuple(range(i, i + PER_CHUNK)) for i in range(0, KVH, PER_CHUNK)]
    message = jax.ShapeDtypeStruct((peers, PER_CHUNK, 2, seg_rows, WIDTH), bf16)
    part = jax.ShapeDtypeStruct((PER_CHUNK, 2, seg_rows, WIDTH), bf16)

    caches = [
        jax.ShapeDtypeStruct((KVH * SPARE, 2, padded, HD), bf16),
        jax.ShapeDtypeStruct((KVH * SPARE, 2, HD, padded), bf16),
    ]

    def route(turns, prepares):
        outputs = [message] + caches if prepares else [part] * peers
        return pl.pallas_call(
            functools.partial(route_kernel, turns, not prepares, n_seg, seg_rows, tokens),
            out_shape=outputs,
            in_specs=[SMEM, ANY, ANY] + [VMEM] * 2 * prepares,
            out_specs=[ANY] * len(outputs),
            scratch_shapes=[
                pltpu.VMEM((n_seg, PER_CHUNK, 2, seg_rows, WIDTH), bf16),
                pltpu.SemaphoreType.DMA((n_seg, PER_CHUNK, 2)),
                pltpu.SemaphoreType.DMA((n_seg,)),
            ]
            + [
                pltpu.VMEM((KVH, 2, padded, HD), bf16),
                pltpu.VMEM((KVH, 2, HD, padded), bf16),
                pltpu.SemaphoreType.DMA((2,)),
            ]
            * prepares,
            compiler_params=pltpu.CompilerParams(vmem_limit_bytes=VMEM_BYTES),
            cost_estimate=pl.CostEstimate(
                flops=0, bytes_accessed=(2 + 10 * prepares) << 20, transcendentals=0
            ),
            name=f"route_{turns[0]}",
        )(by_segment, queries, grad_out, *[keys, values] * prepares)

    def attend(turns, hands, received):
        work = slots * lanes * tokens * HD * len(turns)
        grad = jax.ShapeDtypeStruct((2, padded, HD)[hands - 1 :], bf16)
        results = pl.pallas_call(
            functools.partial(attend_kernel, turns, hands, peers, seg_rows, tokens),
            out_shape=[message] + [grad] * hands * len(turns),
            in_specs=[SMEM] + [ANY] * (2 + len(received)),
            out_specs=[ANY] * (1 + hands * len(turns)),
            scratch_shapes=[
                pltpu.VMEM((len(turns), 2, padded, HD), bf16),
                pltpu.VMEM((len(turns), 2, HD, padded), bf16),
                pltpu.VMEM((len(turns), slots, 2, seg_rows, WIDTH), bf16),
                pltpu.VMEM((len(turns), slots, 2, seg_rows, WIDTH), bf16),
                pltpu.VMEM((len(turns), padded, lanes), f32),
                pltpu.VMEM((2, len(turns), padded, lanes), bf16),
                pltpu.VMEM((len(turns), padded, lanes), bf16),
                pltpu.VMEM((len(turns), 2, padded, HD), f32),
                pltpu.VMEM((len(turns), 2, padded, HD), bf16),
                pltpu.SMEM((slots,), jnp.int32),
                pltpu.SemaphoreType.DMA((len(turns), 4)),
                pltpu.SemaphoreType.DMA((len(turns), slots)),
                pltpu.SemaphoreType.DMA((len(turns), slots)),
                pltpu.SemaphoreType.DMA((len(turns), 2)),
            ],
            compiler_params=pltpu.CompilerParams(vmem_limit_bytes=KERNEL_BYTES),
            cost_estimate=pl.CostEstimate(
                flops=12 * work, bytes_accessed=8 << 20, transcendentals=slots * lanes * tokens
            ),
            name=f"attend_{turns[0]}",
        )(by_segment, *prepared, *received)
        return results

    def collect(turns, returned, before):
        whole = jax.ShapeDtypeStruct(queries.shape, bf16)
        return pl.pallas_call(
            functools.partial(collect_kernel, turns, n_seg, seg_rows),
            out_shape=[whole, whole],
            in_specs=[SMEM, ANY] + [ANY] * len(before),
            out_specs=[ANY, ANY],
            input_output_aliases={2: 0, 3: 1} if before else {},
            scratch_shapes=[
                pltpu.VMEM((PER_CHUNK, 2, n_seg * seg_rows, WIDTH), bf16),
                pltpu.SemaphoreType.DMA((PER_CHUNK, 2, n_seg)),
                pltpu.SemaphoreType.DMA((PER_CHUNK, 2)),
            ],
            compiler_params=pltpu.CompilerParams(vmem_limit_bytes=KERNEL_BYTES),
            cost_estimate=pl.CostEstimate(flops=0, bytes_accessed=4 << 20, transcendentals=0),
            name=f"collect_{turns[0]}",
        )(by_segment, returned, *before)

    def exchange(array):
        return lax.all_to_all(array, "enc", split_axis=0, concat_axis=0, tiled=True)

    first, second = chunks
    received = [xor_permute(array, "enc", k) for k, array in enumerate(route(first, 0))]
    routed, *prepared = route(second, 1)
    *received, routed = lax.optimization_barrier((*received, routed))
    received_later = exchange(routed)
    butterfly = n_seq == KVH
    returned, *grads = attend(first, 1, received)
    answer = exchange(returned)
    if butterfly:
        passed = xor_permute(grads[0], "seq", 1)
    received_later, grads[1] = lax.optimization_barrier((received_later, grads[1]))
    returned, *more = attend(second, 1, [received_later])
    answer, returned = lax.optimization_barrier((answer, returned))
    answer_later = exchange(returned)
    if butterfly:
        passed, grads[1], more[0] = lax.optimization_barrier((passed, grads[1], more[0]))
        pair = (grads[1].astype(f32) + passed.astype(f32)).astype(bf16)
        pair = xor_permute(pair, "seq", 2)
        near = xor_permute(more[0], "seq", 1)
    half = collect(first, answer, [])
    attended, grad_queries = collect(second, answer_later, half)

    if butterfly:
        summed = [
            sum(term[j, :tokens].astype(f32) for term in (more[1], near, pair)).astype(bf16)
            for j in range(2)
        ]
        return attended, grad_queries, summed[0][None], summed[1][None]
    joined = jnp.concatenate(grads + more, axis=2)[:, :tokens]
    summed = lax.psum_scatter(joined, "seq", scatter_dimension=2, tiled=True)
    return attended, grad_queries, summed[0][None], summed[1][None]


def solution(mesh):
    placed = (
        P(("seq", "enc"), None),
        P("enc", None, None),
        P("enc", None, None),
        P(),
        P(("seq", "enc"), None),
    )
    return jax.shard_map(
        per_device,
        mesh=mesh,
        in_specs=placed,
        out_specs=(
            P(("seq", "enc"), None),
            P(("seq", "enc"), None),
            P("enc", None, "seq"),
            P("enc", None, "seq"),
        ),
        check_vma=False,
    )
```

```python
import functools

import jax
import jax.numpy as jnp
from jax import lax
from jax.experimental import pallas as pl
from jax.experimental.pallas import tpu as pltpu
from jax.sharding import PartitionSpec as P

HQ = 32
KVH = 4
HD = 128
GROUP = HQ // KVH
WIDTH = GROUP * HD
SCALE = HD ** (-0.5)
LOG2E = 1.4426950408889634
CHUNK = 512
SLICE = 128
LOWEST = -3.0e38
PER_CHUNK = 2
VMEM_BYTES = 58 << 20
KERNEL_BYTES = 58 << 20
SPARE = 1
ANY = pl.BlockSpec(memory_space=pl.ANY)
SMEM = pl.BlockSpec(memory_space=pltpu.SMEM)
VMEM = pl.BlockSpec(memory_space=pltpu.VMEM)


def head_at(turn):
    if lax.axis_size("seq") == KVH:
        return lax.axis_index("seq") ^ (KVH - 1 - turn)
    return turn


def route_kernel(turns, apart, n_seg, seg_rows, tokens, reads, q_hbm, g_hbm, *refs):
    stage, in_sems, out_sems, *more = refs[-3:] if apart else refs[-6:]
    me = lax.axis_index("enc")
    row = lax.axis_index("seq") * lax.axis_size("enc") + me
    arriving = [[] for _ in range(n_seg)]
    for r in range(n_seg):
        rows = slice(r * seg_rows, (r + 1) * seg_rows)
        for i, turn in enumerate(turns):
            columns = pl.ds(pl.multiple_of(head_at(turn) * WIDTH, WIDTH), WIDTH)
            for which, source in enumerate((q_hbm, g_hbm)):
                arriving[r].append(
                    pltpu.make_async_copy(
                        source.at[rows, columns],
                        stage.at[r, i, which],
                        in_sems.at[r, i, which],
                    )
                )

    def leaving(r, target):
        return pltpu.make_async_copy(stage.at[r], target, out_sems.at[r])

    for copies in arriving:
        for copy in copies:
            copy.start()
    for r, copies in enumerate(arriving):
        for copy in copies:
            copy.wait()
        if apart:
            for k, out in enumerate(refs[:-3]):

                @pl.when(reads[r, row] == me ^ k)
                def _():
                    leaving(r, out).start()

        else:
            leaving(r, refs[2].at[reads[r, row]]).start()
    if not apart:
        k_in, v_in, _, *targets = refs[:5]
        straight, turned, cache_sems = more
        prepare(tokens, k_in, v_in, straight, turned)
        copies = [
            pltpu.make_async_copy(source, target.at[pl.ds(0, KVH)], cache_sems.at[i])
            for i, (source, target) in enumerate(((straight, targets[0]), (turned, targets[1])))
        ]
        for copy in copies:
            copy.start()
        for copy in copies:
            copy.wait()
    for r in range(n_seg):
        leaving(r, refs[0] if apart else refs[2].at[0]).wait()


def collect_kernel(turns, n_seg, seg_rows, reads, returned, *refs):
    o_hbm, dq_hbm, stage, in_sems, out_sems = refs[-5:]
    row = lax.axis_index("seq") * lax.axis_size("enc") + lax.axis_index("enc")
    arriving, leaving = [], []
    for i, turn in enumerate(turns):
        columns = pl.ds(pl.multiple_of(head_at(turn) * WIDTH, WIDTH), WIDTH)
        for which, target in enumerate((o_hbm, dq_hbm)):
            arriving.append(
                [
                    pltpu.make_async_copy(
                        returned.at[reads[r, row], i, which],
                        stage.at[i, which, r * seg_rows : (r + 1) * seg_rows, :],
                        in_sems.at[i, which, r],
                    )
                    for r in range(n_seg)
                ]
            )
            leaving.append(
                pltpu.make_async_copy(
                    stage.at[i, which], target.at[:, columns], out_sems.at[i, which]
                )
            )
    for copies in arriving:
        for copy in copies:
            copy.start()
    for copies, out in zip(arriving, leaving):
        for copy in copies:
            copy.wait()
        out.start()
    for out in leaving:
        out.wait()


def is_read(reads, row, image):
    found = jnp.int32(0)
    for r in range(reads.shape[0]):
        found = found + (reads[r, row] == image).astype(jnp.int32)
    return found > 0


def prepare(tokens, k_in, v_in, straight, turned):
    padded = straight.shape[2]
    whole = tokens // 16 * 16
    for which, source in enumerate((k_in, v_in)):
        for head in range(KVH):
            columns = slice(head * HD, (head + 1) * HD)
            straight[head, which, 0:whole, :] = source[0, 0:whole, columns]
            if whole < tokens:
                last = jnp.zeros((padded - tokens, HD), jnp.bfloat16)
                straight[head, which, whole:padded, :] = jnp.concatenate(
                    [source[0, whole:tokens, columns], last], axis=0
                )
            turned[head, which] = (
                straight[head, which].astype(jnp.float32).T.astype(jnp.bfloat16)
            )


def attend_kernel(turns, hands, peers, seg_rows, tokens, reads, caches, turned_caches, *refs):
    outs = 1 + hands * len(turns)
    received, refs = refs[: len(refs) - 14 - outs], refs[len(refs) - 14 - outs :]
    returned, grads = refs[0], refs[1:outs]
    (
        straight,
        turned,
        inbox,
        outbox,
        scores,
        even_odd,
        dscores,
        sums,
        staged,
        owners,
        kv_sems,
        in_sems,
        out_sems,
        grad_sems,
    ) = refs[outs:]
    me = lax.axis_index("enc")
    base = lax.axis_index("seq") * peers
    slots = inbox.shape[1]
    padded = straight.shape[2]
    pieces = [(a, min(a + CHUNK, padded)) for a in range(0, padded, CHUNK)]
    lanes = GROUP * seg_rows
    f32, bf16 = jnp.float32, jnp.bfloat16

    kv_copies = [
        [
            pltpu.make_async_copy(
                source.at[head_at(turn), which], target.at[i, which], kv_sems.at[i, j]
            )
            for j, (source, target, which) in enumerate(
                (
                    (caches, straight, 0),
                    (turned_caches, turned, 1),
                    (caches, straight, 1),
                    (turned_caches, turned, 0),
                )
            )
        ]
        for i, turn in enumerate(turns)
    ]

    def arriving(i, slot, k):
        source = received[k] if len(received) > 1 else received[0].at[me ^ k]
        return pltpu.make_async_copy(source.at[i], inbox.at[i, slot], in_sems.at[i, slot])

    def leaving(i, slot, owner):
        return pltpu.make_async_copy(
            outbox.at[i, slot], returned.at[owner, i], out_sems.at[i, slot]
        )

    def handing(i):
        pairs = [(staged.at[i], grads[i])]
        if hands == 2:
            pairs = [(staged.at[i, j], grads[2 * i + j]) for j in range(2)]
        return [
            pltpu.make_async_copy(source, target, grad_sems.at[i, j])
            for j, (source, target) in enumerate(pairs)
        ]

    for copies in kv_copies:
        copies[0].start()
    count = jnp.int32(0)
    for k in range(peers):
        found = is_read(reads, base + (me ^ k), me)

        @pl.when(found)
        def _():
            owners[count] = me ^ k
            for i in range(len(turns)):
                arriving(i, count, k).start()

        count = count + found.astype(jnp.int32)
    for j in range(1, 4):
        for copies in kv_copies:
            copies[j].start()

    sums[...] = jnp.zeros_like(sums)

    def stacked(i, slot, which):
        return jnp.concatenate(
            [inbox[i, slot, which, :, h * HD : (h + 1) * HD] for h in range(GROUP)], axis=0
        )

    def store(i, slot, which, turned_value):
        value = turned_value.T.astype(bf16)
        for h in range(GROUP):
            outbox[i, slot, which, :, h * HD : (h + 1) * HD] = value[
                h * seg_rows : (h + 1) * seg_rows, :
            ]

    def slices(a, b):
        return [(c, min(c + SLICE, b)) for c in range(a, b, SLICE)]

    def folded(value, reduce):
        return reduce(value.reshape(-1, 8, lanes), axis=0)

    def forward(i, slot, weights):
        q_turned = stacked(i, slot, 0).astype(f32).T.astype(bf16)
        tops, totals, outs = [], [], []

        def score():
            part = jnp.dot(straight[i, 0], q_turned, preferred_element_type=f32)
            for c, d in slices(0, padded):
                piece = part[c:d, :]
                if d > tokens:
                    token = lax.broadcasted_iota(jnp.int32, piece.shape, 0) + c
                    piece = jnp.where(token < tokens, piece, LOWEST)
                scores[i, c:d, :] = piece
                tops.append(folded(piece, jnp.max))

        def weigh(a, b):
            if a == 0:
                tops[:] = [jnp.max(functools.reduce(jnp.maximum, tops), axis=0, keepdims=True)]
            for c, d in slices(a, b):
                piece = jnp.exp2((scores[i, c:d, :] - tops[0]) * (SCALE * LOG2E))
                totals.append(folded(piece, jnp.sum))
                weights[i, c:d, :] = piece.astype(bf16)
            outs.append(
                jnp.dot(turned[i, 1, :, a:b], weights[i, a:b, :], preferred_element_type=f32)
            )

        def finish():
            total = jnp.sum(functools.reduce(jnp.add, totals), axis=0, keepdims=True)
            inverse = 1.0 / total
            out = functools.reduce(jnp.add, outs) * inverse
            store(i, slot, 0, out)
            g = (stacked(i, slot, 1).astype(f32).T * inverse).astype(bf16)
            exact = g.astype(f32)
            delta = jnp.sum(exact * out.astype(bf16).astype(f32), axis=0, keepdims=True)
            return delta, g, exact.T.astype(bf16)

        return score, weigh, finish

    def backward(i, slot, weights, delta, g_turned, g):
        q = stacked(i, slot, 0)
        turned_dq = []

        def values_part(a, b):
            dprob = jnp.dot(straight[i, 1, a:b, :], g_turned, preferred_element_type=f32)
            for c, d in slices(a, b):
                piece = weights[i, c:d, :].astype(f32) * (dprob[c - a : d - a, :] - delta)
                dscores[i, c:d, :] = piece.astype(bf16)

        def values_sum():
            sums[i, 1] += jnp.dot(weights[i], g, preferred_element_type=f32)

        def keys_sum():
            sums[i, 0] += jnp.dot(dscores[i], q, preferred_element_type=f32)

        def queries_part(a, b):
            turned_dq.append(
                jnp.dot(turned[i, 0, :, a:b], dscores[i, a:b, :], preferred_element_type=f32)
            )

        def finish():
            store(i, slot, 1, functools.reduce(jnp.add, turned_dq) * SCALE)

        return values_part, values_sum, keys_sum, queries_part, finish

    heads = range(len(turns))

    def one_slot(slot, carry, last=False):
        weights, next_weights = even_odd.at[slot & 1], even_odd.at[(slot + 1) & 1]
        behind = [backward(i, slot, weights, *carry[i]) for i in heads]
        ahead = []
        if not last:
            for i in heads:
                arriving(i, slot + 1, 0).wait()
            ahead = [forward(i, slot + 1, next_weights) for i in heads]

        for score, _, _ in ahead:
            score()
        for a, b in pieces:
            for values_part, *_ in behind:
                values_part(a, b)
        for _, values_sum, keys_sum, _, _ in behind:
            values_sum()
            keys_sum()
        for a, b in pieces:
            for _, weigh, _ in ahead:
                weigh(a, b)
            for _, _, _, queries_part, _ in behind:
                queries_part(a, b)
        for *_, finish in behind:
            finish()
        carry = [finish() for _, _, finish in ahead]
        for i in heads:
            leaving(i, slot, owners[slot]).start()
        return carry

    @pl.when(count > 0)
    def _():
        for i in heads:
            arriving(i, 0, 0).wait()
            kv_copies[i][0].wait()
        first = [forward(i, 0, even_odd.at[0]) for i in heads]
        for score, _, _ in first:
            score()
        for i in heads:
            kv_copies[i][1].wait()
        for a, b in pieces:
            for _, weigh, _ in first:
                weigh(a, b)
        carry = [finish() for _, _, finish in first]
        for i in heads:
            kv_copies[i][2].wait()
            kv_copies[i][3].wait()
        carry = lax.fori_loop(0, count - 1, one_slot, carry)
        one_slot(count - 1, carry, last=True)
        for i in heads:
            staged[i, 0] = (sums[i, 0] * SCALE).astype(bf16)
            staged[i, 1] = sums[i, 1].astype(bf16)
            for copy in handing(i):
                copy.start()

    @pl.when(count == 0)
    def _():
        staged[...] = jnp.zeros_like(staged)
        for i in range(len(turns)):
            for copy in kv_copies[i]:
                copy.wait()
            for copy in handing(i):
                copy.start()

    for i in range(len(turns)):
        for slot in range(slots):

            @pl.when(slot < count)
            def _():
                leaving(i, slot, 0).wait()

        for copy in handing(i):
            copy.wait()


def xor_permute(array, axis, k):
    if k == 0:
        return array
    size = lax.axis_size(axis)
    return lax.ppermute(array, axis, [(i, i ^ k) for i in range(size)])


def per_device(queries, keys, values, reads, grad_out):
    peers = lax.axis_size("enc")
    n_seq = lax.axis_size("seq")
    n_seg = reads.shape[1]
    by_segment = reads.T
    seg_rows = queries.shape[0] // n_seg
    slots = min(peers, 3 * n_seg // 2)
    tokens = keys.shape[1]
    padded = (tokens + 15) // 16 * 16
    lanes = GROUP * seg_rows
    bf16, f32 = jnp.bfloat16, jnp.float32
    chunks = [tuple(range(i, i + PER_CHUNK)) for i in range(0, KVH, PER_CHUNK)]
    message = jax.ShapeDtypeStruct((peers, PER_CHUNK, 2, seg_rows, WIDTH), bf16)
    part = jax.ShapeDtypeStruct((PER_CHUNK, 2, seg_rows, WIDTH), bf16)

    caches = [
        jax.ShapeDtypeStruct((KVH * SPARE, 2, padded, HD), bf16),
        jax.ShapeDtypeStruct((KVH * SPARE, 2, HD, padded), bf16),
    ]

    def route(turns, prepares):
        outputs = [message] + caches if prepares else [part] * peers
        return pl.pallas_call(
            functools.partial(route_kernel, turns, not prepares, n_seg, seg_rows, tokens),
            out_shape=outputs,
            in_specs=[SMEM, ANY, ANY] + [VMEM] * 2 * prepares,
            out_specs=[ANY] * len(outputs),
            scratch_shapes=[
                pltpu.VMEM((n_seg, PER_CHUNK, 2, seg_rows, WIDTH), bf16),
                pltpu.SemaphoreType.DMA((n_seg, PER_CHUNK, 2)),
                pltpu.SemaphoreType.DMA((n_seg,)),
            ]
            + [
                pltpu.VMEM((KVH, 2, padded, HD), bf16),
                pltpu.VMEM((KVH, 2, HD, padded), bf16),
                pltpu.SemaphoreType.DMA((2,)),
            ]
            * prepares,
            compiler_params=pltpu.CompilerParams(vmem_limit_bytes=VMEM_BYTES),
            cost_estimate=pl.CostEstimate(
                flops=0, bytes_accessed=(2 + 10 * prepares) << 20, transcendentals=0
            ),
            name=f"route_{turns[0]}",
        )(by_segment, queries, grad_out, *[keys, values] * prepares)

    def attend(turns, hands, received):
        work = slots * lanes * tokens * HD * len(turns)
        grad = jax.ShapeDtypeStruct((2, padded, HD)[hands - 1 :], bf16)
        results = pl.pallas_call(
            functools.partial(attend_kernel, turns, hands, peers, seg_rows, tokens),
            out_shape=[message] + [grad] * hands * len(turns),
            in_specs=[SMEM] + [ANY] * (2 + len(received)),
            out_specs=[ANY] * (1 + hands * len(turns)),
            scratch_shapes=[
                pltpu.VMEM((len(turns), 2, padded, HD), bf16),
                pltpu.VMEM((len(turns), 2, HD, padded), bf16),
                pltpu.VMEM((len(turns), slots, 2, seg_rows, WIDTH), bf16),
                pltpu.VMEM((len(turns), slots, 2, seg_rows, WIDTH), bf16),
                pltpu.VMEM((len(turns), padded, lanes), f32),
                pltpu.VMEM((2, len(turns), padded, lanes), bf16),
                pltpu.VMEM((len(turns), padded, lanes), bf16),
                pltpu.VMEM((len(turns), 2, padded, HD), f32),
                pltpu.VMEM((len(turns), 2, padded, HD), bf16),
                pltpu.SMEM((slots,), jnp.int32),
                pltpu.SemaphoreType.DMA((len(turns), 4)),
                pltpu.SemaphoreType.DMA((len(turns), slots)),
                pltpu.SemaphoreType.DMA((len(turns), slots)),
                pltpu.SemaphoreType.DMA((len(turns), 2)),
            ],
            compiler_params=pltpu.CompilerParams(vmem_limit_bytes=KERNEL_BYTES),
            cost_estimate=pl.CostEstimate(
                flops=12 * work, bytes_accessed=8 << 20, transcendentals=slots * lanes * tokens
            ),
            name=f"attend_{turns[0]}",
        )(by_segment, *prepared, *received)
        return results

    def collect(turns, returned, before):
        whole = jax.ShapeDtypeStruct(queries.shape, bf16)
        return pl.pallas_call(
            functools.partial(collect_kernel, turns, n_seg, seg_rows),
            out_shape=[whole, whole],
            in_specs=[SMEM, ANY] + [ANY] * len(before),
            out_specs=[ANY, ANY],
            input_output_aliases={2: 0, 3: 1} if before else {},
            scratch_shapes=[
                pltpu.VMEM((PER_CHUNK, 2, n_seg * seg_rows, WIDTH), bf16),
                pltpu.SemaphoreType.DMA((PER_CHUNK, 2, n_seg)),
                pltpu.SemaphoreType.DMA((PER_CHUNK, 2)),
            ],
            compiler_params=pltpu.CompilerParams(vmem_limit_bytes=KERNEL_BYTES),
            cost_estimate=pl.CostEstimate(flops=0, bytes_accessed=4 << 20, transcendentals=0),
            name=f"collect_{turns[0]}",
        )(by_segment, returned, *before)

    def exchange(array):
        return lax.all_to_all(array, "enc", split_axis=0, concat_axis=0, tiled=True)

    first, second = chunks
    received = [xor_permute(array, "enc", k) for k, array in enumerate(route(first, 0))]
    routed, *prepared = route(second, 1)
    *received, routed = lax.optimization_barrier((*received, routed))
    received_later = exchange(routed)
    butterfly = n_seq == KVH
    returned, *grads = attend(first, 1, received)
    answer = exchange(returned)
    if butterfly:
        passed = xor_permute(grads[0], "seq", 1)
    received_later, grads[1] = lax.optimization_barrier((received_later, grads[1]))
    returned, *more = attend(second, 1, [received_later])
    answer, returned = lax.optimization_barrier((answer, returned))
    answer_later = exchange(returned)
    if butterfly:
        passed, grads[1], more[0] = lax.optimization_barrier((passed, grads[1], more[0]))
        pair = (grads[1].astype(f32) + passed.astype(f32)).astype(bf16)
        pair = xor_permute(pair, "seq", 2)
        near = xor_permute(more[0], "seq", 1)
    half = collect(first, answer, [])
    attended, grad_queries = collect(second, answer_later, half)

    if butterfly:
        summed = [
            sum(term[j, :tokens].astype(f32) for term in (more[1], near, pair)).astype(bf16)
            for j in range(2)
        ]
        return attended, grad_queries, summed[0][None], summed[1][None]
    joined = jnp.concatenate(grads + more, axis=2)[:, :tokens]
    summed = lax.psum_scatter(joined, "seq", scatter_dimension=2, tiled=True)
    return attended, grad_queries, summed[0][None], summed[1][None]


def solution(mesh):
    placed = (
        P(("seq", "enc"), None),
        P("enc", None, None),
        P("enc", None, None),
        P(),
        P(("seq", "enc"), None),
    )
    return jax.shard_map(
        per_device,
        mesh=mesh,
        in_specs=placed,
        out_specs=(
            P(("seq", "enc"), None),
            P(("seq", "enc"), None),
            P("enc", None, "seq"),
            P("enc", None, "seq"),
        ),
        check_vma=False,
    )
```

```python
import functools

import jax
import jax.numpy as jnp
from jax import lax
from jax.experimental import pallas as pl
from jax.experimental.pallas import tpu as pltpu
from jax.sharding import PartitionSpec as P

HQ = 32
KVH = 4
HD = 128
GROUP = HQ // KVH
WIDTH = GROUP * HD
SCALE = HD ** (-0.5)
LOG2E = 1.4426950408889634
CHUNK = 512
SLICE = 128
LOWEST = -3.0e38
PER_CHUNK = 2
VMEM_BYTES = 63 << 20
ANY = pl.BlockSpec(memory_space=pl.ANY)
SMEM = pl.BlockSpec(memory_space=pltpu.SMEM)
VMEM = pl.BlockSpec(memory_space=pltpu.VMEM)


def head_at(turn):
    if lax.axis_size("seq") == KVH:
        return lax.axis_index("seq") ^ (KVH - 1 - turn)
    return turn


def route_kernel(turns, apart, n_seg, seg_rows, tokens, reads, q_hbm, g_hbm, *refs):
    stage, in_sems, out_sems, *more = refs[-3:] if apart else refs[-6:]
    me = lax.axis_index("enc")
    row = lax.axis_index("seq") * lax.axis_size("enc") + me
    arriving = [[] for _ in range(n_seg)]
    for r in range(n_seg):
        rows = slice(r * seg_rows, (r + 1) * seg_rows)
        for i, turn in enumerate(turns):
            columns = pl.ds(pl.multiple_of(head_at(turn) * WIDTH, WIDTH), WIDTH)
            for which, source in enumerate((q_hbm, g_hbm)):
                arriving[r].append(
                    pltpu.make_async_copy(
                        source.at[rows, columns],
                        stage.at[r, i, which],
                        in_sems.at[r, i, which],
                    )
                )

    def leaving(r, target):
        return pltpu.make_async_copy(stage.at[r], target, out_sems.at[r])

    for copies in arriving:
        for copy in copies:
            copy.start()
    for r, copies in enumerate(arriving):
        for copy in copies:
            copy.wait()
        if apart:
            for k, out in enumerate(refs[:-3]):

                @pl.when(reads[r, row] == me ^ k)
                def _():
                    leaving(r, out).start()

        else:
            leaving(r, refs[2].at[reads[r, row]]).start()
    if not apart:
        k_in, v_in, _, *targets = refs[:5]
        straight, turned, cache_sems = more
        prepare(tokens, k_in, v_in, straight, turned)
        copies = [
            pltpu.make_async_copy(source, target.at[pl.ds(0, KVH)], cache_sems.at[i])
            for i, (source, target) in enumerate(((straight, targets[0]), (turned, targets[1])))
        ]
        for copy in copies:
            copy.start()
        for copy in copies:
            copy.wait()
    for r in range(n_seg):
        leaving(r, refs[0] if apart else refs[2].at[0]).wait()


def collect_kernel(turns, n_seg, seg_rows, reads, returned, *refs):
    o_hbm, dq_hbm, stage, in_sems, out_sems = refs[-5:]
    row = lax.axis_index("seq") * lax.axis_size("enc") + lax.axis_index("enc")
    arriving, leaving = [], []
    for i, turn in enumerate(turns):
        columns = pl.ds(pl.multiple_of(head_at(turn) * WIDTH, WIDTH), WIDTH)
        for which, target in enumerate((o_hbm, dq_hbm)):
            arriving.append(
                [
                    pltpu.make_async_copy(
                        returned.at[reads[r, row], i, which],
                        stage.at[i, which, r * seg_rows : (r + 1) * seg_rows, :],
                        in_sems.at[i, which, r],
                    )
                    for r in range(n_seg)
                ]
            )
            leaving.append(
                pltpu.make_async_copy(
                    stage.at[i, which], target.at[:, columns], out_sems.at[i, which]
                )
            )
    for copies in arriving:
        for copy in copies:
            copy.start()
    for copies, out in zip(arriving, leaving):
        for copy in copies:
            copy.wait()
        out.start()
    for out in leaving:
        out.wait()


def is_read(reads, row, image):
    found = jnp.int32(0)
    for r in range(reads.shape[0]):
        found = found + (reads[r, row] == image).astype(jnp.int32)
    return found > 0


def prepare(tokens, k_in, v_in, straight, turned):
    padded = straight.shape[2]
    whole = tokens // 16 * 16
    for which, source in enumerate((k_in, v_in)):
        for head in range(KVH):
            columns = slice(head * HD, (head + 1) * HD)
            straight[head, which, 0:whole, :] = source[0, 0:whole, columns]
            if whole < tokens:
                last = jnp.zeros((padded - tokens, HD), jnp.bfloat16)
                straight[head, which, whole:padded, :] = jnp.concatenate(
                    [source[0, whole:tokens, columns], last], axis=0
                )
            turned[head, which] = (
                straight[head, which].astype(jnp.float32).T.astype(jnp.bfloat16)
            )


def attend_kernel(turns, offset, before, peers, seg_rows, tokens, reads, caches, turned_caches, *refs):
    outs = 1 + len(turns)
    received, refs = refs[: len(refs) - 14 - outs], refs[len(refs) - 14 - outs :]
    received = received[: len(received) - before]
    returned, grads = refs[0], refs[1:outs]
    (
        straight,
        turned,
        inbox,
        outbox,
        scores,
        even_odd,
        dscores,
        sums,
        staged,
        owners,
        kv_sems,
        in_sems,
        out_sems,
        grad_sems,
    ) = refs[outs:]
    me = lax.axis_index("enc")
    base = lax.axis_index("seq") * peers
    slots = inbox.shape[1]
    padded = straight.shape[2]
    pieces = [(a, min(a + CHUNK, padded)) for a in range(0, padded, CHUNK)]
    lanes = GROUP * seg_rows
    f32, bf16 = jnp.float32, jnp.bfloat16

    kv_copies = [
        [
            pltpu.make_async_copy(
                source.at[head_at(turn), which], target.at[i, which], kv_sems.at[i, j]
            )
            for j, (source, target, which) in enumerate(
                (
                    (caches, straight, 0),
                    (turned_caches, turned, 1),
                    (caches, straight, 1),
                    (turned_caches, turned, 0),
                )
            )
        ]
        for i, turn in enumerate(turns)
    ]

    def arriving(i, slot, k):
        source = received[k] if len(received) > 1 else received[0].at[me ^ k]
        return pltpu.make_async_copy(source.at[offset + i], inbox.at[i, slot], in_sems.at[i, slot])

    def leaving(i, slot, owner):
        return pltpu.make_async_copy(
            outbox.at[i, slot], returned.at[owner, offset + i], out_sems.at[i, slot]
        )

    def handing(i):
        return pltpu.make_async_copy(staged.at[i], grads[i], grad_sems.at[i])

    for copies in kv_copies:
        copies[0].start()
    count = jnp.int32(0)
    for k in range(peers):
        found = is_read(reads, base + (me ^ k), me)

        @pl.when(found)
        def _():
            owners[count] = me ^ k
            for i in range(len(turns)):
                arriving(i, count, k).start()

        count = count + found.astype(jnp.int32)
    for j in range(1, 4):
        for copies in kv_copies:
            copies[j].start()

    sums[...] = jnp.zeros_like(sums)

    def stacked(i, slot, which):
        return jnp.concatenate(
            [inbox[i, slot, which, :, h * HD : (h + 1) * HD] for h in range(GROUP)], axis=0
        )

    def store(i, slot, which, turned_value):
        value = turned_value.T.astype(bf16)
        for h in range(GROUP):
            outbox[i, slot, which, :, h * HD : (h + 1) * HD] = value[
                h * seg_rows : (h + 1) * seg_rows, :
            ]

    def slices(a, b):
        return [(c, min(c + SLICE, b)) for c in range(a, b, SLICE)]

    def folded(value, reduce):
        return reduce(value.reshape(-1, 8, lanes), axis=0)

    def forward(u, i, slot, weights):
        source = jnp.minimum(slot, count - 1)
        q_turned = stacked(i, source, 0).astype(f32).T.astype(bf16)
        tops, totals, outs = [], [], []

        def score():
            part = jnp.dot(straight[i, 0], q_turned, preferred_element_type=f32)
            for c, d in slices(0, padded):
                piece = part[c:d, :]
                if d > tokens:
                    token = lax.broadcasted_iota(jnp.int32, piece.shape, 0) + c
                    piece = jnp.where(token < tokens, piece, LOWEST)
                scores[u, c:d, :] = piece
                tops.append(folded(piece, jnp.max))

        def weigh(a, b):
            if a == 0:
                tops[:] = [jnp.max(functools.reduce(jnp.maximum, tops), axis=0, keepdims=True)]
            for c, d in slices(a, b):
                piece = jnp.exp2((scores[u, c:d, :] - tops[0]) * (SCALE * LOG2E))
                totals.append(folded(piece, jnp.sum))
                weights[u, c:d, :] = piece.astype(bf16)
            outs.append(
                jnp.dot(turned[i, 1, :, a:b], weights[u, a:b, :], preferred_element_type=f32)
            )

        def finish():
            total = jnp.sum(functools.reduce(jnp.add, totals), axis=0, keepdims=True)
            inverse = 1.0 / total
            share = inverse * (slot < count).astype(f32)
            out = functools.reduce(jnp.add, outs) * inverse
            store(i, slot, 0, out)
            g = (stacked(i, source, 1).astype(f32).T * share).astype(bf16)
            exact = g.astype(f32)
            delta = jnp.sum(exact * out.astype(bf16).astype(f32), axis=0, keepdims=True)
            return delta, g, exact.T.astype(bf16)

        return score, weigh, finish

    def backward(u, i, slot, weights, delta, g_turned, g):
        q = stacked(i, jnp.minimum(slot, count - 1), 0)
        turned_dq = []

        def values_part(a, b):
            dprob = jnp.dot(straight[i, 1, a:b, :], g_turned, preferred_element_type=f32)
            for c, d in slices(a, b):
                piece = weights[u, c:d, :].astype(f32) * (dprob[c - a : d - a, :] - delta)
                dscores[u, c:d, :] = piece.astype(bf16)

        def values_sum():
            sums[i, 1] += jnp.dot(weights[u], g, preferred_element_type=f32)

        def keys_sum():
            sums[i, 0] += jnp.dot(dscores[u], q, preferred_element_type=f32)

        def queries_part(a, b):
            turned_dq.append(
                jnp.dot(turned[i, 0, :, a:b], dscores[u, a:b, :], preferred_element_type=f32)
            )

        def finish():
            store(i, slot, 1, functools.reduce(jnp.add, turned_dq) * SCALE)

        return values_part, values_sum, keys_sum, queries_part, finish

    paired = len(turns) == 2
    steps = count if paired else (count + 1) // 2

    def unit(u, step):
        return (u, step) if paired else (0, 2 * step + u)

    def await_step(step):
        for u in range(2):
            i, slot = unit(u, step)

            @pl.when(slot < count)
            def _():
                arriving(i, slot, 0).wait()

    def one_step(step, carry, last=False):
        weights, next_weights = even_odd.at[step & 1], even_odd.at[(step + 1) & 1]
        behind = [backward(u, *unit(u, step), weights, *carry[u]) for u in range(2)]
        ahead = []
        if not last:
            await_step(step + 1)
            ahead = [forward(u, *unit(u, step + 1), next_weights) for u in range(2)]

        for score, _, _ in ahead:
            score()
        for a, b in pieces:
            for values_part, *_ in behind:
                values_part(a, b)
        for _, values_sum, keys_sum, _, _ in behind:
            values_sum()
            keys_sum()
        for a, b in pieces:
            for _, weigh, _ in ahead:
                weigh(a, b)
            for _, _, _, queries_part, _ in behind:
                queries_part(a, b)
        for *_, finish in behind:
            finish()
        carry = [finish() for _, _, finish in ahead]
        for u in range(2):
            i, slot = unit(u, step)

            @pl.when(slot < count)
            def _():
                leaving(i, slot, owners[slot]).start()

        return carry

    heads = range(len(turns))

    @pl.when(count > 0)
    def _():
        await_step(0)
        for i in heads:
            kv_copies[i][0].wait()
        first = [forward(u, *unit(u, 0), even_odd.at[0]) for u in range(2)]
        for score, _, _ in first:
            score()
        for i in heads:
            kv_copies[i][1].wait()
        for a, b in pieces:
            for _, weigh, _ in first:
                weigh(a, b)
        carry = [finish() for _, _, finish in first]
        for i in heads:
            kv_copies[i][2].wait()
            kv_copies[i][3].wait()
        carry = lax.fori_loop(0, steps - 1, one_step, carry)
        one_step(steps - 1, carry, last=True)
        for i in heads:
            staged[i, 0] = (sums[i, 0] * SCALE).astype(bf16)
            staged[i, 1] = sums[i, 1].astype(bf16)
            handing(i).start()

    @pl.when(count == 0)
    def _():
        staged[...] = jnp.zeros_like(staged)
        for i in range(len(turns)):
            for copy in kv_copies[i]:
                copy.wait()
            handing(i).start()

    for i in range(len(turns)):
        for slot in range(slots):

            @pl.when(slot < count)
            def _():
                leaving(i, slot, 0).wait()

        handing(i).wait()


def xor_permute(array, axis, k):
    if k == 0:
        return array
    size = lax.axis_size(axis)
    return lax.ppermute(array, axis, [(i, i ^ k) for i in range(size)])


def per_device(queries, keys, values, reads, grad_out):
    peers = lax.axis_size("enc")
    n_seq = lax.axis_size("seq")
    n_seg = reads.shape[1]
    by_segment = reads.T
    seg_rows = queries.shape[0] // n_seg
    slots = min(peers, 3 * n_seg // 2)
    tokens = keys.shape[1]
    padded = (tokens + 15) // 16 * 16
    lanes = GROUP * seg_rows
    bf16, f32 = jnp.bfloat16, jnp.float32
    chunks = [tuple(range(i, i + PER_CHUNK)) for i in range(0, KVH, PER_CHUNK)]
    message = jax.ShapeDtypeStruct((peers, PER_CHUNK, 2, seg_rows, WIDTH), bf16)
    part = jax.ShapeDtypeStruct((PER_CHUNK, 2, seg_rows, WIDTH), bf16)

    caches = [
        jax.ShapeDtypeStruct((KVH, 2, padded, HD), bf16),
        jax.ShapeDtypeStruct((KVH, 2, HD, padded), bf16),
    ]

    def route(turns, prepares):
        outputs = [message] + caches if prepares else [part] * peers
        return pl.pallas_call(
            functools.partial(route_kernel, turns, not prepares, n_seg, seg_rows, tokens),
            out_shape=outputs,
            in_specs=[SMEM, ANY, ANY] + [VMEM] * 2 * prepares,
            out_specs=[ANY] * len(outputs),
            scratch_shapes=[
                pltpu.VMEM((n_seg, PER_CHUNK, 2, seg_rows, WIDTH), bf16),
                pltpu.SemaphoreType.DMA((n_seg, PER_CHUNK, 2)),
                pltpu.SemaphoreType.DMA((n_seg,)),
            ]
            + [
                pltpu.VMEM((KVH, 2, padded, HD), bf16),
                pltpu.VMEM((KVH, 2, HD, padded), bf16),
                pltpu.SemaphoreType.DMA((2,)),
            ]
            * prepares,
            compiler_params=pltpu.CompilerParams(vmem_limit_bytes=VMEM_BYTES),
            cost_estimate=pl.CostEstimate(
                flops=0, bytes_accessed=(2 + 10 * prepares) << 20, transcendentals=0
            ),
            name=f"route_{turns[0]}",
        )(by_segment, queries, grad_out, *[keys, values] * prepares)

    def attend(turns, offset, received, before):
        work = slots * lanes * tokens * HD * len(turns)
        grad = jax.ShapeDtypeStruct((2, padded, HD), bf16)
        room = slots + slots % 2
        return pl.pallas_call(
            functools.partial(
                attend_kernel, turns, offset, len(before), peers, seg_rows, tokens
            ),
            out_shape=[message] + [grad] * len(turns),
            in_specs=[SMEM] + [ANY] * (2 + len(received) + len(before)),
            out_specs=[ANY] * (1 + len(turns)),
            input_output_aliases={3 + len(received): 0} if before else {},
            scratch_shapes=[
                pltpu.VMEM((len(turns), 2, padded, HD), bf16),
                pltpu.VMEM((len(turns), 2, HD, padded), bf16),
                pltpu.VMEM((len(turns), slots, 2, seg_rows, WIDTH), bf16),
                pltpu.VMEM((len(turns), room, 2, seg_rows, WIDTH), bf16),
                pltpu.VMEM((2, padded, lanes), f32),
                pltpu.VMEM((2, 2, padded, lanes), bf16),
                pltpu.VMEM((2, padded, lanes), bf16),
                pltpu.VMEM((len(turns), 2, padded, HD), f32),
                pltpu.VMEM((len(turns), 2, padded, HD), bf16),
                pltpu.SMEM((slots,), jnp.int32),
                pltpu.SemaphoreType.DMA((len(turns), 4)),
                pltpu.SemaphoreType.DMA((len(turns), slots)),
                pltpu.SemaphoreType.DMA((len(turns), slots)),
                pltpu.SemaphoreType.DMA((len(turns),)),
            ],
            compiler_params=pltpu.CompilerParams(vmem_limit_bytes=VMEM_BYTES),
            cost_estimate=pl.CostEstimate(
                flops=12 * work if len(turns) == 2 else work,
                bytes_accessed=8 << 20 if len(turns) == 2 else 1 << 20,
                transcendentals=slots * lanes * tokens if len(turns) == 2 else 0,
            ),
            name=f"attend_{turns[0]}",
        )(by_segment, *prepared, *received, *before)

    def collect(turns, returned, before):
        whole = jax.ShapeDtypeStruct(queries.shape, bf16)
        return pl.pallas_call(
            functools.partial(collect_kernel, turns, n_seg, seg_rows),
            out_shape=[whole, whole],
            in_specs=[SMEM, ANY] + [ANY] * len(before),
            out_specs=[ANY, ANY],
            input_output_aliases={2: 0, 3: 1} if before else {},
            scratch_shapes=[
                pltpu.VMEM((PER_CHUNK, 2, n_seg * seg_rows, WIDTH), bf16),
                pltpu.SemaphoreType.DMA((PER_CHUNK, 2, n_seg)),
                pltpu.SemaphoreType.DMA((PER_CHUNK, 2)),
            ],
            compiler_params=pltpu.CompilerParams(vmem_limit_bytes=VMEM_BYTES),
            cost_estimate=pl.CostEstimate(flops=0, bytes_accessed=4 << 20, transcendentals=0),
            name=f"collect_{turns[0]}",
        )(by_segment, returned, *before)

    def exchange(array):
        return lax.all_to_all(array, "enc", split_axis=0, concat_axis=0, tiled=True)

    first, second = chunks
    received = [xor_permute(array, "enc", k) for k, array in enumerate(route(first, 0))]
    routed, *prepared = route(second, 1)
    *received, routed = lax.optimization_barrier((*received, routed))
    received_later = exchange(routed)
    butterfly = n_seq == KVH
    returned, *grads = attend(first[:1], 0, received, [])
    if butterfly:
        passed = xor_permute(grads[0], "seq", 1)
    returned, last = attend(first[1:], 1, received, [returned])
    grads.append(last)
    if butterfly:
        passed, last = lax.optimization_barrier((passed, last))
        pair = [(last[j].astype(f32) + passed[j].astype(f32)).astype(bf16) for j in range(2)]
        returned, *pair = lax.optimization_barrier((returned, *pair))
        pair = [xor_permute(one, "seq", 2) for one in pair]
    answer = exchange(returned)
    received_later, returned = lax.optimization_barrier((received_later, returned))
    returned, *more = attend(second, 0, [received_later], [])
    if butterfly:
        pair[0], returned = lax.optimization_barrier((pair[0], returned))
    answer, returned = lax.optimization_barrier((answer, returned))
    answer_later = exchange(returned)
    if butterfly:
        near = xor_permute(more[0], "seq", 1)
    half = collect(first, answer, [])
    attended, grad_queries = collect(second, answer_later, half)

    if butterfly:
        summed = [
            sum(
                term[:tokens].astype(f32) for term in (more[1][j], near[j], pair[j])
            ).astype(bf16)
            for j in range(2)
        ]
        return attended, grad_queries, summed[0][None], summed[1][None]
    joined = jnp.concatenate(grads + more, axis=2)[:, :tokens]
    summed = lax.psum_scatter(joined, "seq", scatter_dimension=2, tiled=True)
    return attended, grad_queries, summed[0][None], summed[1][None]


def solution(mesh):
    placed = (
        P(("seq", "enc"), None),
        P("enc", None, None),
        P("enc", None, None),
        P(),
        P(("seq", "enc"), None),
    )
    return jax.shard_map(
        per_device,
        mesh=mesh,
        in_specs=placed,
        out_specs=(
            P(("seq", "enc"), None),
            P(("seq", "enc"), None),
            P("enc", None, "seq"),
            P("enc", None, "seq"),
        ),
        check_vma=False,
    )
```

```python
import functools

import jax
import jax.numpy as jnp
from jax import lax
from jax.experimental import pallas as pl
from jax.experimental.pallas import tpu as pltpu
from jax.sharding import PartitionSpec as P

HQ = 32
KVH = 4
HD = 128
GROUP = HQ // KVH
WIDTH = GROUP * HD
SCALE = HD ** (-0.5)
LOG2E = 1.4426950408889634
CHUNK = 512
SLICE = 128
LOWEST = -3.0e38
PER_CHUNK = 2
VMEM_BYTES = 63 << 20
ANY = pl.BlockSpec(memory_space=pl.ANY)
SMEM = pl.BlockSpec(memory_space=pltpu.SMEM)
VMEM = pl.BlockSpec(memory_space=pltpu.VMEM)


def head_at(turn):
    if lax.axis_size("seq") == KVH:
        return lax.axis_index("seq") ^ (KVH - 1 - turn)
    return turn


def route_kernel(turns, apart, n_seg, seg_rows, tokens, reads, q_hbm, g_hbm, *refs):
    stage, in_sems, out_sems, *more = refs[-3:] if apart else refs[-6:]
    me = lax.axis_index("enc")
    row = lax.axis_index("seq") * lax.axis_size("enc") + me
    arriving = [[] for _ in range(n_seg)]
    for r in range(n_seg):
        rows = slice(r * seg_rows, (r + 1) * seg_rows)
        for i, turn in enumerate(turns):
            columns = pl.ds(pl.multiple_of(head_at(turn) * WIDTH, WIDTH), WIDTH)
            for which, source in enumerate((q_hbm, g_hbm)):
                arriving[r].append(
                    pltpu.make_async_copy(
                        source.at[rows, columns],
                        stage.at[r, i, which],
                        in_sems.at[r, i, which],
                    )
                )

    def leaving(r, target):
        return pltpu.make_async_copy(stage.at[r], target, out_sems.at[r])

    for copies in arriving:
        for copy in copies:
            copy.start()
    for r, copies in enumerate(arriving):
        for copy in copies:
            copy.wait()
        if apart:
            for k, out in enumerate(refs[:-3]):

                @pl.when(reads[r, row] == me ^ k)
                def _():
                    leaving(r, out).start()

        else:
            leaving(r, refs[2].at[reads[r, row]]).start()
    if not apart:
        k_in, v_in, _, *targets = refs[:5]
        straight, turned, cache_sems = more
        prepare(tokens, k_in, v_in, straight, turned)
        copies = [
            pltpu.make_async_copy(source, target.at[pl.ds(0, KVH)], cache_sems.at[i])
            for i, (source, target) in enumerate(((straight, targets[0]), (turned, targets[1])))
        ]
        for copy in copies:
            copy.start()
        for copy in copies:
            copy.wait()
    for r in range(n_seg):
        leaving(r, refs[0] if apart else refs[2].at[0]).wait()


def collect_kernel(turns, n_seg, seg_rows, reads, returned, *refs):
    o_hbm, dq_hbm, stage, in_sems, out_sems = refs[-5:]
    row = lax.axis_index("seq") * lax.axis_size("enc") + lax.axis_index("enc")
    arriving, leaving = [], []
    for i, turn in enumerate(turns):
        columns = pl.ds(pl.multiple_of(head_at(turn) * WIDTH, WIDTH), WIDTH)
        for which, target in enumerate((o_hbm, dq_hbm)):
            arriving.append(
                [
                    pltpu.make_async_copy(
                        returned.at[reads[r, row], i, which],
                        stage.at[i, which, r * seg_rows : (r + 1) * seg_rows, :],
                        in_sems.at[i, which, r],
                    )
                    for r in range(n_seg)
                ]
            )
            leaving.append(
                pltpu.make_async_copy(
                    stage.at[i, which], target.at[:, columns], out_sems.at[i, which]
                )
            )
    for copies in arriving:
        for copy in copies:
            copy.start()
    for copies, out in zip(arriving, leaving):
        for copy in copies:
            copy.wait()
        out.start()
    for out in leaving:
        out.wait()


def is_read(reads, row, image):
    found = jnp.int32(0)
    for r in range(reads.shape[0]):
        found = found + (reads[r, row] == image).astype(jnp.int32)
    return found > 0


def prepare(tokens, k_in, v_in, straight, turned):
    padded = straight.shape[2]
    whole = tokens // 16 * 16
    for which, source in enumerate((k_in, v_in)):
        for head in range(KVH):
            columns = slice(head * HD, (head + 1) * HD)
            straight[head, which, 0:whole, :] = source[0, 0:whole, columns]
            if whole < tokens:
                last = jnp.zeros((padded - tokens, HD), jnp.bfloat16)
                straight[head, which, whole:padded, :] = jnp.concatenate(
                    [source[0, whole:tokens, columns], last], axis=0
                )
            turned[head, which] = (
                straight[head, which].astype(jnp.float32).T.astype(jnp.bfloat16)
            )


def attend_kernel(turns, offset, before, peers, seg_rows, tokens, reads, caches, turned_caches, *refs):
    outs = 1 + len(turns)
    received, refs = refs[: len(refs) - 14 - outs], refs[len(refs) - 14 - outs :]
    received = received[: len(received) - before]
    returned, grads = refs[0], refs[1:outs]
    (
        straight,
        turned,
        inbox,
        outbox,
        scores,
        even_odd,
        dscores,
        sums,
        staged,
        owners,
        kv_sems,
        in_sems,
        out_sems,
        grad_sems,
    ) = refs[outs:]
    me = lax.axis_index("enc")
    base = lax.axis_index("seq") * peers
    slots = inbox.shape[1]
    padded = straight.shape[2]
    pieces = [(a, min(a + CHUNK, padded)) for a in range(0, padded, CHUNK)]
    lanes = GROUP * seg_rows
    f32, bf16 = jnp.float32, jnp.bfloat16

    kv_copies = [
        [
            pltpu.make_async_copy(
                source.at[head_at(turn), which], target.at[i, which], kv_sems.at[i, j]
            )
            for j, (source, target, which) in enumerate(
                (
                    (caches, straight, 0),
                    (turned_caches, turned, 1),
                    (caches, straight, 1),
                    (turned_caches, turned, 0),
                )
            )
        ]
        for i, turn in enumerate(turns)
    ]

    def arriving(i, slot, k):
        source = received[k] if len(received) > 1 else received[0].at[me ^ k]
        return pltpu.make_async_copy(source.at[offset + i], inbox.at[i, slot], in_sems.at[i, slot])

    def leaving(i, slot, owner):
        return pltpu.make_async_copy(
            outbox.at[i, slot], returned.at[owner, offset + i], out_sems.at[i, slot]
        )

    def handing(i):
        return pltpu.make_async_copy(staged.at[i], grads[i], grad_sems.at[i])

    for copies in kv_copies:
        copies[0].start()
    count = jnp.int32(0)
    for k in range(peers):
        found = is_read(reads, base + (me ^ k), me)

        @pl.when(found)
        def _():
            owners[count] = me ^ k
            for i in range(len(turns)):
                arriving(i, count, k).start()

        count = count + found.astype(jnp.int32)
    for j in range(1, 4):
        for copies in kv_copies:
            copies[j].start()

    sums[...] = jnp.zeros_like(sums)

    def stacked(i, slot, which):
        return jnp.concatenate(
            [inbox[i, slot, which, :, h * HD : (h + 1) * HD] for h in range(GROUP)], axis=0
        )

    def store(i, slot, which, turned_value):
        value = turned_value.T.astype(bf16)
        for h in range(GROUP):
            outbox[i, slot, which, :, h * HD : (h + 1) * HD] = value[
                h * seg_rows : (h + 1) * seg_rows, :
            ]

    def slices(a, b):
        return [(c, min(c + SLICE, b)) for c in range(a, b, SLICE)]

    def folded(value, reduce):
        return reduce(value.reshape(-1, 8, lanes), axis=0)

    def forward(u, i, slot, weights):
        source = jnp.minimum(slot, count - 1)
        q_turned = stacked(i, source, 0).astype(f32).T.astype(bf16)
        tops, totals, outs = [], [], []

        def score():
            part = jnp.dot(straight[i, 0], q_turned, preferred_element_type=f32)
            for c, d in slices(0, padded):
                piece = part[c:d, :]
                if d > tokens:
                    token = lax.broadcasted_iota(jnp.int32, piece.shape, 0) + c
                    piece = jnp.where(token < tokens, piece, LOWEST)
                scores[u, c:d, :] = piece
                tops.append(folded(piece, jnp.max))

        def weigh(a, b):
            if a == 0:
                tops[:] = [jnp.max(functools.reduce(jnp.maximum, tops), axis=0, keepdims=True)]
            for c, d in slices(a, b):
                piece = jnp.exp2((scores[u, c:d, :] - tops[0]) * (SCALE * LOG2E))
                totals.append(folded(piece, jnp.sum))
                weights[u, c:d, :] = piece.astype(bf16)
            outs.append(
                jnp.dot(turned[i, 1, :, a:b], weights[u, a:b, :], preferred_element_type=f32)
            )

        def finish():
            total = jnp.sum(functools.reduce(jnp.add, totals), axis=0, keepdims=True)
            inverse = 1.0 / total
            share = inverse * (slot < count).astype(f32)
            out = functools.reduce(jnp.add, outs) * inverse
            store(i, slot, 0, out)
            g = (stacked(i, source, 1).astype(f32).T * share).astype(bf16)
            exact = g.astype(f32)
            delta = jnp.sum(exact * out.astype(bf16).astype(f32), axis=0, keepdims=True)
            return delta, g, exact.T.astype(bf16)

        return score, weigh, finish

    def backward(u, i, slot, weights, delta, g_turned, g):
        q = stacked(i, jnp.minimum(slot, count - 1), 0)
        turned_dq = []

        def values_part(a, b):
            dprob = jnp.dot(straight[i, 1, a:b, :], g_turned, preferred_element_type=f32)
            for c, d in slices(a, b):
                piece = weights[u, c:d, :].astype(f32) * (dprob[c - a : d - a, :] - delta)
                dscores[u, c:d, :] = piece.astype(bf16)

        def values_sum():
            sums[i, 1] += jnp.dot(weights[u], g, preferred_element_type=f32)

        def keys_sum():
            sums[i, 0] += jnp.dot(dscores[u], q, preferred_element_type=f32)

        def queries_part(a, b):
            turned_dq.append(
                jnp.dot(turned[i, 0, :, a:b], dscores[u, a:b, :], preferred_element_type=f32)
            )

        def finish():
            store(i, slot, 1, functools.reduce(jnp.add, turned_dq) * SCALE)

        return values_part, values_sum, keys_sum, queries_part, finish

    paired = len(turns) == 2
    steps = count if paired else (count + 1) // 2

    def unit(u, step):
        return (u, step) if paired else (0, 2 * step + u)

    def await_step(step):
        for u in range(2):
            i, slot = unit(u, step)

            @pl.when(slot < count)
            def _():
                arriving(i, slot, 0).wait()

    def one_step(step, carry, last=False):
        weights, next_weights = even_odd.at[step & 1], even_odd.at[(step + 1) & 1]
        behind = [backward(u, *unit(u, step), weights, *carry[u]) for u in range(2)]
        ahead = []
        if not last:
            await_step(step + 1)
            ahead = [forward(u, *unit(u, step + 1), next_weights) for u in range(2)]

        for score, _, _ in ahead:
            score()
        for a, b in pieces:
            for values_part, *_ in behind:
                values_part(a, b)
        for _, values_sum, keys_sum, _, _ in behind:
            values_sum()
            keys_sum()
        for a, b in pieces:
            for _, weigh, _ in ahead:
                weigh(a, b)
            for _, _, _, queries_part, _ in behind:
                queries_part(a, b)
        for *_, finish in behind:
            finish()
        carry = [finish() for _, _, finish in ahead]
        for u in range(2):
            i, slot = unit(u, step)

            @pl.when(slot < count)
            def _():
                leaving(i, slot, owners[slot]).start()

        return carry

    heads = range(len(turns))

    @pl.when(count > 0)
    def _():
        await_step(0)
        for i in heads:
            kv_copies[i][0].wait()
        first = [forward(u, *unit(u, 0), even_odd.at[0]) for u in range(2)]
        for score, _, _ in first:
            score()
        for i in heads:
            kv_copies[i][1].wait()
        for a, b in pieces:
            for _, weigh, _ in first:
                weigh(a, b)
        carry = [finish() for _, _, finish in first]
        for i in heads:
            kv_copies[i][2].wait()
            kv_copies[i][3].wait()
        carry = lax.fori_loop(0, steps - 1, one_step, carry)
        one_step(steps - 1, carry, last=True)
        for i in heads:
            staged[i, 0] = (sums[i, 0] * SCALE).astype(bf16)
            staged[i, 1] = sums[i, 1].astype(bf16)
            handing(i).start()

    @pl.when(count == 0)
    def _():
        staged[...] = jnp.zeros_like(staged)
        for i in range(len(turns)):
            for copy in kv_copies[i]:
                copy.wait()
            handing(i).start()

    for i in range(len(turns)):
        for slot in range(slots):

            @pl.when(slot < count)
            def _():
                leaving(i, slot, 0).wait()

        handing(i).wait()


def xor_permute(array, axis, k):
    if k == 0:
        return array
    size = lax.axis_size(axis)
    return lax.ppermute(array, axis, [(i, i ^ k) for i in range(size)])


def per_device(queries, keys, values, reads, grad_out):
    peers = lax.axis_size("enc")
    n_seq = lax.axis_size("seq")
    n_seg = reads.shape[1]
    by_segment = reads.T
    seg_rows = queries.shape[0] // n_seg
    slots = min(peers, 3 * n_seg // 2)
    tokens = keys.shape[1]
    padded = (tokens + 15) // 16 * 16
    lanes = GROUP * seg_rows
    bf16, f32 = jnp.bfloat16, jnp.float32
    chunks = [tuple(range(i, i + PER_CHUNK)) for i in range(0, KVH, PER_CHUNK)]
    message = jax.ShapeDtypeStruct((peers, PER_CHUNK, 2, seg_rows, WIDTH), bf16)
    part = jax.ShapeDtypeStruct((PER_CHUNK, 2, seg_rows, WIDTH), bf16)

    caches = [
        jax.ShapeDtypeStruct((KVH, 2, padded, HD), bf16),
        jax.ShapeDtypeStruct((KVH, 2, HD, padded), bf16),
    ]

    def route(turns, prepares):
        outputs = [message] + caches if prepares else [part] * peers
        return pl.pallas_call(
            functools.partial(route_kernel, turns, not prepares, n_seg, seg_rows, tokens),
            out_shape=outputs,
            in_specs=[SMEM, ANY, ANY] + [VMEM] * 2 * prepares,
            out_specs=[ANY] * len(outputs),
            scratch_shapes=[
                pltpu.VMEM((n_seg, PER_CHUNK, 2, seg_rows, WIDTH), bf16),
                pltpu.SemaphoreType.DMA((n_seg, PER_CHUNK, 2)),
                pltpu.SemaphoreType.DMA((n_seg,)),
            ]
            + [
                pltpu.VMEM((KVH, 2, padded, HD), bf16),
                pltpu.VMEM((KVH, 2, HD, padded), bf16),
                pltpu.SemaphoreType.DMA((2,)),
            ]
            * prepares,
            compiler_params=pltpu.CompilerParams(vmem_limit_bytes=VMEM_BYTES),
            cost_estimate=pl.CostEstimate(
                flops=0, bytes_accessed=(2 + 10 * prepares) << 20, transcendentals=0
            ),
            name=f"route_{turns[0]}",
        )(by_segment, queries, grad_out, *[keys, values] * prepares)

    def attend(turns, offset, received, before):
        work = slots * lanes * tokens * HD * len(turns)
        grad = jax.ShapeDtypeStruct((2, padded, HD), bf16)
        room = slots + slots % 2
        return pl.pallas_call(
            functools.partial(
                attend_kernel, turns, offset, len(before), peers, seg_rows, tokens
            ),
            out_shape=[message] + [grad] * len(turns),
            in_specs=[SMEM] + [ANY] * (2 + len(received) + len(before)),
            out_specs=[ANY] * (1 + len(turns)),
            input_output_aliases={3 + len(received): 0} if before else {},
            scratch_shapes=[
                pltpu.VMEM((len(turns), 2, padded, HD), bf16),
                pltpu.VMEM((len(turns), 2, HD, padded), bf16),
                pltpu.VMEM((len(turns), slots, 2, seg_rows, WIDTH), bf16),
                pltpu.VMEM((len(turns), room, 2, seg_rows, WIDTH), bf16),
                pltpu.VMEM((2, padded, lanes), f32),
                pltpu.VMEM((2, 2, padded, lanes), bf16),
                pltpu.VMEM((2, padded, lanes), bf16),
                pltpu.VMEM((len(turns), 2, padded, HD), f32),
                pltpu.VMEM((len(turns), 2, padded, HD), bf16),
                pltpu.SMEM((slots,), jnp.int32),
                pltpu.SemaphoreType.DMA((len(turns), 4)),
                pltpu.SemaphoreType.DMA((len(turns), slots)),
                pltpu.SemaphoreType.DMA((len(turns), slots)),
                pltpu.SemaphoreType.DMA((len(turns),)),
            ],
            compiler_params=pltpu.CompilerParams(vmem_limit_bytes=VMEM_BYTES),
            cost_estimate=pl.CostEstimate(
                flops=12 * work if len(turns) == 2 else work,
                bytes_accessed=8 << 20 if len(turns) == 2 else 1 << 20,
                transcendentals=slots * lanes * tokens if len(turns) == 2 else 0,
            ),
            name=f"attend_{turns[0]}",
        )(by_segment, *prepared, *received, *before)

    def collect(turns, returned, before):
        whole = jax.ShapeDtypeStruct(queries.shape, bf16)
        return pl.pallas_call(
            functools.partial(collect_kernel, turns, n_seg, seg_rows),
            out_shape=[whole, whole],
            in_specs=[SMEM, ANY] + [ANY] * len(before),
            out_specs=[ANY, ANY],
            input_output_aliases={2: 0, 3: 1} if before else {},
            scratch_shapes=[
                pltpu.VMEM((PER_CHUNK, 2, n_seg * seg_rows, WIDTH), bf16),
                pltpu.SemaphoreType.DMA((PER_CHUNK, 2, n_seg)),
                pltpu.SemaphoreType.DMA((PER_CHUNK, 2)),
            ],
            compiler_params=pltpu.CompilerParams(vmem_limit_bytes=VMEM_BYTES),
            cost_estimate=pl.CostEstimate(flops=0, bytes_accessed=4 << 20, transcendentals=0),
            name=f"collect_{turns[0]}",
        )(by_segment, returned, *before)

    def exchange(array):
        return lax.all_to_all(array, "enc", split_axis=0, concat_axis=0, tiled=True)

    def exchange_apart(arrays):
        order = sorted(range(peers), key=lambda k: (-(k >> 1).bit_count(), k & 1, k))
        arrived = {k: xor_permute(arrays[k], "enc", k) for k in order}
        return [arrived[k] for k in range(peers)]

    first, second = chunks
    received = exchange_apart(route(first, 0))
    routed, *prepared = route(second, 1)
    *received, routed = lax.optimization_barrier((*received, routed))
    received_later = exchange(routed)
    butterfly = n_seq == KVH
    returned, *grads = attend(first[:1], 0, received, [])
    if butterfly:
        passed = xor_permute(grads[0], "seq", 1)
    returned, last = attend(first[1:], 1, received, [returned])
    grads.append(last)
    if butterfly:
        passed, last = lax.optimization_barrier((passed, last))
        pair = [(last[j].astype(f32) + passed[j].astype(f32)).astype(bf16) for j in range(2)]
        pair = [xor_permute(one, "seq", 2) for one in pair]
    answer = exchange(returned)
    received_later, returned = lax.optimization_barrier((received_later, returned))
    returned, *more = attend(second, 0, [received_later], [])
    if butterfly:
        pair[0], returned = lax.optimization_barrier((pair[0], returned))
    answer, returned = lax.optimization_barrier((answer, returned))
    answer_later = exchange(returned)
    if butterfly:
        pair[1], turn_two = lax.optimization_barrier((pair[1], more[0]))
        near = xor_permute(turn_two, "seq", 1)
    half = collect(first, answer, [])
    attended, grad_queries = collect(second, answer_later, half)

    if butterfly:
        summed = [
            sum(
                term[:tokens].astype(f32) for term in (more[1][j], near[j], pair[j])
            ).astype(bf16)
            for j in range(2)
        ]
        return attended, grad_queries, summed[0][None], summed[1][None]
    joined = jnp.concatenate(grads + more, axis=2)[:, :tokens]
    summed = lax.psum_scatter(joined, "seq", scatter_dimension=2, tiled=True)
    return attended, grad_queries, summed[0][None], summed[1][None]


def solution(mesh):
    placed = (
        P(("seq", "enc"), None),
        P("enc", None, None),
        P("enc", None, None),
        P(),
        P(("seq", "enc"), None),
    )
    return jax.shard_map(
        per_device,
        mesh=mesh,
        in_specs=placed,
        out_specs=(
            P(("seq", "enc"), None),
            P(("seq", "enc"), None),
            P("enc", None, "seq"),
            P("enc", None, "seq"),
        ),
        check_vma=False,
    )
```

```python
import functools

import jax
import jax.numpy as jnp
from jax import lax
from jax.experimental import pallas as pl
from jax.experimental.pallas import tpu as pltpu
from jax.sharding import PartitionSpec as P

HQ = 32
KVH = 4
HD = 128
GROUP = HQ // KVH
WIDTH = GROUP * HD
SCALE = HD ** (-0.5)
LOG2E = 1.4426950408889634
CHUNK = 512
SLICE = 128
LOWEST = -3.0e38
PER_CHUNK = 2
VMEM_BYTES = 63 << 20
ANY = pl.BlockSpec(memory_space=pl.ANY)
SMEM = pl.BlockSpec(memory_space=pltpu.SMEM)
VMEM = pl.BlockSpec(memory_space=pltpu.VMEM)


def head_at(turn):
    if lax.axis_size("seq") == KVH:
        return lax.axis_index("seq") ^ (KVH - 1 - turn)
    return turn


def route_kernel(turns, apart, n_seg, seg_rows, tokens, reads, q_hbm, g_hbm, *refs):
    stage, in_sems, out_sems, *more = refs[-3:] if apart else refs[-6:]
    me = lax.axis_index("enc")
    row = lax.axis_index("seq") * lax.axis_size("enc") + me
    arriving = [[] for _ in range(n_seg)]
    for r in range(n_seg):
        rows = slice(r * seg_rows, (r + 1) * seg_rows)
        for i, turn in enumerate(turns):
            columns = pl.ds(pl.multiple_of(head_at(turn) * WIDTH, WIDTH), WIDTH)
            for which, source in enumerate((q_hbm, g_hbm)):
                arriving[r].append(
                    pltpu.make_async_copy(
                        source.at[rows, columns],
                        stage.at[r, i, which],
                        in_sems.at[r, i, which],
                    )
                )

    def leaving(r, target):
        return pltpu.make_async_copy(stage.at[r], target, out_sems.at[r])

    for copies in arriving:
        for copy in copies:
            copy.start()
    for r, copies in enumerate(arriving):
        for copy in copies:
            copy.wait()
        if apart:
            for k, out in enumerate(refs[:-3]):

                @pl.when(reads[r, row] == me ^ k)
                def _():
                    leaving(r, out).start()

        else:
            leaving(r, refs[2].at[reads[r, row]]).start()
    if not apart:
        k_in, v_in, _, *targets = refs[:5]
        straight, turned, cache_sems = more
        prepare(tokens, k_in, v_in, straight, turned)
        copies = [
            pltpu.make_async_copy(source, target.at[pl.ds(0, KVH)], cache_sems.at[i])
            for i, (source, target) in enumerate(((straight, targets[0]), (turned, targets[1])))
        ]
        for copy in copies:
            copy.start()
        for copy in copies:
            copy.wait()
    for r in range(n_seg):
        leaving(r, refs[0] if apart else refs[2].at[0]).wait()


def collect_kernel(turns, n_seg, seg_rows, reads, returned, *refs):
    o_hbm, dq_hbm, stage, in_sems, out_sems = refs[-5:]
    row = lax.axis_index("seq") * lax.axis_size("enc") + lax.axis_index("enc")
    arriving, leaving = [], []
    for i, turn in enumerate(turns):
        columns = pl.ds(pl.multiple_of(head_at(turn) * WIDTH, WIDTH), WIDTH)
        for which, target in enumerate((o_hbm, dq_hbm)):
            arriving.append(
                [
                    pltpu.make_async_copy(
                        returned.at[reads[r, row], i, which],
                        stage.at[i, which, r * seg_rows : (r + 1) * seg_rows, :],
                        in_sems.at[i, which, r],
                    )
                    for r in range(n_seg)
                ]
            )
            leaving.append(
                pltpu.make_async_copy(
                    stage.at[i, which], target.at[:, columns], out_sems.at[i, which]
                )
            )
    for copies in arriving:
        for copy in copies:
            copy.start()
    for copies, out in zip(arriving, leaving):
        for copy in copies:
            copy.wait()
        out.start()
    for out in leaving:
        out.wait()


def is_read(reads, row, image):
    found = jnp.int32(0)
    for r in range(reads.shape[0]):
        found = found + (reads[r, row] == image).astype(jnp.int32)
    return found > 0


def prepare(tokens, k_in, v_in, straight, turned):
    padded = straight.shape[2]
    whole = tokens // 16 * 16
    for which, source in enumerate((k_in, v_in)):
        for head in range(KVH):
            columns = slice(head * HD, (head + 1) * HD)
            straight[head, which, 0:whole, :] = source[0, 0:whole, columns]
            if whole < tokens:
                last = jnp.zeros((padded - tokens, HD), jnp.bfloat16)
                straight[head, which, whole:padded, :] = jnp.concatenate(
                    [source[0, whole:tokens, columns], last], axis=0
                )
            turned[head, which] = (
                straight[head, which].astype(jnp.float32).T.astype(jnp.bfloat16)
            )


def attend_kernel(turns, offset, before, peers, seg_rows, tokens, reads, caches, turned_caches, *refs):
    outs = 1 + len(turns)
    received, refs = refs[: len(refs) - 14 - outs], refs[len(refs) - 14 - outs :]
    received = received[: len(received) - before]
    returned, grads = refs[0], refs[1:outs]
    (
        straight,
        turned,
        inbox,
        outbox,
        scores,
        even_odd,
        dscores,
        sums,
        staged,
        owners,
        kv_sems,
        in_sems,
        out_sems,
        grad_sems,
    ) = refs[outs:]
    me = lax.axis_index("enc")
    base = lax.axis_index("seq") * peers
    slots = inbox.shape[1]
    padded = straight.shape[2]
    pieces = [(a, min(a + CHUNK, padded)) for a in range(0, padded, CHUNK)]
    lanes = GROUP * seg_rows
    f32, bf16 = jnp.float32, jnp.bfloat16

    kv_copies = [
        [
            pltpu.make_async_copy(
                source.at[head_at(turn), which], target.at[i, which], kv_sems.at[i, j]
            )
            for j, (source, target, which) in enumerate(
                (
                    (caches, straight, 0),
                    (turned_caches, turned, 1),
                    (caches, straight, 1),
                    (turned_caches, turned, 0),
                )
            )
        ]
        for i, turn in enumerate(turns)
    ]

    def arriving(i, slot, k):
        source = received[k] if len(received) > 1 else received[0].at[me ^ k]
        return pltpu.make_async_copy(source.at[offset + i], inbox.at[i, slot], in_sems.at[i, slot])

    def leaving(i, slot, owner):
        return pltpu.make_async_copy(
            outbox.at[i, slot], returned.at[owner, offset + i], out_sems.at[i, slot]
        )

    def handing(i):
        return pltpu.make_async_copy(staged.at[i], grads[i], grad_sems.at[i])

    for copies in kv_copies:
        copies[0].start()
    count = jnp.int32(0)
    for k in range(peers):
        found = is_read(reads, base + (me ^ k), me)

        @pl.when(found)
        def _():
            owners[count] = me ^ k
            for i in range(len(turns)):
                arriving(i, count, k).start()

        count = count + found.astype(jnp.int32)
    for j in range(1, 4):
        for copies in kv_copies:
            copies[j].start()

    sums[...] = jnp.zeros_like(sums)

    def stacked(i, slot, which):
        return jnp.concatenate(
            [inbox[i, slot, which, :, h * HD : (h + 1) * HD] for h in range(GROUP)], axis=0
        )

    def store(i, slot, which, turned_value):
        value = turned_value.T.astype(bf16)
        for h in range(GROUP):
            outbox[i, slot, which, :, h * HD : (h + 1) * HD] = value[
                h * seg_rows : (h + 1) * seg_rows, :
            ]

    def slices(a, b):
        return [(c, min(c + SLICE, b)) for c in range(a, b, SLICE)]

    def folded(value, reduce):
        return reduce(value.reshape(-1, 8, lanes), axis=0)

    def forward(u, i, slot, weights):
        source = jnp.minimum(slot, count - 1)
        q_turned = stacked(i, source, 0).astype(f32).T.astype(bf16)
        tops, totals, outs = [], [], []

        def score():
            part = jnp.dot(straight[i, 0], q_turned, preferred_element_type=f32)
            for c, d in slices(0, padded):
                piece = part[c:d, :]
                if d > tokens:
                    token = lax.broadcasted_iota(jnp.int32, piece.shape, 0) + c
                    piece = jnp.where(token < tokens, piece, LOWEST)
                scores[u, c:d, :] = piece
                tops.append(folded(piece, jnp.max))

        def weigh(a, b):
            if a == 0:
                tops[:] = [jnp.max(functools.reduce(jnp.maximum, tops), axis=0, keepdims=True)]
            for c, d in slices(a, b):
                piece = jnp.exp2((scores[u, c:d, :] - tops[0]) * (SCALE * LOG2E))
                totals.append(folded(piece, jnp.sum))
                weights[u, c:d, :] = piece.astype(bf16)
            outs.append(
                jnp.dot(turned[i, 1, :, a:b], weights[u, a:b, :], preferred_element_type=f32)
            )

        def finish():
            total = jnp.sum(functools.reduce(jnp.add, totals), axis=0, keepdims=True)
            inverse = 1.0 / total
            share = inverse * (slot < count).astype(f32)
            out = functools.reduce(jnp.add, outs) * inverse
            store(i, slot, 0, out)
            g = (stacked(i, source, 1).astype(f32).T * share).astype(bf16)
            exact = g.astype(f32)
            delta = jnp.sum(exact * out.astype(bf16).astype(f32), axis=0, keepdims=True)
            return delta, g, exact.T.astype(bf16)

        return score, weigh, finish

    def backward(u, i, slot, weights, delta, g_turned, g):
        q = stacked(i, jnp.minimum(slot, count - 1), 0)
        turned_dq = []

        def values_part(a, b):
            dprob = jnp.dot(straight[i, 1, a:b, :], g_turned, preferred_element_type=f32)
            for c, d in slices(a, b):
                piece = weights[u, c:d, :].astype(f32) * (dprob[c - a : d - a, :] - delta)
                dscores[u, c:d, :] = piece.astype(bf16)

        def values_sum():
            sums[i, 1] += jnp.dot(weights[u], g, preferred_element_type=f32)

        def keys_sum():
            sums[i, 0] += jnp.dot(dscores[u], q, preferred_element_type=f32)

        def queries_part(a, b):
            turned_dq.append(
                jnp.dot(turned[i, 0, :, a:b], dscores[u, a:b, :], preferred_element_type=f32)
            )

        def finish():
            store(i, slot, 1, functools.reduce(jnp.add, turned_dq) * SCALE)

        return values_part, values_sum, keys_sum, queries_part, finish

    paired = len(turns) == 2
    steps = count if paired else (count + 1) // 2

    def unit(u, step):
        return (u, step) if paired else (0, 2 * step + u)

    def await_step(step):
        for u in range(2):
            i, slot = unit(u, step)

            @pl.when(slot < count)
            def _():
                arriving(i, slot, 0).wait()

    def one_step(step, carry, last=False):
        weights, next_weights = even_odd.at[step & 1], even_odd.at[(step + 1) & 1]
        behind = [backward(u, *unit(u, step), weights, *carry[u]) for u in range(2)]
        ahead = []
        if not last:
            await_step(step + 1)
            ahead = [forward(u, *unit(u, step + 1), next_weights) for u in range(2)]

        for score, _, _ in ahead:
            score()
        for a, b in pieces:
            for values_part, *_ in behind:
                values_part(a, b)
        for _, values_sum, keys_sum, _, _ in behind:
            values_sum()
            keys_sum()
        for a, b in pieces:
            for _, weigh, _ in ahead:
                weigh(a, b)
            for _, _, _, queries_part, _ in behind:
                queries_part(a, b)
        for *_, finish in behind:
            finish()
        carry = [finish() for _, _, finish in ahead]
        for u in range(2):
            i, slot = unit(u, step)

            @pl.when(slot < count)
            def _():
                leaving(i, slot, owners[slot]).start()

        return carry

    heads = range(len(turns))

    @pl.when(count > 0)
    def _():
        await_step(0)
        for i in heads:
            kv_copies[i][0].wait()
        first = [forward(u, *unit(u, 0), even_odd.at[0]) for u in range(2)]
        for score, _, _ in first:
            score()
        for i in heads:
            kv_copies[i][1].wait()
        for a, b in pieces:
            for _, weigh, _ in first:
                weigh(a, b)
        carry = [finish() for _, _, finish in first]
        for i in heads:
            kv_copies[i][2].wait()
            kv_copies[i][3].wait()
        carry = lax.fori_loop(0, steps - 1, one_step, carry)
        one_step(steps - 1, carry, last=True)
        for i in heads:
            staged[i, 0] = (sums[i, 0] * SCALE).astype(bf16)
            staged[i, 1] = sums[i, 1].astype(bf16)
            handing(i).start()

    @pl.when(count == 0)
    def _():
        staged[...] = jnp.zeros_like(staged)
        for i in range(len(turns)):
            for copy in kv_copies[i]:
                copy.wait()
            handing(i).start()

    for i in range(len(turns)):
        for slot in range(slots):

            @pl.when(slot < count)
            def _():
                leaving(i, slot, 0).wait()

        handing(i).wait()


def xor_permute(array, axis, k):
    if k == 0:
        return array
    size = lax.axis_size(axis)
    return lax.ppermute(array, axis, [(i, i ^ k) for i in range(size)])


def per_device(queries, keys, values, reads, grad_out):
    peers = lax.axis_size("enc")
    n_seq = lax.axis_size("seq")
    n_seg = reads.shape[1]
    by_segment = reads.T
    seg_rows = queries.shape[0] // n_seg
    slots = min(peers, 3 * n_seg // 2)
    tokens = keys.shape[1]
    padded = (tokens + 15) // 16 * 16
    lanes = GROUP * seg_rows
    bf16, f32 = jnp.bfloat16, jnp.float32
    chunks = [tuple(range(i, i + PER_CHUNK)) for i in range(0, KVH, PER_CHUNK)]
    message = jax.ShapeDtypeStruct((peers, PER_CHUNK, 2, seg_rows, WIDTH), bf16)
    part = jax.ShapeDtypeStruct((PER_CHUNK, 2, seg_rows, WIDTH), bf16)

    caches = [
        jax.ShapeDtypeStruct((KVH, 2, padded, HD), bf16),
        jax.ShapeDtypeStruct((KVH, 2, HD, padded), bf16),
    ]

    def route(turns, prepares):
        outputs = [message] + caches if prepares else [part] * peers
        return pl.pallas_call(
            functools.partial(route_kernel, turns, not prepares, n_seg, seg_rows, tokens),
            out_shape=outputs,
            in_specs=[SMEM, ANY, ANY] + [VMEM] * 2 * prepares,
            out_specs=[ANY] * len(outputs),
            scratch_shapes=[
                pltpu.VMEM((n_seg, PER_CHUNK, 2, seg_rows, WIDTH), bf16),
                pltpu.SemaphoreType.DMA((n_seg, PER_CHUNK, 2)),
                pltpu.SemaphoreType.DMA((n_seg,)),
            ]
            + [
                pltpu.VMEM((KVH, 2, padded, HD), bf16),
                pltpu.VMEM((KVH, 2, HD, padded), bf16),
                pltpu.SemaphoreType.DMA((2,)),
            ]
            * prepares,
            compiler_params=pltpu.CompilerParams(vmem_limit_bytes=VMEM_BYTES),
            cost_estimate=pl.CostEstimate(
                flops=0, bytes_accessed=(2 + 10 * prepares) << 20, transcendentals=0
            ),
            name=f"route_{turns[0]}",
        )(by_segment, queries, grad_out, *[keys, values] * prepares)

    def attend(turns, offset, received, before):
        work = slots * lanes * tokens * HD * len(turns)
        grad = jax.ShapeDtypeStruct((2, padded, HD), bf16)
        room = slots + slots % 2
        return pl.pallas_call(
            functools.partial(
                attend_kernel, turns, offset, len(before), peers, seg_rows, tokens
            ),
            out_shape=[message] + [grad] * len(turns),
            in_specs=[SMEM] + [ANY] * (2 + len(received) + len(before)),
            out_specs=[ANY] * (1 + len(turns)),
            input_output_aliases={3 + len(received): 0} if before else {},
            scratch_shapes=[
                pltpu.VMEM((len(turns), 2, padded, HD), bf16),
                pltpu.VMEM((len(turns), 2, HD, padded), bf16),
                pltpu.VMEM((len(turns), slots, 2, seg_rows, WIDTH), bf16),
                pltpu.VMEM((len(turns), room, 2, seg_rows, WIDTH), bf16),
                pltpu.VMEM((2, padded, lanes), f32),
                pltpu.VMEM((2, 2, padded, lanes), bf16),
                pltpu.VMEM((2, padded, lanes), bf16),
                pltpu.VMEM((len(turns), 2, padded, HD), f32),
                pltpu.VMEM((len(turns), 2, padded, HD), bf16),
                pltpu.SMEM((slots,), jnp.int32),
                pltpu.SemaphoreType.DMA((len(turns), 4)),
                pltpu.SemaphoreType.DMA((len(turns), slots)),
                pltpu.SemaphoreType.DMA((len(turns), slots)),
                pltpu.SemaphoreType.DMA((len(turns),)),
            ],
            compiler_params=pltpu.CompilerParams(vmem_limit_bytes=VMEM_BYTES),
            cost_estimate=pl.CostEstimate(
                flops=12 * work if len(turns) == 2 else work,
                bytes_accessed=8 << 20 if len(turns) == 2 else 1 << 20,
                transcendentals=slots * lanes * tokens if len(turns) == 2 else 0,
            ),
            name=f"attend_{turns[0]}",
        )(by_segment, *prepared, *received, *before)

    def collect(turns, returned, before):
        whole = jax.ShapeDtypeStruct(queries.shape, bf16)
        return pl.pallas_call(
            functools.partial(collect_kernel, turns, n_seg, seg_rows),
            out_shape=[whole, whole],
            in_specs=[SMEM, ANY] + [ANY] * len(before),
            out_specs=[ANY, ANY],
            input_output_aliases={2: 0, 3: 1} if before else {},
            scratch_shapes=[
                pltpu.VMEM((PER_CHUNK, 2, n_seg * seg_rows, WIDTH), bf16),
                pltpu.SemaphoreType.DMA((PER_CHUNK, 2, n_seg)),
                pltpu.SemaphoreType.DMA((PER_CHUNK, 2)),
            ],
            compiler_params=pltpu.CompilerParams(vmem_limit_bytes=VMEM_BYTES),
            cost_estimate=pl.CostEstimate(flops=0, bytes_accessed=4 << 20, transcendentals=0),
            name=f"collect_{turns[0]}",
        )(by_segment, returned, *before)

    def exchange(array):
        return lax.all_to_all(array, "enc", split_axis=0, concat_axis=0, tiled=True)

    def exchange_apart(arrays):
        order = sorted(range(peers), key=lambda k: (-(k >> 1).bit_count(), k & 1, k))
        arrived = {k: xor_permute(arrays[k], "enc", k) for k in order}
        return [arrived[k] for k in range(peers)]

    first, second = chunks
    received = exchange_apart(route(first, 0))
    routed, *prepared = route(second, 1)
    *received, routed = lax.optimization_barrier((*received, routed))
    received_later = exchange(routed)
    butterfly = n_seq == KVH
    returned, *grads = attend(first[:1], 0, received, [])
    if butterfly:
        passed = xor_permute(grads[0], "seq", 1)
    returned, last = attend(first[1:], 1, received, [returned])
    grads.append(last)
    if butterfly:
        passed, last = lax.optimization_barrier((passed, last))
        half = padded // 32 * 16
        cuts = [(0, 0, padded), (1, 0, half), (1, half, padded)]
        pair = [
            (last[j, a:b].astype(f32) + passed[j, a:b].astype(f32)).astype(bf16)
            for j, a, b in cuts
        ]
        pair = [xor_permute(one, "seq", 2) for one in pair]
    answer = exchange(returned)
    received_later, returned = lax.optimization_barrier((received_later, returned))
    returned, *more = attend(second, 0, [received_later], [])
    if butterfly:
        *pair[:2], returned = lax.optimization_barrier((*pair[:2], returned))
    answer, returned = lax.optimization_barrier((answer, returned))
    answer_later = exchange(returned)
    if butterfly:
        near = xor_permute(more[0], "seq", 1)
    early = collect(first, answer, [])
    attended, grad_queries = collect(second, answer_later, early)

    if butterfly:
        pair = [pair[0], jnp.concatenate(pair[1:], axis=0)]
        summed = [
            sum(
                term[:tokens].astype(f32) for term in (more[1][j], near[j], pair[j])
            ).astype(bf16)
            for j in range(2)
        ]
        return attended, grad_queries, summed[0][None], summed[1][None]
    joined = jnp.concatenate(grads + more, axis=2)[:, :tokens]
    summed = lax.psum_scatter(joined, "seq", scatter_dimension=2, tiled=True)
    return attended, grad_queries, summed[0][None], summed[1][None]


def solution(mesh):
    placed = (
        P(("seq", "enc"), None),
        P("enc", None, None),
        P("enc", None, None),
        P(),
        P(("seq", "enc"), None),
    )
    return jax.shard_map(
        per_device,
        mesh=mesh,
        in_specs=placed,
        out_specs=(
            P(("seq", "enc"), None),
            P(("seq", "enc"), None),
            P("enc", None, "seq"),
            P("enc", None, "seq"),
        ),
        check_vma=False,
    )
```

```python
import functools

import jax
import jax.numpy as jnp
from jax import lax
from jax.experimental import pallas as pl
from jax.experimental.pallas import tpu as pltpu
from jax.sharding import PartitionSpec as P

HQ = 32
KVH = 4
HD = 128
GROUP = HQ // KVH
WIDTH = GROUP * HD
SCALE = HD ** (-0.5)
LOG2E = 1.4426950408889634
CHUNK = 512
SLICE = 128
LOWEST = -3.0e38
PER_CHUNK = 2
VMEM_BYTES = 63 << 20
ANY = pl.BlockSpec(memory_space=pl.ANY)
SMEM = pl.BlockSpec(memory_space=pltpu.SMEM)
VMEM = pl.BlockSpec(memory_space=pltpu.VMEM)


def head_at(turn):
    if lax.axis_size("seq") == KVH:
        return lax.axis_index("seq") ^ (KVH - 1 - turn)
    return turn


def route_kernel(turns, apart, n_seg, seg_rows, tokens, reads, q_hbm, g_hbm, *refs):
    stage, in_sems, out_sems, *more = refs[-3:] if apart else refs[-6:]
    me = lax.axis_index("enc")
    row = lax.axis_index("seq") * lax.axis_size("enc") + me
    arriving = [[] for _ in range(n_seg)]
    for r in range(n_seg):
        rows = slice(r * seg_rows, (r + 1) * seg_rows)
        for i, turn in enumerate(turns):
            columns = pl.ds(pl.multiple_of(head_at(turn) * WIDTH, WIDTH), WIDTH)
            for which, source in enumerate((q_hbm, g_hbm)):
                arriving[r].append(
                    pltpu.make_async_copy(
                        source.at[rows, columns],
                        stage.at[r, i, which],
                        in_sems.at[r, i, which],
                    )
                )

    def leaving(r, i, target):
        return pltpu.make_async_copy(stage.at[r, i], target, out_sems.at[r, i])

    for copies in arriving:
        for copy in copies:
            copy.start()
    for r, copies in enumerate(arriving):
        for copy in copies:
            copy.wait()
        if apart:
            peers = len(refs[:-3]) // len(turns)
            for k in range(peers):

                @pl.when(reads[r, row] == me ^ k)
                def _():
                    for i in range(len(turns)):
                        leaving(r, i, refs[i * peers + k]).start()

        else:
            for i in range(len(turns)):
                leaving(r, i, refs[2].at[reads[r, row], i]).start()
    if not apart:
        k_in, v_in, _, *targets = refs[:5]
        straight, turned, cache_sems = more
        prepare(tokens, k_in, v_in, straight, turned)
        copies = [
            pltpu.make_async_copy(source, target.at[pl.ds(0, KVH)], cache_sems.at[i])
            for i, (source, target) in enumerate(((straight, targets[0]), (turned, targets[1])))
        ]
        for copy in copies:
            copy.start()
        for copy in copies:
            copy.wait()
    for r in range(n_seg):
        for i in range(len(turns)):
            leaving(r, i, refs[0] if apart else refs[2].at[0, 0]).wait()


def collect_kernel(turns, n_seg, seg_rows, reads, returned, *refs):
    o_hbm, dq_hbm, stage, in_sems, out_sems = refs[-5:]
    row = lax.axis_index("seq") * lax.axis_size("enc") + lax.axis_index("enc")
    arriving, leaving = [], []
    for i, turn in enumerate(turns):
        columns = pl.ds(pl.multiple_of(head_at(turn) * WIDTH, WIDTH), WIDTH)
        for which, target in enumerate((o_hbm, dq_hbm)):
            arriving.append(
                [
                    pltpu.make_async_copy(
                        returned.at[reads[r, row], i, which],
                        stage.at[i, which, r * seg_rows : (r + 1) * seg_rows, :],
                        in_sems.at[i, which, r],
                    )
                    for r in range(n_seg)
                ]
            )
            leaving.append(
                pltpu.make_async_copy(
                    stage.at[i, which], target.at[:, columns], out_sems.at[i, which]
                )
            )
    for copies in arriving:
        for copy in copies:
            copy.start()
    for copies, out in zip(arriving, leaving):
        for copy in copies:
            copy.wait()
        out.start()
    for out in leaving:
        out.wait()


def is_read(reads, row, image):
    found = jnp.int32(0)
    for r in range(reads.shape[0]):
        found = found + (reads[r, row] == image).astype(jnp.int32)
    return found > 0


def prepare(tokens, k_in, v_in, straight, turned):
    padded = straight.shape[2]
    whole = tokens // 16 * 16
    for which, source in enumerate((k_in, v_in)):
        for head in range(KVH):
            columns = slice(head * HD, (head + 1) * HD)
            straight[head, which, 0:whole, :] = source[0, 0:whole, columns]
            if whole < tokens:
                last = jnp.zeros((padded - tokens, HD), jnp.bfloat16)
                straight[head, which, whole:padded, :] = jnp.concatenate(
                    [source[0, whole:tokens, columns], last], axis=0
                )
            turned[head, which] = (
                straight[head, which].astype(jnp.float32).T.astype(jnp.bfloat16)
            )


def attend_kernel(turns, offset, before, peers, seg_rows, tokens, reads, caches, turned_caches, *refs):
    outs = 1 + len(turns)
    received, refs = refs[: len(refs) - 14 - outs], refs[len(refs) - 14 - outs :]
    received = received[: len(received) - before]
    returned, grads = refs[0], refs[1:outs]
    (
        straight,
        turned,
        inbox,
        outbox,
        scores,
        even_odd,
        dscores,
        sums,
        staged,
        owners,
        kv_sems,
        in_sems,
        out_sems,
        grad_sems,
    ) = refs[outs:]
    me = lax.axis_index("enc")
    base = lax.axis_index("seq") * peers
    slots = inbox.shape[1]
    padded = straight.shape[2]
    pieces = [(a, min(a + CHUNK, padded)) for a in range(0, padded, CHUNK)]
    lanes = GROUP * seg_rows
    f32, bf16 = jnp.float32, jnp.bfloat16

    kv_copies = [
        [
            pltpu.make_async_copy(
                source.at[head_at(turn), which], target.at[i, which], kv_sems.at[i, j]
            )
            for j, (source, target, which) in enumerate(
                (
                    (caches, straight, 0),
                    (turned_caches, turned, 1),
                    (caches, straight, 1),
                    (turned_caches, turned, 0),
                )
            )
        ]
        for i, turn in enumerate(turns)
    ]

    def arriving(i, slot, k):
        source = received[k] if len(received) > 1 else received[0].at[me ^ k, offset + i]
        return pltpu.make_async_copy(source, inbox.at[i, slot], in_sems.at[i, slot])

    def leaving(i, slot, owner):
        return pltpu.make_async_copy(
            outbox.at[i, slot], returned.at[owner, offset + i], out_sems.at[i, slot]
        )

    def handing(i):
        return pltpu.make_async_copy(staged.at[i], grads[i], grad_sems.at[i])

    for copies in kv_copies:
        copies[0].start()
    count = jnp.int32(0)
    for k in range(peers):
        found = is_read(reads, base + (me ^ k), me)

        @pl.when(found)
        def _():
            owners[count] = me ^ k
            for i in range(len(turns)):
                arriving(i, count, k).start()

        count = count + found.astype(jnp.int32)
    for j in range(1, 4):
        for copies in kv_copies:
            copies[j].start()

    sums[...] = jnp.zeros_like(sums)

    def stacked(i, slot, which):
        return jnp.concatenate(
            [inbox[i, slot, which, :, h * HD : (h + 1) * HD] for h in range(GROUP)], axis=0
        )

    def store(i, slot, which, turned_value):
        value = turned_value.T.astype(bf16)
        for h in range(GROUP):
            outbox[i, slot, which, :, h * HD : (h + 1) * HD] = value[
                h * seg_rows : (h + 1) * seg_rows, :
            ]

    def slices(a, b):
        return [(c, min(c + SLICE, b)) for c in range(a, b, SLICE)]

    def folded(value, reduce):
        return reduce(value.reshape(-1, 8, lanes), axis=0)

    def forward(u, i, slot, weights):
        source = jnp.minimum(slot, count - 1)
        q_turned = stacked(i, source, 0).astype(f32).T.astype(bf16)
        tops, totals, outs = [], [], []

        def score():
            part = jnp.dot(straight[i, 0], q_turned, preferred_element_type=f32)
            for c, d in slices(0, padded):
                piece = part[c:d, :]
                if d > tokens:
                    token = lax.broadcasted_iota(jnp.int32, piece.shape, 0) + c
                    piece = jnp.where(token < tokens, piece, LOWEST)
                scores[u, c:d, :] = piece
                tops.append(folded(piece, jnp.max))

        def weigh(a, b):
            if a == 0:
                tops[:] = [jnp.max(functools.reduce(jnp.maximum, tops), axis=0, keepdims=True)]
            for c, d in slices(a, b):
                piece = jnp.exp2((scores[u, c:d, :] - tops[0]) * (SCALE * LOG2E))
                totals.append(folded(piece, jnp.sum))
                weights[u, c:d, :] = piece.astype(bf16)
            outs.append(
                jnp.dot(turned[i, 1, :, a:b], weights[u, a:b, :], preferred_element_type=f32)
            )

        def finish():
            total = jnp.sum(functools.reduce(jnp.add, totals), axis=0, keepdims=True)
            inverse = 1.0 / total
            share = inverse * (slot < count).astype(f32)
            out = functools.reduce(jnp.add, outs) * inverse
            store(i, slot, 0, out)
            g = (stacked(i, source, 1).astype(f32).T * share).astype(bf16)
            exact = g.astype(f32)
            delta = jnp.sum(exact * out.astype(bf16).astype(f32), axis=0, keepdims=True)
            return delta, g, exact.T.astype(bf16)

        return score, weigh, finish

    def backward(u, i, slot, weights, delta, g_turned, g):
        q = stacked(i, jnp.minimum(slot, count - 1), 0)
        turned_dq = []

        def values_part(a, b):
            dprob = jnp.dot(straight[i, 1, a:b, :], g_turned, preferred_element_type=f32)
            for c, d in slices(a, b):
                piece = weights[u, c:d, :].astype(f32) * (dprob[c - a : d - a, :] - delta)
                dscores[u, c:d, :] = piece.astype(bf16)

        def values_sum():
            sums[i, 1] += jnp.dot(weights[u], g, preferred_element_type=f32)

        def keys_sum():
            sums[i, 0] += jnp.dot(dscores[u], q, preferred_element_type=f32)

        def queries_part(a, b):
            turned_dq.append(
                jnp.dot(turned[i, 0, :, a:b], dscores[u, a:b, :], preferred_element_type=f32)
            )

        def finish():
            store(i, slot, 1, functools.reduce(jnp.add, turned_dq) * SCALE)

        return values_part, values_sum, keys_sum, queries_part, finish

    paired = len(turns) == 2
    steps = count if paired else (count + 1) // 2

    def unit(u, step):
        return (u, step) if paired else (0, 2 * step + u)

    def await_step(step):
        for u in range(2):
            i, slot = unit(u, step)

            @pl.when(slot < count)
            def _():
                arriving(i, slot, 0).wait()

    def one_step(step, carry, last=False):
        weights, next_weights = even_odd.at[step & 1], even_odd.at[(step + 1) & 1]
        behind = [backward(u, *unit(u, step), weights, *carry[u]) for u in range(2)]
        ahead = []
        if not last:
            await_step(step + 1)
            ahead = [forward(u, *unit(u, step + 1), next_weights) for u in range(2)]

        for score, _, _ in ahead:
            score()
        for a, b in pieces:
            for values_part, *_ in behind:
                values_part(a, b)
        for _, values_sum, keys_sum, _, _ in behind:
            values_sum()
            keys_sum()
        for a, b in pieces:
            for _, weigh, _ in ahead:
                weigh(a, b)
            for _, _, _, queries_part, _ in behind:
                queries_part(a, b)
        for *_, finish in behind:
            finish()
        carry = [finish() for _, _, finish in ahead]
        for u in range(2):
            i, slot = unit(u, step)

            @pl.when(slot < count)
            def _():
                leaving(i, slot, owners[slot]).start()

        return carry

    heads = range(len(turns))

    @pl.when(count > 0)
    def _():
        await_step(0)
        for i in heads:
            kv_copies[i][0].wait()
        first = [forward(u, *unit(u, 0), even_odd.at[0]) for u in range(2)]
        for score, _, _ in first:
            score()
        for i in heads:
            kv_copies[i][1].wait()
        for a, b in pieces:
            for _, weigh, _ in first:
                weigh(a, b)
        carry = [finish() for _, _, finish in first]
        for i in heads:
            kv_copies[i][2].wait()
            kv_copies[i][3].wait()
        carry = lax.fori_loop(0, steps - 1, one_step, carry)
        one_step(steps - 1, carry, last=True)
        for i in heads:
            staged[i, 0] = (sums[i, 0] * SCALE).astype(bf16)
            staged[i, 1] = sums[i, 1].astype(bf16)
            handing(i).start()

    @pl.when(count == 0)
    def _():
        staged[...] = jnp.zeros_like(staged)
        for i in range(len(turns)):
            for copy in kv_copies[i]:
                copy.wait()
            handing(i).start()

    for i in range(len(turns)):
        for slot in range(slots):

            @pl.when(slot < count)
            def _():
                leaving(i, slot, 0).wait()

        handing(i).wait()


def xor_permute(array, axis, k):
    if k == 0:
        return array
    size = lax.axis_size(axis)
    return lax.ppermute(array, axis, [(i, i ^ k) for i in range(size)])


def per_device(queries, keys, values, reads, grad_out):
    peers = lax.axis_size("enc")
    n_seq = lax.axis_size("seq")
    n_seg = reads.shape[1]
    by_segment = reads.T
    seg_rows = queries.shape[0] // n_seg
    slots = min(peers, 3 * n_seg // 2)
    tokens = keys.shape[1]
    padded = (tokens + 15) // 16 * 16
    lanes = GROUP * seg_rows
    bf16, f32 = jnp.bfloat16, jnp.float32
    chunks = [tuple(range(i, i + PER_CHUNK)) for i in range(0, KVH, PER_CHUNK)]
    message = jax.ShapeDtypeStruct((peers, PER_CHUNK, 2, seg_rows, WIDTH), bf16)
    part = jax.ShapeDtypeStruct((2, seg_rows, WIDTH), bf16)

    caches = [
        jax.ShapeDtypeStruct((KVH, 2, padded, HD), bf16),
        jax.ShapeDtypeStruct((KVH, 2, HD, padded), bf16),
    ]

    def route(turns, prepares):
        outputs = [message] + caches if prepares else [part] * peers * len(turns)
        return pl.pallas_call(
            functools.partial(route_kernel, turns, not prepares, n_seg, seg_rows, tokens),
            out_shape=outputs,
            in_specs=[SMEM, ANY, ANY] + [VMEM] * 2 * prepares,
            out_specs=[ANY] * len(outputs),
            scratch_shapes=[
                pltpu.VMEM((n_seg, PER_CHUNK, 2, seg_rows, WIDTH), bf16),
                pltpu.SemaphoreType.DMA((n_seg, PER_CHUNK, 2)),
                pltpu.SemaphoreType.DMA((n_seg, PER_CHUNK)),
            ]
            + [
                pltpu.VMEM((KVH, 2, padded, HD), bf16),
                pltpu.VMEM((KVH, 2, HD, padded), bf16),
                pltpu.SemaphoreType.DMA((2,)),
            ]
            * prepares,
            compiler_params=pltpu.CompilerParams(vmem_limit_bytes=VMEM_BYTES),
            cost_estimate=pl.CostEstimate(
                flops=0, bytes_accessed=(2 + 10 * prepares) << 20, transcendentals=0
            ),
            name=f"route_{turns[0]}",
        )(by_segment, queries, grad_out, *[keys, values] * prepares)

    def attend(turns, offset, received, before):
        work = slots * lanes * tokens * HD * len(turns)
        grad = jax.ShapeDtypeStruct((2, padded, HD), bf16)
        room = slots + slots % 2
        return pl.pallas_call(
            functools.partial(
                attend_kernel, turns, offset, len(before), peers, seg_rows, tokens
            ),
            out_shape=[message] + [grad] * len(turns),
            in_specs=[SMEM] + [ANY] * (2 + len(received) + len(before)),
            out_specs=[ANY] * (1 + len(turns)),
            input_output_aliases={3 + len(received): 0} if before else {},
            scratch_shapes=[
                pltpu.VMEM((len(turns), 2, padded, HD), bf16),
                pltpu.VMEM((len(turns), 2, HD, padded), bf16),
                pltpu.VMEM((len(turns), slots, 2, seg_rows, WIDTH), bf16),
                pltpu.VMEM((len(turns), room, 2, seg_rows, WIDTH), bf16),
                pltpu.VMEM((2, padded, lanes), f32),
                pltpu.VMEM((2, 2, padded, lanes), bf16),
                pltpu.VMEM((2, padded, lanes), bf16),
                pltpu.VMEM((len(turns), 2, padded, HD), f32),
                pltpu.VMEM((len(turns), 2, padded, HD), bf16),
                pltpu.SMEM((slots,), jnp.int32),
                pltpu.SemaphoreType.DMA((len(turns), 4)),
                pltpu.SemaphoreType.DMA((len(turns), slots)),
                pltpu.SemaphoreType.DMA((len(turns), slots)),
                pltpu.SemaphoreType.DMA((len(turns),)),
            ],
            compiler_params=pltpu.CompilerParams(vmem_limit_bytes=VMEM_BYTES),
            cost_estimate=pl.CostEstimate(
                flops=12 * work if len(turns) == 2 else work,
                bytes_accessed=8 << 20 if len(turns) == 2 else 1 << 20,
                transcendentals=slots * lanes * tokens if len(turns) == 2 else 0,
            ),
            name=f"attend_{turns[0]}",
        )(by_segment, *prepared, *received, *before)

    def collect(turns, returned, before):
        whole = jax.ShapeDtypeStruct(queries.shape, bf16)
        return pl.pallas_call(
            functools.partial(collect_kernel, turns, n_seg, seg_rows),
            out_shape=[whole, whole],
            in_specs=[SMEM, ANY] + [ANY] * len(before),
            out_specs=[ANY, ANY],
            input_output_aliases={2: 0, 3: 1} if before else {},
            scratch_shapes=[
                pltpu.VMEM((PER_CHUNK, 2, n_seg * seg_rows, WIDTH), bf16),
                pltpu.SemaphoreType.DMA((PER_CHUNK, 2, n_seg)),
                pltpu.SemaphoreType.DMA((PER_CHUNK, 2)),
            ],
            compiler_params=pltpu.CompilerParams(vmem_limit_bytes=VMEM_BYTES),
            cost_estimate=pl.CostEstimate(flops=0, bytes_accessed=4 << 20, transcendentals=0),
            name=f"collect_{turns[0]}",
        )(by_segment, returned, *before)

    def exchange(array):
        return lax.all_to_all(array, "enc", split_axis=0, concat_axis=0, tiled=True)

    def exchange_apart(arrays):
        order = sorted(range(peers), key=lambda k: (-(k >> 1).bit_count(), k & 1, k))
        arrived = {k: xor_permute(arrays[k], "enc", k) for k in order}
        return [arrived[k] for k in range(peers)]

    first, second = chunks
    apart = route(first, 0)
    received = [exchange_apart(apart[i * peers : (i + 1) * peers]) for i in range(PER_CHUNK)]
    routed, *prepared = route(second, 1)
    butterfly = n_seq == KVH
    returned, *grads = attend(first[:1], 0, received[0], [])
    *received[1], grads[0], routed = lax.optimization_barrier((*received[1], grads[0], routed))
    received_later = exchange(routed)
    if butterfly:
        passed = xor_permute(grads[0], "seq", 1)
    returned, last = attend(first[1:], 1, received[1], [returned])
    grads.append(last)
    if butterfly:
        passed, last = lax.optimization_barrier((passed, last))
        half = padded // 32 * 16
        cuts = [(0, 0, padded), (1, 0, half), (1, half, padded)]
        pair = [
            (last[j, a:b].astype(f32) + passed[j, a:b].astype(f32)).astype(bf16)
            for j, a, b in cuts
        ]
        returned, *pair = lax.optimization_barrier((returned, *pair))
        pair = [xor_permute(one, "seq", 2) for one in pair]
    answer = exchange(returned)
    received_later, returned = lax.optimization_barrier((received_later, returned))
    returned, *more = attend(second, 0, [received_later], [])
    if butterfly:
        *pair[:2], returned = lax.optimization_barrier((*pair[:2], returned))
    answer, returned = lax.optimization_barrier((answer, returned))
    answer_later = exchange(returned)
    if butterfly:
        near = xor_permute(more[0], "seq", 1)
    early = collect(first, answer, [])
    attended, grad_queries = collect(second, answer_later, early)

    if butterfly:
        pair = [pair[0], jnp.concatenate(pair[1:], axis=0)]
        summed = [
            sum(
                term[:tokens].astype(f32) for term in (more[1][j], near[j], pair[j])
            ).astype(bf16)
            for j in range(2)
        ]
        return attended, grad_queries, summed[0][None], summed[1][None]
    joined = jnp.concatenate(grads + more, axis=2)[:, :tokens]
    summed = lax.psum_scatter(joined, "seq", scatter_dimension=2, tiled=True)
    return attended, grad_queries, summed[0][None], summed[1][None]


def solution(mesh):
    placed = (
        P(("seq", "enc"), None),
        P("enc", None, None),
        P("enc", None, None),
        P(),
        P(("seq", "enc"), None),
    )
    return jax.shard_map(
        per_device,
        mesh=mesh,
        in_specs=placed,
        out_specs=(
            P(("seq", "enc"), None),
            P(("seq", "enc"), None),
            P("enc", None, "seq"),
            P("enc", None, "seq"),
        ),
        check_vma=False,
    )
```

```python
import functools

import jax
import jax.numpy as jnp
from jax import lax
from jax.experimental import pallas as pl
from jax.experimental.pallas import tpu as pltpu
from jax.sharding import PartitionSpec as P

HQ = 32
KVH = 4
HD = 128
GROUP = HQ // KVH
WIDTH = GROUP * HD
SCALE = HD ** (-0.5)
LOG2E = 1.4426950408889634
CHUNK = 512
SLICE = 128
LOWEST = -3.0e38
PER_CHUNK = 2
VMEM_BYTES = 63 << 20
ANY = pl.BlockSpec(memory_space=pl.ANY)
SMEM = pl.BlockSpec(memory_space=pltpu.SMEM)
VMEM = pl.BlockSpec(memory_space=pltpu.VMEM)


def head_at(turn):
    if lax.axis_size("seq") == KVH:
        return lax.axis_index("seq") ^ (KVH - 1 - turn)
    return turn


def route_kernel(turns, apart, n_seg, seg_rows, tokens, reads, q_hbm, g_hbm, *refs):
    stage, in_sems, out_sems, *more = refs[-3:] if apart else refs[-6:]
    me = lax.axis_index("enc")
    row = lax.axis_index("seq") * lax.axis_size("enc") + me
    arriving = [[] for _ in range(n_seg)]
    for r in range(n_seg):
        rows = slice(r * seg_rows, (r + 1) * seg_rows)
        for i, turn in enumerate(turns):
            columns = pl.ds(pl.multiple_of(head_at(turn) * WIDTH, WIDTH), WIDTH)
            for which, source in enumerate((q_hbm, g_hbm)):
                arriving[r].append(
                    pltpu.make_async_copy(
                        source.at[rows, columns],
                        stage.at[r, i, which],
                        in_sems.at[r, i, which],
                    )
                )

    def leaving(r, target):
        return pltpu.make_async_copy(stage.at[r], target, out_sems.at[r])

    for copies in arriving:
        for copy in copies:
            copy.start()
    for r, copies in enumerate(arriving):
        for copy in copies:
            copy.wait()
        if apart:
            for k, out in enumerate(refs[:-3]):

                @pl.when(reads[r, row] == me ^ k)
                def _():
                    leaving(r, out).start()

        else:
            leaving(r, refs[2].at[reads[r, row]]).start()
    if not apart:
        k_in, v_in, _, *targets = refs[:5]
        straight, turned, cache_sems = more
        prepare(tokens, k_in, v_in, straight, turned)
        copies = [
            pltpu.make_async_copy(source, target.at[pl.ds(0, KVH)], cache_sems.at[i])
            for i, (source, target) in enumerate(((straight, targets[0]), (turned, targets[1])))
        ]
        for copy in copies:
            copy.start()
        for copy in copies:
            copy.wait()
    for r in range(n_seg):
        leaving(r, refs[0] if apart else refs[2].at[0]).wait()


def collect_kernel(turns, n_seg, seg_rows, reads, returned, *refs):
    o_hbm, dq_hbm, stage, in_sems, out_sems = refs[-5:]
    row = lax.axis_index("seq") * lax.axis_size("enc") + lax.axis_index("enc")
    arriving, leaving = [], []
    for i, turn in enumerate(turns):
        columns = pl.ds(pl.multiple_of(head_at(turn) * WIDTH, WIDTH), WIDTH)
        for which, target in enumerate((o_hbm, dq_hbm)):
            arriving.append(
                [
                    pltpu.make_async_copy(
                        returned.at[reads[r, row], i, which],
                        stage.at[i, which, r * seg_rows : (r + 1) * seg_rows, :],
                        in_sems.at[i, which, r],
                    )
                    for r in range(n_seg)
                ]
            )
            leaving.append(
                pltpu.make_async_copy(
                    stage.at[i, which], target.at[:, columns], out_sems.at[i, which]
                )
            )
    for copies in arriving:
        for copy in copies:
            copy.start()
    for copies, out in zip(arriving, leaving):
        for copy in copies:
            copy.wait()
        out.start()
    for out in leaving:
        out.wait()


def is_read(reads, row, image):
    found = jnp.int32(0)
    for r in range(reads.shape[0]):
        found = found + (reads[r, row] == image).astype(jnp.int32)
    return found > 0


def prepare(tokens, k_in, v_in, straight, turned):
    padded = straight.shape[2]
    whole = tokens // 16 * 16
    for which, source in enumerate((k_in, v_in)):
        for head in range(KVH):
            columns = slice(head * HD, (head + 1) * HD)
            straight[head, which, 0:whole, :] = source[0, 0:whole, columns]
            if whole < tokens:
                last = jnp.zeros((padded - tokens, HD), jnp.bfloat16)
                straight[head, which, whole:padded, :] = jnp.concatenate(
                    [source[0, whole:tokens, columns], last], axis=0
                )
            turned[head, which] = (
                straight[head, which].astype(jnp.float32).T.astype(jnp.bfloat16)
            )


def attend_kernel(turns, offset, before, peers, seg_rows, tokens, reads, caches, turned_caches, *refs):
    outs = 1 + len(turns)
    received, refs = refs[: len(refs) - 14 - outs], refs[len(refs) - 14 - outs :]
    received = received[: len(received) - before]
    returned, grads = refs[0], refs[1:outs]
    (
        straight,
        turned,
        inbox,
        outbox,
        scores,
        even_odd,
        dscores,
        sums,
        staged,
        owners,
        kv_sems,
        in_sems,
        out_sems,
        grad_sems,
    ) = refs[outs:]
    me = lax.axis_index("enc")
    base = lax.axis_index("seq") * peers
    slots = inbox.shape[1]
    padded = straight.shape[2]
    pieces = [(a, min(a + CHUNK, padded)) for a in range(0, padded, CHUNK)]
    lanes = GROUP * seg_rows
    f32, bf16 = jnp.float32, jnp.bfloat16

    kv_copies = [
        [
            pltpu.make_async_copy(
                source.at[head_at(turn), which], target.at[i, which], kv_sems.at[i, j]
            )
            for j, (source, target, which) in enumerate(
                (
                    (caches, straight, 0),
                    (turned_caches, turned, 1),
                    (caches, straight, 1),
                    (turned_caches, turned, 0),
                )
            )
        ]
        for i, turn in enumerate(turns)
    ]

    def arriving(i, slot, k):
        source = received[k] if len(received) > 1 else received[0].at[me ^ k]
        return pltpu.make_async_copy(source.at[offset + i], inbox.at[i, slot], in_sems.at[i, slot])

    def leaving(i, slot, owner):
        return pltpu.make_async_copy(
            outbox.at[i, slot], returned.at[owner, offset + i], out_sems.at[i, slot]
        )

    def handing(i, j):
        return pltpu.make_async_copy(staged.at[i, j], grads[i].at[j], grad_sems.at[i, j])

    for copies in kv_copies:
        copies[0].start()
    count = jnp.int32(0)
    for k in range(peers):
        found = is_read(reads, base + (me ^ k), me)

        @pl.when(found)
        def _():
            owners[count] = me ^ k
            for i in range(len(turns)):
                arriving(i, count, k).start()

        count = count + found.astype(jnp.int32)
    for j in range(1, 4):
        for copies in kv_copies:
            copies[j].start()

    sums[...] = jnp.zeros_like(sums)

    def stacked(i, slot, which):
        return jnp.concatenate(
            [inbox[i, slot, which, :, h * HD : (h + 1) * HD] for h in range(GROUP)], axis=0
        )

    def store(i, slot, which, turned_value):
        value = turned_value.T.astype(bf16)
        for h in range(GROUP):
            outbox[i, slot, which, :, h * HD : (h + 1) * HD] = value[
                h * seg_rows : (h + 1) * seg_rows, :
            ]

    def slices(a, b):
        return [(c, min(c + SLICE, b)) for c in range(a, b, SLICE)]

    def folded(value, reduce):
        return reduce(value.reshape(-1, 8, lanes), axis=0)

    def forward(u, i, slot, weights):
        source = jnp.minimum(slot, count - 1)
        own = slice(u * lanes, (u + 1) * lanes)
        q_turned = stacked(i, source, 0).astype(f32).T.astype(bf16)
        tops, totals, outs = [], [], []

        def score():
            part = jnp.dot(straight[i, 0], q_turned, preferred_element_type=f32)
            for c, d in slices(0, padded):
                piece = part[c:d, :]
                if d > tokens:
                    token = lax.broadcasted_iota(jnp.int32, piece.shape, 0) + c
                    piece = jnp.where(token < tokens, piece, LOWEST)
                scores[u, c:d, :] = piece
                tops.append(folded(piece, jnp.max))

        def weigh(a, b):
            if a == 0:
                tops[:] = [jnp.max(functools.reduce(jnp.maximum, tops), axis=0, keepdims=True)]
            for c, d in slices(a, b):
                piece = jnp.exp2((scores[u, c:d, :] - tops[0]) * (SCALE * LOG2E))
                totals.append(folded(piece, jnp.sum))
                weights[c:d, own] = piece.astype(bf16)
            outs.append(
                jnp.dot(turned[i, 1, :, a:b], weights[a:b, own], preferred_element_type=f32)
            )

        def finish():
            total = jnp.sum(functools.reduce(jnp.add, totals), axis=0, keepdims=True)
            inverse = 1.0 / total
            share = inverse * (slot < count).astype(f32)
            out = functools.reduce(jnp.add, outs) * inverse
            store(i, slot, 0, out)
            g = (stacked(i, source, 1).astype(f32).T * share).astype(bf16)
            exact = g.astype(f32)
            delta = jnp.sum(exact * out.astype(bf16).astype(f32), axis=0, keepdims=True)
            return delta, g, exact.T.astype(bf16)

        return score, weigh, finish

    def backward(u, i, slot, weights, delta, g_turned, g):
        q = stacked(i, jnp.minimum(slot, count - 1), 0)
        own = slice(u * lanes, (u + 1) * lanes)
        turned_dq = []

        def values_part(a, b):
            dprob = jnp.dot(straight[i, 1, a:b, :], g_turned, preferred_element_type=f32)
            for c, d in slices(a, b):
                piece = weights[c:d, own].astype(f32) * (dprob[c - a : d - a, :] - delta)
                dscores[c:d, own] = piece.astype(bf16)

        def queries_part(a, b):
            turned_dq.append(
                jnp.dot(turned[i, 0, :, a:b], dscores[a:b, own], preferred_element_type=f32)
            )

        def finish():
            store(i, slot, 1, functools.reduce(jnp.add, turned_dq) * SCALE)

        return values_part, (q, g), queries_part, finish

    heads = range(len(turns))
    paired = len(turns) == 2
    steps = count if paired else (count + 1) // 2

    def unit(u, step):
        return (u, step) if paired else (0, 2 * step + u)

    def await_step(step):
        for u in range(2):
            i, slot = unit(u, step)

            @pl.when(slot < count)
            def _():
                arriving(i, slot, 0).wait()

    def one_step(step, carry, last=False):
        weights, next_weights = even_odd.at[step & 1], even_odd.at[(step + 1) & 1]
        behind = [backward(u, *unit(u, step), weights, *carry[u]) for u in range(2)]
        ahead = []
        if not last:
            await_step(step + 1)
            ahead = [forward(u, *unit(u, step + 1), next_weights) for u in range(2)]

        for score, _, _ in ahead:
            score()
        for a, b in pieces:
            for values_part, *_ in behind:
                values_part(a, b)
        rows = [both for _, both, _, _ in behind]
        for j, left in ((1, weights), (0, dscores)):
            for i in heads:
                own = slice(i * lanes, (i + 1) * lanes) if paired else slice(None)
                right = rows[i][j] if paired else jnp.concatenate([r[j] for r in rows], axis=0)
                sums[i, j] += jnp.dot(left[:, own], right, preferred_element_type=f32)
            if last:
                for i in heads:
                    staged[i, j] = (sums[i, j] * (1.0 if j else SCALE)).astype(bf16)
                    handing(i, j).start()
        for a, b in pieces:
            for _, weigh, _ in ahead:
                weigh(a, b)
            for _, _, queries_part, _ in behind:
                queries_part(a, b)
        for *_, finish in behind:
            finish()
        carry = [finish() for _, _, finish in ahead]
        for u in range(2):
            i, slot = unit(u, step)

            @pl.when(slot < count)
            def _():
                leaving(i, slot, owners[slot]).start()

        return carry

    @pl.when(count > 0)
    def _():
        await_step(0)
        for i in heads:
            kv_copies[i][0].wait()
        first = [forward(u, *unit(u, 0), even_odd.at[0]) for u in range(2)]
        for score, _, _ in first:
            score()
        for i in heads:
            kv_copies[i][1].wait()
        for a, b in pieces:
            for _, weigh, _ in first:
                weigh(a, b)
        carry = [finish() for _, _, finish in first]
        for i in heads:
            kv_copies[i][2].wait()
            kv_copies[i][3].wait()
        carry = lax.fori_loop(0, steps - 1, one_step, carry)
        one_step(steps - 1, carry, last=True)

    @pl.when(count == 0)
    def _():
        staged[...] = jnp.zeros_like(staged)
        for i in range(len(turns)):
            for copy in kv_copies[i]:
                copy.wait()
            for j in range(2):
                handing(i, j).start()

    for i in range(len(turns)):
        for slot in range(slots):

            @pl.when(slot < count)
            def _():
                leaving(i, slot, 0).wait()

        for j in range(2):
            handing(i, j).wait()


def xor_permute(array, axis, k):
    if k == 0:
        return array
    size = lax.axis_size(axis)
    return lax.ppermute(array, axis, [(i, i ^ k) for i in range(size)])


def per_device(queries, keys, values, reads, grad_out):
    peers = lax.axis_size("enc")
    n_seq = lax.axis_size("seq")
    n_seg = reads.shape[1]
    by_segment = reads.T
    seg_rows = queries.shape[0] // n_seg
    slots = min(peers, 3 * n_seg // 2)
    tokens = keys.shape[1]
    padded = (tokens + 15) // 16 * 16
    lanes = GROUP * seg_rows
    bf16, f32 = jnp.bfloat16, jnp.float32
    chunks = [tuple(range(i, i + PER_CHUNK)) for i in range(0, KVH, PER_CHUNK)]
    message = jax.ShapeDtypeStruct((peers, PER_CHUNK, 2, seg_rows, WIDTH), bf16)
    part = jax.ShapeDtypeStruct((PER_CHUNK, 2, seg_rows, WIDTH), bf16)

    caches = [
        jax.ShapeDtypeStruct((KVH, 2, padded, HD), bf16),
        jax.ShapeDtypeStruct((KVH, 2, HD, padded), bf16),
    ]

    def route(turns, prepares):
        outputs = [message] + caches if prepares else [part] * peers
        return pl.pallas_call(
            functools.partial(route_kernel, turns, not prepares, n_seg, seg_rows, tokens),
            out_shape=outputs,
            in_specs=[SMEM, ANY, ANY] + [VMEM] * 2 * prepares,
            out_specs=[ANY] * len(outputs),
            scratch_shapes=[
                pltpu.VMEM((n_seg, PER_CHUNK, 2, seg_rows, WIDTH), bf16),
                pltpu.SemaphoreType.DMA((n_seg, PER_CHUNK, 2)),
                pltpu.SemaphoreType.DMA((n_seg,)),
            ]
            + [
                pltpu.VMEM((KVH, 2, padded, HD), bf16),
                pltpu.VMEM((KVH, 2, HD, padded), bf16),
                pltpu.SemaphoreType.DMA((2,)),
            ]
            * prepares,
            compiler_params=pltpu.CompilerParams(vmem_limit_bytes=VMEM_BYTES),
            cost_estimate=pl.CostEstimate(
                flops=0, bytes_accessed=(2 + 10 * prepares) << 20, transcendentals=0
            ),
            name=f"route_{turns[0]}",
        )(by_segment, queries, grad_out, *[keys, values] * prepares)

    def attend(turns, offset, received, before):
        work = slots * lanes * tokens * HD * len(turns)
        grad = jax.ShapeDtypeStruct((2, padded, HD), bf16)
        room = slots + slots % 2
        return pl.pallas_call(
            functools.partial(
                attend_kernel, turns, offset, len(before), peers, seg_rows, tokens
            ),
            out_shape=[message] + [grad] * len(turns),
            in_specs=[SMEM] + [ANY] * (2 + len(received) + len(before)),
            out_specs=[ANY] * (1 + len(turns)),
            input_output_aliases={3 + len(received): 0} if before else {},
            scratch_shapes=[
                pltpu.VMEM((len(turns), 2, padded, HD), bf16),
                pltpu.VMEM((len(turns), 2, HD, padded), bf16),
                pltpu.VMEM((len(turns), slots, 2, seg_rows, WIDTH), bf16),
                pltpu.VMEM((len(turns), room, 2, seg_rows, WIDTH), bf16),
                pltpu.VMEM((2, padded, lanes), f32),
                pltpu.VMEM((2, padded, 2 * lanes), bf16),
                pltpu.VMEM((padded, 2 * lanes), bf16),
                pltpu.VMEM((len(turns), 2, padded, HD), f32),
                pltpu.VMEM((len(turns), 2, padded, HD), bf16),
                pltpu.SMEM((slots,), jnp.int32),
                pltpu.SemaphoreType.DMA((len(turns), 4)),
                pltpu.SemaphoreType.DMA((len(turns), slots)),
                pltpu.SemaphoreType.DMA((len(turns), slots)),
                pltpu.SemaphoreType.DMA((len(turns), 2)),
            ],
            compiler_params=pltpu.CompilerParams(vmem_limit_bytes=VMEM_BYTES),
            cost_estimate=pl.CostEstimate(
                flops=12 * work if len(turns) == 2 else work,
                bytes_accessed=8 << 20 if len(turns) == 2 else 1 << 20,
                transcendentals=slots * lanes * tokens if len(turns) == 2 else 0,
            ),
            name=f"attend_{turns[0]}",
        )(by_segment, *prepared, *received, *before)

    def collect(turns, returned, before):
        whole = jax.ShapeDtypeStruct(queries.shape, bf16)
        return pl.pallas_call(
            functools.partial(collect_kernel, turns, n_seg, seg_rows),
            out_shape=[whole, whole],
            in_specs=[SMEM, ANY] + [ANY] * len(before),
            out_specs=[ANY, ANY],
            input_output_aliases={2: 0, 3: 1} if before else {},
            scratch_shapes=[
                pltpu.VMEM((PER_CHUNK, 2, n_seg * seg_rows, WIDTH), bf16),
                pltpu.SemaphoreType.DMA((PER_CHUNK, 2, n_seg)),
                pltpu.SemaphoreType.DMA((PER_CHUNK, 2)),
            ],
            compiler_params=pltpu.CompilerParams(vmem_limit_bytes=VMEM_BYTES),
            cost_estimate=pl.CostEstimate(flops=0, bytes_accessed=4 << 20, transcendentals=0),
            name=f"collect_{turns[0]}",
        )(by_segment, returned, *before)

    def exchange(array):
        return lax.all_to_all(array, "enc", split_axis=0, concat_axis=0, tiled=True)

    def exchange_apart(arrays):
        order = sorted(range(peers), key=lambda k: (-(k >> 1).bit_count(), k & 1, k))
        arrived = {k: xor_permute(arrays[k], "enc", k) for k in order}
        return [arrived[k] for k in range(peers)]

    first, second = chunks
    received = exchange_apart(route(first, 0))
    routed, *prepared = route(second, 1)
    *received, routed = lax.optimization_barrier((*received, routed))
    received_later = exchange(routed)
    butterfly = n_seq == KVH
    returned, *grads = attend(first[:1], 0, received, [])
    if butterfly:
        passed = xor_permute(grads[0], "seq", 1)
    returned, last = attend(first[1:], 1, received, [returned])
    grads.append(last)
    if butterfly:
        passed, last = lax.optimization_barrier((passed, last))
        half = padded // 32 * 16
        cuts = [(0, 0, padded), (1, 0, half), (1, half, padded)]
        pair = [
            (last[j, a:b].astype(f32) + passed[j, a:b].astype(f32)).astype(bf16)
            for j, a, b in cuts
        ]
        pair = [xor_permute(one, "seq", 2) for one in pair]
    answer = exchange(returned)
    received_later, returned = lax.optimization_barrier((received_later, returned))
    returned, *more = attend(second, 0, [received_later], [])
    if butterfly:
        *pair[:2], returned = lax.optimization_barrier((*pair[:2], returned))
    answer, returned = lax.optimization_barrier((answer, returned))
    answer_later = exchange(returned)
    if butterfly:
        near = xor_permute(more[0], "seq", 1)
    early = collect(first, answer, [])
    attended, grad_queries = collect(second, answer_later, early)

    if butterfly:
        pair = [pair[0], jnp.concatenate(pair[1:], axis=0)]
        summed = [
            sum(
                term[:tokens].astype(f32) for term in (more[1][j], near[j], pair[j])
            ).astype(bf16)
            for j in range(2)
        ]
        return attended, grad_queries, summed[0][None], summed[1][None]
    joined = jnp.concatenate(grads + more, axis=2)[:, :tokens]
    summed = lax.psum_scatter(joined, "seq", scatter_dimension=2, tiled=True)
    return attended, grad_queries, summed[0][None], summed[1][None]


def solution(mesh):
    placed = (
        P(("seq", "enc"), None),
        P("enc", None, None),
        P("enc", None, None),
        P(),
        P(("seq", "enc"), None),
    )
    return jax.shard_map(
        per_device,
        mesh=mesh,
        in_specs=placed,
        out_specs=(
            P(("seq", "enc"), None),
            P(("seq", "enc"), None),
            P("enc", None, "seq"),
            P("enc", None, "seq"),
        ),
        check_vma=False,
    )
```

```python
import functools

import jax
import jax.numpy as jnp
from jax import lax
from jax.experimental import pallas as pl
from jax.experimental.pallas import tpu as pltpu
from jax.sharding import PartitionSpec as P

HQ = 32
KVH = 4
HD = 128
GROUP = HQ // KVH
WIDTH = GROUP * HD
SCALE = HD ** (-0.5)
LOG2E = 1.4426950408889634
CHUNK = 1024
SLICE = 128
LOWEST = -3.0e38
PER_CHUNK = 2
VMEM_BYTES = 63 << 20
ANY = pl.BlockSpec(memory_space=pl.ANY)
SMEM = pl.BlockSpec(memory_space=pltpu.SMEM)
VMEM = pl.BlockSpec(memory_space=pltpu.VMEM)


def head_at(turn):
    if lax.axis_size("seq") == KVH:
        return lax.axis_index("seq") ^ (KVH - 1 - turn)
    return turn


def route_kernel(turns, apart, n_seg, seg_rows, tokens, reads, q_hbm, g_hbm, *refs):
    stage, in_sems, out_sems, *more = refs[-3:] if apart else refs[-6:]
    me = lax.axis_index("enc")
    row = lax.axis_index("seq") * lax.axis_size("enc") + me
    arriving = [[] for _ in range(n_seg)]
    for r in range(n_seg):
        rows = slice(r * seg_rows, (r + 1) * seg_rows)
        for i, turn in enumerate(turns):
            columns = pl.ds(pl.multiple_of(head_at(turn) * WIDTH, WIDTH), WIDTH)
            for which, source in enumerate((q_hbm, g_hbm)):
                arriving[r].append(
                    pltpu.make_async_copy(
                        source.at[rows, columns],
                        stage.at[r, i, which],
                        in_sems.at[r, i, which],
                    )
                )

    def leaving(r, target):
        return pltpu.make_async_copy(stage.at[r], target, out_sems.at[r])

    for copies in arriving:
        for copy in copies:
            copy.start()
    for r, copies in enumerate(arriving):
        for copy in copies:
            copy.wait()
        if apart:
            for k, out in enumerate(refs[:-3]):

                @pl.when(reads[r, row] == me ^ k)
                def _():
                    leaving(r, out).start()

        else:
            leaving(r, refs[2].at[reads[r, row]]).start()
    if not apart:
        k_in, v_in, _, *targets = refs[:5]
        straight, turned, cache_sems = more
        prepare(tokens, k_in, v_in, straight, turned)
        copies = [
            pltpu.make_async_copy(source, target.at[pl.ds(0, KVH)], cache_sems.at[i])
            for i, (source, target) in enumerate(((straight, targets[0]), (turned, targets[1])))
        ]
        for copy in copies:
            copy.start()
        for copy in copies:
            copy.wait()
    for r in range(n_seg):
        leaving(r, refs[0] if apart else refs[2].at[0]).wait()


def collect_kernel(turns, n_seg, seg_rows, reads, returned, *refs):
    o_hbm, dq_hbm, stage, in_sems, out_sems = refs[-5:]
    row = lax.axis_index("seq") * lax.axis_size("enc") + lax.axis_index("enc")
    arriving, leaving = [], []
    for i, turn in enumerate(turns):
        columns = pl.ds(pl.multiple_of(head_at(turn) * WIDTH, WIDTH), WIDTH)
        for which, target in enumerate((o_hbm, dq_hbm)):
            arriving.append(
                [
                    pltpu.make_async_copy(
                        returned.at[reads[r, row], i, which],
                        stage.at[i, which, r * seg_rows : (r + 1) * seg_rows, :],
                        in_sems.at[i, which, r],
                    )
                    for r in range(n_seg)
                ]
            )
            leaving.append(
                pltpu.make_async_copy(
                    stage.at[i, which], target.at[:, columns], out_sems.at[i, which]
                )
            )
    for copies in arriving:
        for copy in copies:
            copy.start()
    for copies, out in zip(arriving, leaving):
        for copy in copies:
            copy.wait()
        out.start()
    for out in leaving:
        out.wait()


def is_read(reads, row, image):
    found = jnp.int32(0)
    for r in range(reads.shape[0]):
        found = found + (reads[r, row] == image).astype(jnp.int32)
    return found > 0


def prepare(tokens, k_in, v_in, straight, turned):
    padded = straight.shape[2]
    whole = tokens // 16 * 16
    for which, source in enumerate((k_in, v_in)):
        for head in range(KVH):
            columns = slice(head * HD, (head + 1) * HD)
            straight[head, which, 0:whole, :] = source[0, 0:whole, columns]
            if whole < tokens:
                last = jnp.zeros((padded - tokens, HD), jnp.bfloat16)
                straight[head, which, whole:padded, :] = jnp.concatenate(
                    [source[0, whole:tokens, columns], last], axis=0
                )
            turned[head, which] = (
                straight[head, which].astype(jnp.float32).T.astype(jnp.bfloat16)
            )


def attend_kernel(turns, offset, before, peers, seg_rows, tokens, reads, caches, turned_caches, *refs):
    outs = 1 + len(turns)
    received, refs = refs[: len(refs) - 14 - outs], refs[len(refs) - 14 - outs :]
    received = received[: len(received) - before]
    returned, grads = refs[0], refs[1:outs]
    (
        straight,
        turned,
        inbox,
        outbox,
        scores,
        even_odd,
        dscores,
        sums,
        staged,
        owners,
        kv_sems,
        in_sems,
        out_sems,
        grad_sems,
    ) = refs[outs:]
    me = lax.axis_index("enc")
    base = lax.axis_index("seq") * peers
    slots = inbox.shape[1]
    padded = straight.shape[2]
    pieces = [(a, min(a + CHUNK, padded)) for a in range(0, padded, CHUNK)]
    lanes = GROUP * seg_rows
    f32, bf16 = jnp.float32, jnp.bfloat16

    kv_copies = [
        [
            pltpu.make_async_copy(
                source.at[head_at(turn), which], target.at[i, which], kv_sems.at[i, j]
            )
            for j, (source, target, which) in enumerate(
                (
                    (caches, straight, 0),
                    (turned_caches, turned, 1),
                    (caches, straight, 1),
                    (turned_caches, turned, 0),
                )
            )
        ]
        for i, turn in enumerate(turns)
    ]

    def arriving(i, slot, k):
        source = received[k] if len(received) > 1 else received[0].at[me ^ k]
        return pltpu.make_async_copy(source.at[offset + i], inbox.at[i, slot], in_sems.at[i, slot])

    def leaving(i, slot, owner):
        return pltpu.make_async_copy(
            outbox.at[i, slot], returned.at[owner, offset + i], out_sems.at[i, slot]
        )

    def handing(i):
        return pltpu.make_async_copy(staged.at[i], grads[i], grad_sems.at[i])

    for copies in kv_copies:
        copies[0].start()
    count = jnp.int32(0)
    for k in range(peers):
        found = is_read(reads, base + (me ^ k), me)

        @pl.when(found)
        def _():
            owners[count] = me ^ k
            for i in range(len(turns)):
                arriving(i, count, k).start()

        count = count + found.astype(jnp.int32)
    for j in range(1, 4):
        for copies in kv_copies:
            copies[j].start()

    sums[...] = jnp.zeros_like(sums)

    def stacked(i, slot, which):
        return jnp.concatenate(
            [inbox[i, slot, which, :, h * HD : (h + 1) * HD] for h in range(GROUP)], axis=0
        )

    def store(i, slot, which, turned_value):
        value = turned_value.T.astype(bf16)
        for h in range(GROUP):
            outbox[i, slot, which, :, h * HD : (h + 1) * HD] = value[
                h * seg_rows : (h + 1) * seg_rows, :
            ]

    def slices(a, b):
        return [(c, min(c + SLICE, b)) for c in range(a, b, SLICE)]

    def folded(value, reduce):
        return reduce(value.reshape(-1, 8, lanes), axis=0)

    def forward(u, i, slot, weights):
        source = jnp.minimum(slot, count - 1)
        q_turned = stacked(i, source, 0).astype(f32).T.astype(bf16)
        tops, totals, outs = [], [], []

        def score():
            part = jnp.dot(straight[i, 0], q_turned, preferred_element_type=f32)
            for c, d in slices(0, padded):
                piece = part[c:d, :]
                if d > tokens:
                    token = lax.broadcasted_iota(jnp.int32, piece.shape, 0) + c
                    piece = jnp.where(token < tokens, piece, LOWEST)
                scores[u, c:d, :] = piece
                tops.append(folded(piece, jnp.max))

        def weigh(a, b):
            if a == 0:
                tops[:] = [jnp.max(functools.reduce(jnp.maximum, tops), axis=0, keepdims=True)]
            for c, d in slices(a, b):
                piece = jnp.exp2((scores[u, c:d, :] - tops[0]) * (SCALE * LOG2E))
                totals.append(folded(piece, jnp.sum))
                weights[u, c:d, :] = piece.astype(bf16)
            outs.append(
                jnp.dot(turned[i, 1, :, a:b], weights[u, a:b, :], preferred_element_type=f32)
            )

        def finish():
            total = jnp.sum(functools.reduce(jnp.add, totals), axis=0, keepdims=True)
            inverse = 1.0 / total
            share = inverse * (slot < count).astype(f32)
            out = functools.reduce(jnp.add, outs) * inverse
            store(i, slot, 0, out)
            g = (stacked(i, source, 1).astype(f32).T * share).astype(bf16)
            exact = g.astype(f32)
            delta = jnp.sum(exact * out.astype(bf16).astype(f32), axis=0, keepdims=True)
            return delta, g, exact.T.astype(bf16)

        return score, weigh, finish

    def backward(u, i, slot, weights, delta, g_turned, g):
        q = stacked(i, jnp.minimum(slot, count - 1), 0)
        turned_dq = []

        def values_part(a, b):
            dprob = jnp.dot(straight[i, 1, a:b, :], g_turned, preferred_element_type=f32)
            for c, d in slices(a, b):
                piece = weights[u, c:d, :].astype(f32) * (dprob[c - a : d - a, :] - delta)
                dscores[u, c:d, :] = piece.astype(bf16)

        def values_sum():
            sums[i, 1] += jnp.dot(weights[u], g, preferred_element_type=f32)

        def keys_sum():
            sums[i, 0] += jnp.dot(dscores[u], q, preferred_element_type=f32)

        def queries_part(a, b):
            turned_dq.append(
                jnp.dot(turned[i, 0, :, a:b], dscores[u, a:b, :], preferred_element_type=f32)
            )

        def finish():
            store(i, slot, 1, functools.reduce(jnp.add, turned_dq) * SCALE)

        return values_part, values_sum, keys_sum, queries_part, finish

    paired = len(turns) == 2
    steps = count if paired else (count + 1) // 2

    def unit(u, step):
        return (u, step) if paired else (0, 2 * step + u)

    def await_step(step):
        for u in range(2):
            i, slot = unit(u, step)

            @pl.when(slot < count)
            def _():
                arriving(i, slot, 0).wait()

    def one_step(step, carry, last=False):
        weights, next_weights = even_odd.at[step & 1], even_odd.at[(step + 1) & 1]
        behind = [backward(u, *unit(u, step), weights, *carry[u]) for u in range(2)]
        ahead = []
        if not last:
            await_step(step + 1)
            ahead = [forward(u, *unit(u, step + 1), next_weights) for u in range(2)]

        for score, _, _ in ahead:
            score()
        for a, b in pieces:
            for values_part, *_ in behind:
                values_part(a, b)
        for _, values_sum, keys_sum, _, _ in behind:
            values_sum()
            keys_sum()
        for a, b in pieces:
            for _, weigh, _ in ahead:
                weigh(a, b)
            for _, _, _, queries_part, _ in behind:
                queries_part(a, b)
        for *_, finish in behind:
            finish()
        carry = [finish() for _, _, finish in ahead]
        for u in range(2):
            i, slot = unit(u, step)

            @pl.when(slot < count)
            def _():
                leaving(i, slot, owners[slot]).start()

        return carry

    heads = range(len(turns))

    @pl.when(count > 0)
    def _():
        await_step(0)
        for i in heads:
            kv_copies[i][0].wait()
        first = [forward(u, *unit(u, 0), even_odd.at[0]) for u in range(2)]
        for score, _, _ in first:
            score()
        for i in heads:
            kv_copies[i][1].wait()
        for a, b in pieces:
            for _, weigh, _ in first:
                weigh(a, b)
        carry = [finish() for _, _, finish in first]
        for i in heads:
            kv_copies[i][2].wait()
            kv_copies[i][3].wait()
        carry = lax.fori_loop(0, steps - 1, one_step, carry)
        one_step(steps - 1, carry, last=True)
        for i in heads:
            staged[i, 0] = (sums[i, 0] * SCALE).astype(bf16)
            staged[i, 1] = sums[i, 1].astype(bf16)
            handing(i).start()

    @pl.when(count == 0)
    def _():
        staged[...] = jnp.zeros_like(staged)
        for i in range(len(turns)):
            for copy in kv_copies[i]:
                copy.wait()
            handing(i).start()

    for i in range(len(turns)):
        for slot in range(slots):

            @pl.when(slot < count)
            def _():
                leaving(i, slot, 0).wait()

        handing(i).wait()


def xor_permute(array, axis, k):
    if k == 0:
        return array
    size = lax.axis_size(axis)
    return lax.ppermute(array, axis, [(i, i ^ k) for i in range(size)])


def per_device(queries, keys, values, reads, grad_out):
    peers = lax.axis_size("enc")
    n_seq = lax.axis_size("seq")
    n_seg = reads.shape[1]
    by_segment = reads.T
    seg_rows = queries.shape[0] // n_seg
    slots = min(peers, 3 * n_seg // 2)
    tokens = keys.shape[1]
    padded = (tokens + 15) // 16 * 16
    lanes = GROUP * seg_rows
    bf16, f32 = jnp.bfloat16, jnp.float32
    chunks = [tuple(range(i, i + PER_CHUNK)) for i in range(0, KVH, PER_CHUNK)]
    message = jax.ShapeDtypeStruct((peers, PER_CHUNK, 2, seg_rows, WIDTH), bf16)
    part = jax.ShapeDtypeStruct((PER_CHUNK, 2, seg_rows, WIDTH), bf16)

    caches = [
        jax.ShapeDtypeStruct((KVH, 2, padded, HD), bf16),
        jax.ShapeDtypeStruct((KVH, 2, HD, padded), bf16),
    ]

    def route(turns, prepares):
        outputs = [message] + caches if prepares else [part] * peers
        return pl.pallas_call(
            functools.partial(route_kernel, turns, not prepares, n_seg, seg_rows, tokens),
            out_shape=outputs,
            in_specs=[SMEM, ANY, ANY] + [VMEM] * 2 * prepares,
            out_specs=[ANY] * len(outputs),
            scratch_shapes=[
                pltpu.VMEM((n_seg, PER_CHUNK, 2, seg_rows, WIDTH), bf16),
                pltpu.SemaphoreType.DMA((n_seg, PER_CHUNK, 2)),
                pltpu.SemaphoreType.DMA((n_seg,)),
            ]
            + [
                pltpu.VMEM((KVH, 2, padded, HD), bf16),
                pltpu.VMEM((KVH, 2, HD, padded), bf16),
                pltpu.SemaphoreType.DMA((2,)),
            ]
            * prepares,
            compiler_params=pltpu.CompilerParams(vmem_limit_bytes=VMEM_BYTES),
            cost_estimate=pl.CostEstimate(
                flops=0, bytes_accessed=(2 + 10 * prepares) << 20, transcendentals=0
            ),
            name=f"route_{turns[0]}",
        )(by_segment, queries, grad_out, *[keys, values] * prepares)

    def attend(turns, offset, received, before):
        work = slots * lanes * tokens * HD * len(turns)
        grad = jax.ShapeDtypeStruct((2, padded, HD), bf16)
        room = slots + slots % 2
        return pl.pallas_call(
            functools.partial(
                attend_kernel, turns, offset, len(before), peers, seg_rows, tokens
            ),
            out_shape=[message] + [grad] * len(turns),
            in_specs=[SMEM] + [ANY] * (2 + len(received) + len(before)),
            out_specs=[ANY] * (1 + len(turns)),
            input_output_aliases={3 + len(received): 0} if before else {},
            scratch_shapes=[
                pltpu.VMEM((len(turns), 2, padded, HD), bf16),
                pltpu.VMEM((len(turns), 2, HD, padded), bf16),
                pltpu.VMEM((len(turns), slots, 2, seg_rows, WIDTH), bf16),
                pltpu.VMEM((len(turns), room, 2, seg_rows, WIDTH), bf16),
                pltpu.VMEM((2, padded, lanes), f32),
                pltpu.VMEM((2, 2, padded, lanes), bf16),
                pltpu.VMEM((2, padded, lanes), bf16),
                pltpu.VMEM((len(turns), 2, padded, HD), f32),
                pltpu.VMEM((len(turns), 2, padded, HD), bf16),
                pltpu.SMEM((slots,), jnp.int32),
                pltpu.SemaphoreType.DMA((len(turns), 4)),
                pltpu.SemaphoreType.DMA((len(turns), slots)),
                pltpu.SemaphoreType.DMA((len(turns), slots)),
                pltpu.SemaphoreType.DMA((len(turns),)),
            ],
            compiler_params=pltpu.CompilerParams(vmem_limit_bytes=VMEM_BYTES),
            cost_estimate=pl.CostEstimate(
                flops=12 * work if len(turns) == 2 else work,
                bytes_accessed=8 << 20 if len(turns) == 2 else 1 << 20,
                transcendentals=slots * lanes * tokens if len(turns) == 2 else 0,
            ),
            name=f"attend_{turns[0]}",
        )(by_segment, *prepared, *received, *before)

    def collect(turns, returned, before):
        whole = jax.ShapeDtypeStruct(queries.shape, bf16)
        return pl.pallas_call(
            functools.partial(collect_kernel, turns, n_seg, seg_rows),
            out_shape=[whole, whole],
            in_specs=[SMEM, ANY] + [ANY] * len(before),
            out_specs=[ANY, ANY],
            input_output_aliases={2: 0, 3: 1} if before else {},
            scratch_shapes=[
                pltpu.VMEM((PER_CHUNK, 2, n_seg * seg_rows, WIDTH), bf16),
                pltpu.SemaphoreType.DMA((PER_CHUNK, 2, n_seg)),
                pltpu.SemaphoreType.DMA((PER_CHUNK, 2)),
            ],
            compiler_params=pltpu.CompilerParams(vmem_limit_bytes=8 << 20),
            cost_estimate=pl.CostEstimate(flops=0, bytes_accessed=4 << 20, transcendentals=0),
            name=f"collect_{turns[0]}",
        )(by_segment, returned, *before)

    def exchange(array):
        return lax.all_to_all(array, "enc", split_axis=0, concat_axis=0, tiled=True)

    def exchange_apart(arrays):
        order = sorted(range(peers), key=lambda k: (-(k >> 1).bit_count(), k & 1, k))
        arrived = {k: xor_permute(arrays[k], "enc", k) for k in order}
        return [arrived[k] for k in range(peers)]

    first, second = chunks
    received = exchange_apart(route(first, 0))
    routed, *prepared = route(second, 1)
    *received, routed = lax.optimization_barrier((*received, routed))
    received_later = exchange(routed)
    butterfly = n_seq == KVH
    returned, *grads = attend(first[:1], 0, received, [])
    if butterfly:
        passed = xor_permute(grads[0], "seq", 1)
    returned, last = attend(first[1:], 1, received, [returned])
    grads.append(last)
    if butterfly:
        passed, last = lax.optimization_barrier((passed, last))
        half = padded // 32 * 16
        cuts = [(0, 0, padded), (1, 0, half), (1, half, padded)]
        pair = [
            (last[j, a:b].astype(f32) + passed[j, a:b].astype(f32)).astype(bf16)
            for j, a, b in cuts
        ]
        pair = [xor_permute(one, "seq", 2) for one in pair]
    answer = exchange(returned)
    received_later, returned = lax.optimization_barrier((received_later, returned))
    returned, *more = attend(second, 0, [received_later], [])
    if butterfly:
        *pair[:2], returned = lax.optimization_barrier((*pair[:2], returned))
    answer, returned = lax.optimization_barrier((answer, returned))
    answer_later = exchange(returned)
    if butterfly:
        near = xor_permute(more[0], "seq", 1)
    early = collect(first, answer, [])
    attended, grad_queries = collect(second, answer_later, early)

    if butterfly:
        pair = [pair[0], jnp.concatenate(pair[1:], axis=0)]
        summed = [
            sum(
                term[:tokens].astype(f32) for term in (more[1][j], near[j], pair[j])
            ).astype(bf16)
            for j in range(2)
        ]
        return attended, grad_queries, summed[0][None], summed[1][None]
    joined = jnp.concatenate(grads + more, axis=2)[:, :tokens]
    summed = lax.psum_scatter(joined, "seq", scatter_dimension=2, tiled=True)
    return attended, grad_queries, summed[0][None], summed[1][None]


def solution(mesh):
    placed = (
        P(("seq", "enc"), None),
        P("enc", None, None),
        P("enc", None, None),
        P(),
        P(("seq", "enc"), None),
    )
    return jax.shard_map(
        per_device,
        mesh=mesh,
        in_specs=placed,
        out_specs=(
            P(("seq", "enc"), None),
            P(("seq", "enc"), None),
            P("enc", None, "seq"),
            P("enc", None, "seq"),
        ),
        check_vma=False,
    )
```

```python
import functools

import jax
import jax.numpy as jnp
from jax import lax
from jax.experimental import pallas as pl
from jax.experimental.pallas import tpu as pltpu
from jax.sharding import PartitionSpec as P

HQ = 32
KVH = 4
HD = 128
GROUP = HQ // KVH
WIDTH = GROUP * HD
SCALE = HD ** (-0.5)
LOG2E = 1.4426950408889634
CHUNK = 1024
SLICE = 128
LOWEST = -3.0e38
PER_CHUNK = 2
VMEM_BYTES = 63 << 20
ANY = pl.BlockSpec(memory_space=pl.ANY)
SMEM = pl.BlockSpec(memory_space=pltpu.SMEM)
VMEM = pl.BlockSpec(memory_space=pltpu.VMEM)


def head_at(turn):
    if lax.axis_size("seq") == KVH:
        return lax.axis_index("seq") ^ (KVH - 1 - turn)
    return turn


def route_kernel(turns, apart, n_seg, seg_rows, tokens, reads, q_hbm, g_hbm, *refs):
    stage, in_sems, out_sems, *more = refs[-3:] if apart else refs[-6:]
    me = lax.axis_index("enc")
    row = lax.axis_index("seq") * lax.axis_size("enc") + me
    arriving = [[] for _ in range(n_seg)]
    for r in range(n_seg):
        rows = slice(r * seg_rows, (r + 1) * seg_rows)
        for i, turn in enumerate(turns):
            columns = pl.ds(pl.multiple_of(head_at(turn) * WIDTH, WIDTH), WIDTH)
            for which, source in enumerate((q_hbm, g_hbm)):
                arriving[r].append(
                    pltpu.make_async_copy(
                        source.at[rows, columns],
                        stage.at[r, i, which],
                        in_sems.at[r, i, which],
                    )
                )

    def leaving(r, target):
        return pltpu.make_async_copy(stage.at[r], target, out_sems.at[r])

    for copies in arriving:
        for copy in copies:
            copy.start()
    for r, copies in enumerate(arriving):
        for copy in copies:
            copy.wait()
        if apart:
            for k, out in enumerate(refs[:-3]):

                @pl.when(reads[r, row] == me ^ k)
                def _():
                    leaving(r, out).start()

        else:
            leaving(r, refs[2].at[reads[r, row]]).start()
    if not apart:
        k_in, v_in, _, *targets = refs[:5]
        straight, turned, cache_sems = more
        prepare(tokens, k_in, v_in, straight, turned)
        copies = [
            pltpu.make_async_copy(source, target.at[pl.ds(0, KVH)], cache_sems.at[i])
            for i, (source, target) in enumerate(((straight, targets[0]), (turned, targets[1])))
        ]
        for copy in copies:
            copy.start()
        for copy in copies:
            copy.wait()
    for r in range(n_seg):
        leaving(r, refs[0] if apart else refs[2].at[0]).wait()


def collect_kernel(turns, n_seg, seg_rows, reads, returned, *refs):
    o_hbm, dq_hbm, stage, in_sems, out_sems = refs[-5:]
    row = lax.axis_index("seq") * lax.axis_size("enc") + lax.axis_index("enc")
    arriving, leaving = [], []
    for i, turn in enumerate(turns):
        columns = pl.ds(pl.multiple_of(head_at(turn) * WIDTH, WIDTH), WIDTH)
        for which, target in enumerate((o_hbm, dq_hbm)):
            arriving.append(
                [
                    pltpu.make_async_copy(
                        returned.at[reads[r, row], i, which],
                        stage.at[i, which, r * seg_rows : (r + 1) * seg_rows, :],
                        in_sems.at[i, which, r],
                    )
                    for r in range(n_seg)
                ]
            )
            leaving.append(
                pltpu.make_async_copy(
                    stage.at[i, which], target.at[:, columns], out_sems.at[i, which]
                )
            )
    for copies in arriving:
        for copy in copies:
            copy.start()
    for copies, out in zip(arriving, leaving):
        for copy in copies:
            copy.wait()
        out.start()
    for out in leaving:
        out.wait()


def is_read(reads, row, image):
    found = jnp.int32(0)
    for r in range(reads.shape[0]):
        found = found + (reads[r, row] == image).astype(jnp.int32)
    return found > 0


def prepare(tokens, k_in, v_in, straight, turned):
    padded = straight.shape[2]
    whole = tokens // 16 * 16
    for which, source in enumerate((k_in, v_in)):
        for head in range(KVH):
            columns = slice(head * HD, (head + 1) * HD)
            straight[head, which, 0:whole, :] = source[0, 0:whole, columns]
            if whole < tokens:
                last = jnp.zeros((padded - tokens, HD), jnp.bfloat16)
                straight[head, which, whole:padded, :] = jnp.concatenate(
                    [source[0, whole:tokens, columns], last], axis=0
                )
            turned[head, which] = (
                straight[head, which].astype(jnp.float32).T.astype(jnp.bfloat16)
            )


def attend_kernel(turns, offset, before, order, peers, seg_rows, tokens, reads, caches, turned_caches, *refs):
    outs = 1 + len(turns)
    received, refs = refs[: len(refs) - 14 - outs], refs[len(refs) - 14 - outs :]
    received = received[: len(received) - before]
    returned, grads = refs[0], refs[1:outs]
    (
        straight,
        turned,
        inbox,
        outbox,
        scores,
        even_odd,
        dscores,
        sums,
        staged,
        owners,
        kv_sems,
        in_sems,
        out_sems,
        grad_sems,
    ) = refs[outs:]
    me = lax.axis_index("enc")
    base = lax.axis_index("seq") * peers
    slots = inbox.shape[1]
    padded = straight.shape[2]
    pieces = [(a, min(a + CHUNK, padded)) for a in range(0, padded, CHUNK)]
    lanes = GROUP * seg_rows
    f32, bf16 = jnp.float32, jnp.bfloat16

    kv_copies = [
        [
            pltpu.make_async_copy(
                source.at[head_at(turn), which], target.at[i, which], kv_sems.at[i, j]
            )
            for j, (source, target, which) in enumerate(
                (
                    (caches, straight, 0),
                    (turned_caches, turned, 1),
                    (caches, straight, 1),
                    (turned_caches, turned, 0),
                )
            )
        ]
        for i, turn in enumerate(turns)
    ]

    def arriving(i, slot, k):
        source = received[order.index(k)] if len(received) > 1 else received[0].at[me ^ k]
        return pltpu.make_async_copy(source.at[offset + i], inbox.at[i, slot], in_sems.at[i, slot])

    def leaving(i, slot, owner):
        return pltpu.make_async_copy(
            outbox.at[i, slot], returned.at[owner, offset + i], out_sems.at[i, slot]
        )

    def handing(i):
        return pltpu.make_async_copy(staged.at[i], grads[i], grad_sems.at[i])

    for copies in kv_copies:
        copies[0].start()
    count = jnp.int32(0)
    for k in range(peers):
        found = is_read(reads, base + (me ^ k), me)

        @pl.when(found)
        def _():
            owners[count] = me ^ k
            for i in range(len(turns)):
                arriving(i, count, k).start()

        count = count + found.astype(jnp.int32)
    for j in range(1, 4):
        for copies in kv_copies:
            copies[j].start()

    sums[...] = jnp.zeros_like(sums)

    def stacked(i, slot, which):
        return jnp.concatenate(
            [inbox[i, slot, which, :, h * HD : (h + 1) * HD] for h in range(GROUP)], axis=0
        )

    def store(i, slot, which, turned_value):
        value = turned_value.T.astype(bf16)
        for h in range(GROUP):
            outbox[i, slot, which, :, h * HD : (h + 1) * HD] = value[
                h * seg_rows : (h + 1) * seg_rows, :
            ]

    def slices(a, b):
        return [(c, min(c + SLICE, b)) for c in range(a, b, SLICE)]

    def folded(value, reduce):
        return reduce(value.reshape(-1, 8, lanes), axis=0)

    def forward(u, i, slot, weights):
        source = jnp.minimum(slot, count - 1)
        q_turned = stacked(i, source, 0).astype(f32).T.astype(bf16)
        tops, totals, outs = [], [], []

        def score():
            part = jnp.dot(straight[i, 0], q_turned, preferred_element_type=f32)
            for c, d in slices(0, padded):
                piece = part[c:d, :]
                if d > tokens:
                    token = lax.broadcasted_iota(jnp.int32, piece.shape, 0) + c
                    piece = jnp.where(token < tokens, piece, LOWEST)
                scores[u, c:d, :] = piece
                tops.append(folded(piece, jnp.max))

        def weigh(a, b):
            if a == 0:
                tops[:] = [jnp.max(functools.reduce(jnp.maximum, tops), axis=0, keepdims=True)]
            for c, d in slices(a, b):
                piece = jnp.exp2((scores[u, c:d, :] - tops[0]) * (SCALE * LOG2E))
                totals.append(folded(piece, jnp.sum))
                weights[u, c:d, :] = piece.astype(bf16)
            outs.append(
                jnp.dot(turned[i, 1, :, a:b], weights[u, a:b, :], preferred_element_type=f32)
            )

        def finish():
            total = jnp.sum(functools.reduce(jnp.add, totals), axis=0, keepdims=True)
            inverse = 1.0 / total
            share = inverse * (slot < count).astype(f32)
            out = functools.reduce(jnp.add, outs) * inverse
            store(i, slot, 0, out)
            g = (stacked(i, source, 1).astype(f32).T * share).astype(bf16)
            exact = g.astype(f32)
            delta = jnp.sum(exact * out.astype(bf16).astype(f32), axis=0, keepdims=True)
            return delta, g, exact.T.astype(bf16)

        return score, weigh, finish

    def backward(u, i, slot, weights, delta, g_turned, g):
        q = stacked(i, jnp.minimum(slot, count - 1), 0)
        turned_dq = []

        def values_part(a, b):
            dprob = jnp.dot(straight[i, 1, a:b, :], g_turned, preferred_element_type=f32)
            for c, d in slices(a, b):
                piece = weights[u, c:d, :].astype(f32) * (dprob[c - a : d - a, :] - delta)
                dscores[u, c:d, :] = piece.astype(bf16)

        def values_sum():
            sums[i, 1] += jnp.dot(weights[u], g, preferred_element_type=f32)

        def keys_sum():
            sums[i, 0] += jnp.dot(dscores[u], q, preferred_element_type=f32)

        def queries_part(a, b):
            turned_dq.append(
                jnp.dot(turned[i, 0, :, a:b], dscores[u, a:b, :], preferred_element_type=f32)
            )

        def finish():
            store(i, slot, 1, functools.reduce(jnp.add, turned_dq) * SCALE)

        return values_part, values_sum, keys_sum, queries_part, finish

    paired = len(turns) == 2
    steps = count if paired else (count + 1) // 2

    def unit(u, step):
        return (u, step) if paired else (0, 2 * step + u)

    def await_step(step):
        for u in range(2):
            i, slot = unit(u, step)

            @pl.when(slot < count)
            def _():
                arriving(i, slot, 0).wait()

    def one_step(step, carry, last=False):
        weights, next_weights = even_odd.at[step & 1], even_odd.at[(step + 1) & 1]
        behind = [backward(u, *unit(u, step), weights, *carry[u]) for u in range(2)]
        ahead = []
        if not last:
            await_step(step + 1)
            ahead = [forward(u, *unit(u, step + 1), next_weights) for u in range(2)]

        for score, _, _ in ahead:
            score()
        for a, b in pieces:
            for values_part, *_ in behind:
                values_part(a, b)
        for _, values_sum, keys_sum, _, _ in behind:
            values_sum()
            keys_sum()
        for a, b in pieces:
            for _, weigh, _ in ahead:
                weigh(a, b)
            for _, _, _, queries_part, _ in behind:
                queries_part(a, b)
        for *_, finish in behind:
            finish()
        carry = [finish() for _, _, finish in ahead]
        for u in range(2):
            i, slot = unit(u, step)

            @pl.when(slot < count)
            def _():
                leaving(i, slot, owners[slot]).start()

        return carry

    heads = range(len(turns))

    @pl.when(count > 0)
    def _():
        await_step(0)
        for i in heads:
            kv_copies[i][0].wait()
        first = [forward(u, *unit(u, 0), even_odd.at[0]) for u in range(2)]
        for score, _, _ in first:
            score()
        for i in heads:
            kv_copies[i][1].wait()
        for a, b in pieces:
            for _, weigh, _ in first:
                weigh(a, b)
        carry = [finish() for _, _, finish in first]
        for i in heads:
            kv_copies[i][2].wait()
            kv_copies[i][3].wait()
        carry = lax.fori_loop(0, steps - 1, one_step, carry)
        one_step(steps - 1, carry, last=True)
        for i in heads:
            staged[i, 0] = (sums[i, 0] * SCALE).astype(bf16)
            staged[i, 1] = sums[i, 1].astype(bf16)
            handing(i).start()

    @pl.when(count == 0)
    def _():
        staged[...] = jnp.zeros_like(staged)
        for i in range(len(turns)):
            for copy in kv_copies[i]:
                copy.wait()
            handing(i).start()

    for i in range(len(turns)):
        for slot in range(slots):

            @pl.when(slot < count)
            def _():
                leaving(i, slot, 0).wait()

        handing(i).wait()


def xor_permute(array, axis, k):
    if k == 0:
        return array
    size = lax.axis_size(axis)
    return lax.ppermute(array, axis, [(i, i ^ k) for i in range(size)])


def per_device(queries, keys, values, reads, grad_out):
    peers = lax.axis_size("enc")
    n_seq = lax.axis_size("seq")
    n_seg = reads.shape[1]
    by_segment = reads.T
    seg_rows = queries.shape[0] // n_seg
    slots = min(peers, 3 * n_seg // 2)
    tokens = keys.shape[1]
    padded = (tokens + 15) // 16 * 16
    lanes = GROUP * seg_rows
    bf16, f32 = jnp.bfloat16, jnp.float32
    chunks = [tuple(range(i, i + PER_CHUNK)) for i in range(0, KVH, PER_CHUNK)]
    message = jax.ShapeDtypeStruct((peers, PER_CHUNK, 2, seg_rows, WIDTH), bf16)
    part = jax.ShapeDtypeStruct((PER_CHUNK, 2, seg_rows, WIDTH), bf16)

    caches = [
        jax.ShapeDtypeStruct((KVH, 2, padded, HD), bf16),
        jax.ShapeDtypeStruct((KVH, 2, HD, padded), bf16),
    ]

    def route(turns, prepares):
        outputs = [message] + caches if prepares else [part] * peers
        return pl.pallas_call(
            functools.partial(route_kernel, turns, not prepares, n_seg, seg_rows, tokens),
            out_shape=outputs,
            in_specs=[SMEM, ANY, ANY] + [VMEM] * 2 * prepares,
            out_specs=[ANY] * len(outputs),
            scratch_shapes=[
                pltpu.VMEM((n_seg, PER_CHUNK, 2, seg_rows, WIDTH), bf16),
                pltpu.SemaphoreType.DMA((n_seg, PER_CHUNK, 2)),
                pltpu.SemaphoreType.DMA((n_seg,)),
            ]
            + [
                pltpu.VMEM((KVH, 2, padded, HD), bf16),
                pltpu.VMEM((KVH, 2, HD, padded), bf16),
                pltpu.SemaphoreType.DMA((2,)),
            ]
            * prepares,
            compiler_params=pltpu.CompilerParams(vmem_limit_bytes=VMEM_BYTES),
            cost_estimate=pl.CostEstimate(
                flops=0, bytes_accessed=(2 + 10 * prepares) << 20, transcendentals=0
            ),
            name=f"route_{turns[0]}",
        )(by_segment, queries, grad_out, *[keys, values] * prepares)

    def attend(turns, offset, received, before):
        work = slots * lanes * tokens * HD * len(turns)
        grad = jax.ShapeDtypeStruct((2, padded, HD), bf16)
        room = slots + slots % 2
        return pl.pallas_call(
            functools.partial(
                attend_kernel, turns, offset, len(before), order, peers, seg_rows, tokens
            ),
            out_shape=[message] + [grad] * len(turns),
            in_specs=[SMEM] + [ANY] * (2 + len(received) + len(before)),
            out_specs=[ANY] * (1 + len(turns)),
            input_output_aliases={3 + len(received): 0} if before else {},
            scratch_shapes=[
                pltpu.VMEM((len(turns), 2, padded, HD), bf16),
                pltpu.VMEM((len(turns), 2, HD, padded), bf16),
                pltpu.VMEM((len(turns), slots, 2, seg_rows, WIDTH), bf16),
                pltpu.VMEM((len(turns), room, 2, seg_rows, WIDTH), bf16),
                pltpu.VMEM((2, padded, lanes), f32),
                pltpu.VMEM((2, 2, padded, lanes), bf16),
                pltpu.VMEM((2, padded, lanes), bf16),
                pltpu.VMEM((len(turns), 2, padded, HD), f32),
                pltpu.VMEM((len(turns), 2, padded, HD), bf16),
                pltpu.SMEM((slots,), jnp.int32),
                pltpu.SemaphoreType.DMA((len(turns), 4)),
                pltpu.SemaphoreType.DMA((len(turns), slots)),
                pltpu.SemaphoreType.DMA((len(turns), slots)),
                pltpu.SemaphoreType.DMA((len(turns),)),
            ],
            compiler_params=pltpu.CompilerParams(vmem_limit_bytes=VMEM_BYTES),
            cost_estimate=pl.CostEstimate(
                flops=12 * work if len(turns) == 2 else work,
                bytes_accessed=8 << 20 if len(turns) == 2 else 1 << 20,
                transcendentals=slots * lanes * tokens if len(turns) == 2 else 0,
            ),
            name=f"attend_{turns[0]}",
        )(by_segment, *prepared, *received, *before)

    def collect(turns, returned, before):
        whole = jax.ShapeDtypeStruct(queries.shape, bf16)
        return pl.pallas_call(
            functools.partial(collect_kernel, turns, n_seg, seg_rows),
            out_shape=[whole, whole],
            in_specs=[SMEM, ANY] + [ANY] * len(before),
            out_specs=[ANY, ANY],
            input_output_aliases={2: 0, 3: 1} if before else {},
            scratch_shapes=[
                pltpu.VMEM((PER_CHUNK, 2, n_seg * seg_rows, WIDTH), bf16),
                pltpu.SemaphoreType.DMA((PER_CHUNK, 2, n_seg)),
                pltpu.SemaphoreType.DMA((PER_CHUNK, 2)),
            ],
            compiler_params=pltpu.CompilerParams(vmem_limit_bytes=8 << 20),
            cost_estimate=pl.CostEstimate(flops=0, bytes_accessed=4 << 20, transcendentals=0),
            name=f"collect_{turns[0]}",
        )(by_segment, returned, *before)

    def exchange(array):
        return lax.all_to_all(array, "enc", split_axis=0, concat_axis=0, tiled=True)

    order = [0, 1] + sorted(range(2, peers), key=lambda k: (k & 1, -(k >> 1).bit_count(), k))

    def exchange_apart(arrays):
        return [xor_permute(arrays[k], "enc", k) for k in order]

    first, second = chunks
    received = exchange_apart(route(first, 0))
    routed, *prepared = route(second, 1)
    *received, routed = lax.optimization_barrier((*received, routed))
    received_later = exchange(routed)
    butterfly = n_seq == KVH
    returned, *grads = attend(first[:1], 0, received, [])
    if butterfly:
        passed = xor_permute(grads[0], "seq", 1)
    returned, last = attend(first[1:], 1, received, [returned])
    grads.append(last)
    if butterfly:
        passed, last = lax.optimization_barrier((passed, last))
        half = padded // 32 * 16
        cuts = [(0, 0, padded), (1, 0, half), (1, half, padded)]
        pair = [
            (last[j, a:b].astype(f32) + passed[j, a:b].astype(f32)).astype(bf16)
            for j, a, b in cuts
        ]
        pair = [xor_permute(one, "seq", 2) for one in pair]
    answer = exchange(returned)
    received_later, returned = lax.optimization_barrier((received_later, returned))
    returned, *more = attend(second, 0, [received_later], [])
    if butterfly:
        *pair[:2], returned = lax.optimization_barrier((*pair[:2], returned))
    answer, returned = lax.optimization_barrier((answer, returned))
    answer_later = exchange(returned)
    if butterfly:
        near = xor_permute(more[0], "seq", 1)
    early = collect(first, answer, [])
    attended, grad_queries = collect(second, answer_later, early)

    if butterfly:
        pair = [pair[0], jnp.concatenate(pair[1:], axis=0)]
        summed = [
            sum(
                term[:tokens].astype(f32) for term in (more[1][j], near[j], pair[j])
            ).astype(bf16)
            for j in range(2)
        ]
        return attended, grad_queries, summed[0][None], summed[1][None]
    joined = jnp.concatenate(grads + more, axis=2)[:, :tokens]
    summed = lax.psum_scatter(joined, "seq", scatter_dimension=2, tiled=True)
    return attended, grad_queries, summed[0][None], summed[1][None]


def solution(mesh):
    placed = (
        P(("seq", "enc"), None),
        P("enc", None, None),
        P("enc", None, None),
        P(),
        P(("seq", "enc"), None),
    )
    return jax.shard_map(
        per_device,
        mesh=mesh,
        in_specs=placed,
        out_specs=(
            P(("seq", "enc"), None),
            P(("seq", "enc"), None),
            P("enc", None, "seq"),
            P("enc", None, "seq"),
        ),
        check_vma=False,
    )
```

```python
import functools

import jax
import jax.numpy as jnp
from jax import lax
from jax.experimental import pallas as pl
from jax.experimental.pallas import tpu as pltpu
from jax.sharding import PartitionSpec as P

HQ = 32
KVH = 4
HD = 128
GROUP = HQ // KVH
WIDTH = GROUP * HD
SCALE = HD ** (-0.5)
LOG2E = 1.4426950408889634
CHUNK = 1024
SLICE = 128
LOWEST = -3.0e38
PER_CHUNK = 2
VMEM_BYTES = 63 << 20
ANY = pl.BlockSpec(memory_space=pl.ANY)
SMEM = pl.BlockSpec(memory_space=pltpu.SMEM)
VMEM = pl.BlockSpec(memory_space=pltpu.VMEM)


def head_at(turn):
    if lax.axis_size("seq") == KVH:
        return lax.axis_index("seq") ^ (KVH - 1 - turn)
    return turn


def route_kernel(turns, apart, n_seg, seg_rows, tokens, reads, q_hbm, g_hbm, *refs):
    stage, in_sems, out_sems, *more = refs[-3:] if apart else refs[-6:]
    me = lax.axis_index("enc")
    row = lax.axis_index("seq") * lax.axis_size("enc") + me
    arriving = [[] for _ in range(n_seg)]
    for r in range(n_seg):
        rows = slice(r * seg_rows, (r + 1) * seg_rows)
        for i, turn in enumerate(turns):
            columns = pl.ds(pl.multiple_of(head_at(turn) * WIDTH, WIDTH), WIDTH)
            for which, source in enumerate((q_hbm, g_hbm)):
                arriving[r].append(
                    pltpu.make_async_copy(
                        source.at[rows, columns],
                        stage.at[r, i, which],
                        in_sems.at[r, i, which],
                    )
                )

    def leaving(r, target):
        return pltpu.make_async_copy(stage.at[r], target, out_sems.at[r])

    for copies in arriving:
        for copy in copies:
            copy.start()
    for r, copies in enumerate(arriving):
        for copy in copies:
            copy.wait()
        if apart:
            for k, out in enumerate(refs[:-3]):

                @pl.when(reads[r, row] == me ^ k)
                def _():
                    leaving(r, out).start()

        else:
            leaving(r, refs[2].at[reads[r, row]]).start()
    if not apart:
        k_in, v_in, _, *targets = refs[:5]
        straight, turned, cache_sems = more
        prepare(tokens, k_in, v_in, straight, turned)
        copies = [
            pltpu.make_async_copy(source, target.at[pl.ds(0, KVH)], cache_sems.at[i])
            for i, (source, target) in enumerate(((straight, targets[0]), (turned, targets[1])))
        ]
        for copy in copies:
            copy.start()
        for copy in copies:
            copy.wait()
    for r in range(n_seg):
        leaving(r, refs[0] if apart else refs[2].at[0]).wait()


def collect_kernel(turns, n_seg, seg_rows, reads, returned, *refs):
    o_hbm, dq_hbm, stage, in_sems, out_sems = refs[-5:]
    row = lax.axis_index("seq") * lax.axis_size("enc") + lax.axis_index("enc")
    arriving, leaving = [], []
    for i, turn in enumerate(turns):
        columns = pl.ds(pl.multiple_of(head_at(turn) * WIDTH, WIDTH), WIDTH)
        for which, target in enumerate((o_hbm, dq_hbm)):
            arriving.append(
                [
                    pltpu.make_async_copy(
                        returned.at[reads[r, row], i, which],
                        stage.at[i, which, r * seg_rows : (r + 1) * seg_rows, :],
                        in_sems.at[i, which, r],
                    )
                    for r in range(n_seg)
                ]
            )
            leaving.append(
                pltpu.make_async_copy(
                    stage.at[i, which], target.at[:, columns], out_sems.at[i, which]
                )
            )
    for copies in arriving:
        for copy in copies:
            copy.start()
    for copies, out in zip(arriving, leaving):
        for copy in copies:
            copy.wait()
        out.start()
    for out in leaving:
        out.wait()


def is_read(reads, row, image):
    found = jnp.int32(0)
    for r in range(reads.shape[0]):
        found = found + (reads[r, row] == image).astype(jnp.int32)
    return found > 0


def prepare(tokens, k_in, v_in, straight, turned):
    padded = straight.shape[2]
    whole = tokens // 16 * 16
    for which, source in enumerate((k_in, v_in)):
        for head in range(KVH):
            columns = slice(head * HD, (head + 1) * HD)
            straight[head, which, 0:whole, :] = source[0, 0:whole, columns]
            if whole < tokens:
                last = jnp.zeros((padded - tokens, HD), jnp.bfloat16)
                straight[head, which, whole:padded, :] = jnp.concatenate(
                    [source[0, whole:tokens, columns], last], axis=0
                )
            turned[head, which] = (
                straight[head, which].astype(jnp.float32).T.astype(jnp.bfloat16)
            )


def attend_kernel(turns, offset, before, order, peers, seg_rows, tokens, reads, caches, turned_caches, *refs):
    outs = 1 + len(turns)
    received, refs = refs[: len(refs) - 14 - outs], refs[len(refs) - 14 - outs :]
    received = received[: len(received) - before]
    returned, grads = refs[0], refs[1:outs]
    (
        straight,
        turned,
        inbox,
        outbox,
        scores,
        even_odd,
        dscores,
        sums,
        staged,
        owners,
        kv_sems,
        in_sems,
        out_sems,
        grad_sems,
    ) = refs[outs:]
    me = lax.axis_index("enc")
    base = lax.axis_index("seq") * peers
    slots = inbox.shape[1]
    padded = straight.shape[2]
    pieces = [(a, min(a + CHUNK, padded)) for a in range(0, padded, CHUNK)]
    lanes = GROUP * seg_rows
    f32, bf16 = jnp.float32, jnp.bfloat16

    kv_copies = [
        [
            pltpu.make_async_copy(
                source.at[head_at(turn), which], target.at[i, which], kv_sems.at[i, j]
            )
            for j, (source, target, which) in enumerate(
                (
                    (caches, straight, 0),
                    (turned_caches, turned, 1),
                    (caches, straight, 1),
                    (turned_caches, turned, 0),
                )
            )
        ]
        for i, turn in enumerate(turns)
    ]

    def arriving(i, slot, k):
        source = received[order.index(k)] if len(received) > 1 else received[0].at[me ^ k]
        return pltpu.make_async_copy(source.at[offset + i], inbox.at[i, slot], in_sems.at[i, slot])

    def leaving(i, slot, owner):
        return pltpu.make_async_copy(
            outbox.at[i, slot], returned.at[owner, offset + i], out_sems.at[i, slot]
        )

    def handing(i):
        return pltpu.make_async_copy(staged.at[i], grads[i], grad_sems.at[i])

    for copies in kv_copies:
        copies[0].start()
    count = jnp.int32(0)
    for k in range(peers):
        found = is_read(reads, base + (me ^ k), me)

        @pl.when(found)
        def _():
            owners[count] = me ^ k
            for i in range(len(turns)):
                arriving(i, count, k).start()

        count = count + found.astype(jnp.int32)
    for j in range(1, 4):
        for copies in kv_copies:
            copies[j].start()

    sums[...] = jnp.zeros_like(sums)

    def stacked(i, slot, which):
        return jnp.concatenate(
            [inbox[i, slot, which, :, h * HD : (h + 1) * HD] for h in range(GROUP)], axis=0
        )

    def store(i, slot, which, turned_value):
        value = turned_value.T.astype(bf16)
        for h in range(GROUP):
            outbox[i, slot, which, :, h * HD : (h + 1) * HD] = value[
                h * seg_rows : (h + 1) * seg_rows, :
            ]

    def slices(a, b):
        return [(c, min(c + SLICE, b)) for c in range(a, b, SLICE)]

    def folded(value, reduce):
        return reduce(value.reshape(-1, 8, lanes), axis=0)

    def forward(u, i, slot, weights):
        source = jnp.minimum(slot, count - 1)
        q_turned = stacked(i, source, 0).astype(f32).T.astype(bf16)
        tops, totals, outs = [], [], []

        def score():
            part = jnp.dot(straight[i, 0], q_turned, preferred_element_type=f32)
            for c, d in slices(0, padded):
                piece = part[c:d, :]
                if d > tokens:
                    token = lax.broadcasted_iota(jnp.int32, piece.shape, 0) + c
                    piece = jnp.where(token < tokens, piece, LOWEST)
                scores[u, c:d, :] = piece
                tops.append(folded(piece, jnp.max))

        def weigh(a, b):
            if a == 0:
                tops[:] = [jnp.max(functools.reduce(jnp.maximum, tops), axis=0, keepdims=True)]
            for c, d in slices(a, b):
                piece = jnp.exp2((scores[u, c:d, :] - tops[0]) * (SCALE * LOG2E))
                totals.append(folded(piece, jnp.sum))
                weights[u, c:d, :] = piece.astype(bf16)
            outs.append(
                jnp.dot(turned[i, 1, :, a:b], weights[u, a:b, :], preferred_element_type=f32)
            )

        def finish():
            total = jnp.sum(functools.reduce(jnp.add, totals), axis=0, keepdims=True)
            inverse = 1.0 / total
            share = inverse * (slot < count).astype(f32)
            out = functools.reduce(jnp.add, outs) * inverse
            store(i, slot, 0, out)
            g = (stacked(i, source, 1).astype(f32).T * share).astype(bf16)
            exact = g.astype(f32)
            delta = jnp.sum(exact * out.astype(bf16).astype(f32), axis=0, keepdims=True)
            return delta, g, exact.T.astype(bf16)

        return score, weigh, finish

    def backward(u, i, slot, weights, delta, g_turned, g):
        q = stacked(i, jnp.minimum(slot, count - 1), 0)
        turned_dq = []

        def values_part(a, b):
            dprob = jnp.dot(straight[i, 1, a:b, :], g_turned, preferred_element_type=f32)
            for c, d in slices(a, b):
                piece = weights[u, c:d, :].astype(f32) * (dprob[c - a : d - a, :] - delta)
                dscores[u, c:d, :] = piece.astype(bf16)

        def values_sum():
            sums[i, 1] += jnp.dot(weights[u], g, preferred_element_type=f32)

        def keys_sum():
            sums[i, 0] += jnp.dot(dscores[u], q, preferred_element_type=f32)

        def queries_part(a, b):
            turned_dq.append(
                jnp.dot(turned[i, 0, :, a:b], dscores[u, a:b, :], preferred_element_type=f32)
            )

        def finish():
            store(i, slot, 1, functools.reduce(jnp.add, turned_dq) * SCALE)

        return values_part, values_sum, keys_sum, queries_part, finish

    paired = len(turns) == 2
    steps = count if paired else (count + 1) // 2

    def unit(u, step):
        return (u, step) if paired else (0, 2 * step + u)

    def await_step(step):
        for u in range(2):
            i, slot = unit(u, step)

            @pl.when(slot < count)
            def _():
                arriving(i, slot, 0).wait()

    def one_step(step, carry, last=False):
        weights, next_weights = even_odd.at[step & 1], even_odd.at[(step + 1) & 1]
        behind = [backward(u, *unit(u, step), weights, *carry[u]) for u in range(2)]
        ahead = []
        if not last:
            await_step(step + 1)
            ahead = [forward(u, *unit(u, step + 1), next_weights) for u in range(2)]

        for score, _, _ in ahead:
            score()
        for a, b in pieces:
            for values_part, *_ in behind:
                values_part(a, b)
        for _, values_sum, keys_sum, _, _ in behind:
            values_sum()
            keys_sum()
        for a, b in pieces:
            for _, weigh, _ in ahead:
                weigh(a, b)
            for _, _, _, queries_part, _ in behind:
                queries_part(a, b)
        for *_, finish in behind:
            finish()
        carry = [finish() for _, _, finish in ahead]
        for u in range(2):
            i, slot = unit(u, step)

            @pl.when(slot < count)
            def _():
                leaving(i, slot, owners[slot]).start()

        return carry

    heads = range(len(turns))

    @pl.when(count > 0)
    def _():
        await_step(0)
        for i in heads:
            kv_copies[i][0].wait()
        first = [forward(u, *unit(u, 0), even_odd.at[0]) for u in range(2)]
        for score, _, _ in first:
            score()
        for i in heads:
            kv_copies[i][1].wait()
        for a, b in pieces:
            for _, weigh, _ in first:
                weigh(a, b)
        carry = [finish() for _, _, finish in first]
        for i in heads:
            kv_copies[i][2].wait()
            kv_copies[i][3].wait()
        carry = lax.fori_loop(0, steps - 1, one_step, carry)
        one_step(steps - 1, carry, last=True)
        for i in heads:
            staged[i, 0] = (sums[i, 0] * SCALE).astype(bf16)
            staged[i, 1] = sums[i, 1].astype(bf16)
            handing(i).start()

    @pl.when(count == 0)
    def _():
        staged[...] = jnp.zeros_like(staged)
        for i in range(len(turns)):
            for copy in kv_copies[i]:
                copy.wait()
            handing(i).start()

    for i in range(len(turns)):
        for slot in range(slots):

            @pl.when(slot < count)
            def _():
                leaving(i, slot, 0).wait()

        handing(i).wait()


def xor_permute(array, axis, k):
    if k == 0:
        return array
    size = lax.axis_size(axis)
    return lax.ppermute(array, axis, [(i, i ^ k) for i in range(size)])


def per_device(queries, keys, values, reads, grad_out):
    peers = lax.axis_size("enc")
    n_seq = lax.axis_size("seq")
    n_seg = reads.shape[1]
    by_segment = reads.T
    seg_rows = queries.shape[0] // n_seg
    slots = min(peers, 3 * n_seg // 2)
    tokens = keys.shape[1]
    padded = (tokens + 15) // 16 * 16
    lanes = GROUP * seg_rows
    bf16, f32 = jnp.bfloat16, jnp.float32
    chunks = [tuple(range(i, i + PER_CHUNK)) for i in range(0, KVH, PER_CHUNK)]
    message = jax.ShapeDtypeStruct((peers, PER_CHUNK, 2, seg_rows, WIDTH), bf16)
    part = jax.ShapeDtypeStruct((PER_CHUNK, 2, seg_rows, WIDTH), bf16)

    caches = [
        jax.ShapeDtypeStruct((KVH, 2, padded, HD), bf16),
        jax.ShapeDtypeStruct((KVH, 2, HD, padded), bf16),
    ]

    def route(turns, prepares):
        outputs = [message] + caches if prepares else [part] * peers
        return pl.pallas_call(
            functools.partial(route_kernel, turns, not prepares, n_seg, seg_rows, tokens),
            out_shape=outputs,
            in_specs=[SMEM, ANY, ANY] + [VMEM] * 2 * prepares,
            out_specs=[ANY] * len(outputs),
            scratch_shapes=[
                pltpu.VMEM((n_seg, PER_CHUNK, 2, seg_rows, WIDTH), bf16),
                pltpu.SemaphoreType.DMA((n_seg, PER_CHUNK, 2)),
                pltpu.SemaphoreType.DMA((n_seg,)),
            ]
            + [
                pltpu.VMEM((KVH, 2, padded, HD), bf16),
                pltpu.VMEM((KVH, 2, HD, padded), bf16),
                pltpu.SemaphoreType.DMA((2,)),
            ]
            * prepares,
            compiler_params=pltpu.CompilerParams(vmem_limit_bytes=VMEM_BYTES),
            cost_estimate=pl.CostEstimate(
                flops=0, bytes_accessed=(2 + 10 * prepares) << 20, transcendentals=0
            ),
            name=f"route_{turns[0]}",
        )(by_segment, queries, grad_out, *[keys, values] * prepares)

    def attend(turns, offset, received, before):
        work = slots * lanes * tokens * HD * len(turns)
        grad = jax.ShapeDtypeStruct((2, padded, HD), bf16)
        room = slots + slots % 2
        return pl.pallas_call(
            functools.partial(
                attend_kernel, turns, offset, len(before), order, peers, seg_rows, tokens
            ),
            out_shape=[message] + [grad] * len(turns),
            in_specs=[SMEM] + [ANY] * (2 + len(received) + len(before)),
            out_specs=[ANY] * (1 + len(turns)),
            input_output_aliases={3 + len(received): 0} if before else {},
            scratch_shapes=[
                pltpu.VMEM((len(turns), 2, padded, HD), bf16),
                pltpu.VMEM((len(turns), 2, HD, padded), bf16),
                pltpu.VMEM((len(turns), slots, 2, seg_rows, WIDTH), bf16),
                pltpu.VMEM((len(turns), room, 2, seg_rows, WIDTH), bf16),
                pltpu.VMEM((2, padded, lanes), f32),
                pltpu.VMEM((2, 2, padded, lanes), bf16),
                pltpu.VMEM((2, padded, lanes), bf16),
                pltpu.VMEM((len(turns), 2, padded, HD), f32),
                pltpu.VMEM((len(turns), 2, padded, HD), bf16),
                pltpu.SMEM((slots,), jnp.int32),
                pltpu.SemaphoreType.DMA((len(turns), 4)),
                pltpu.SemaphoreType.DMA((len(turns), slots)),
                pltpu.SemaphoreType.DMA((len(turns), slots)),
                pltpu.SemaphoreType.DMA((len(turns),)),
            ],
            compiler_params=pltpu.CompilerParams(vmem_limit_bytes=VMEM_BYTES),
            cost_estimate=pl.CostEstimate(
                flops=12 * work if len(turns) == 2 else work,
                bytes_accessed=8 << 20 if len(turns) == 2 else 1 << 20,
                transcendentals=slots * lanes * tokens if len(turns) == 2 else 0,
            ),
            name=f"attend_{turns[0]}",
        )(by_segment, *prepared, *received, *before)

    def collect(turns, returned, before):
        whole = jax.ShapeDtypeStruct(queries.shape, bf16)
        return pl.pallas_call(
            functools.partial(collect_kernel, turns, n_seg, seg_rows),
            out_shape=[whole, whole],
            in_specs=[SMEM, ANY] + [ANY] * len(before),
            out_specs=[ANY, ANY],
            input_output_aliases={2: 0, 3: 1} if before else {},
            scratch_shapes=[
                pltpu.VMEM((PER_CHUNK, 2, n_seg * seg_rows, WIDTH), bf16),
                pltpu.SemaphoreType.DMA((PER_CHUNK, 2, n_seg)),
                pltpu.SemaphoreType.DMA((PER_CHUNK, 2)),
            ],
            compiler_params=pltpu.CompilerParams(vmem_limit_bytes=8 << 20),
            cost_estimate=pl.CostEstimate(flops=0, bytes_accessed=4 << 20, transcendentals=0),
            name=f"collect_{turns[0]}",
        )(by_segment, returned, *before)

    def exchange(array):
        return lax.all_to_all(array, "enc", split_axis=0, concat_axis=0, tiled=True)

    order = [0, 1] + sorted(range(2, peers), key=lambda k: (k & 1, -(k >> 1).bit_count(), k))

    def exchange_apart(arrays):
        return [xor_permute(arrays[k], "enc", k) for k in order]

    first, second = chunks
    received = exchange_apart(route(first, 0))
    routed, *prepared = route(second, 1)
    *received, routed = lax.optimization_barrier((*received, routed))
    received_later = exchange(routed)
    butterfly = n_seq == KVH
    returned, *grads = attend(first[:1], 0, received, [])
    if butterfly:
        passed = xor_permute(grads[0], "seq", 1)
    returned, last = attend(first[1:], 1, received, [returned])
    grads.append(last)
    if butterfly:
        passed, last = lax.optimization_barrier((passed, last))
        half = padded // 64 * 16
        cuts = [(0, 0, padded), (1, 0, half), (1, half, padded)]
        pair = [
            (last[j, a:b].astype(f32) + passed[j, a:b].astype(f32)).astype(bf16)
            for j, a, b in cuts
        ]
        pair = [xor_permute(one, "seq", 2) for one in pair]
    answer = exchange(returned)
    received_later, returned = lax.optimization_barrier((received_later, returned))
    returned, *more = attend(second, 0, [received_later], [])
    if butterfly:
        *pair[:2], returned = lax.optimization_barrier((*pair[:2], returned))
    answer, returned = lax.optimization_barrier((answer, returned))
    answer_later = exchange(returned)
    if butterfly:
        near = xor_permute(more[0], "seq", 1)
    early = collect(first, answer, [])
    attended, grad_queries = collect(second, answer_later, early)

    if butterfly:
        pair = [pair[0], jnp.concatenate(pair[1:], axis=0)]
        summed = [
            sum(
                term[:tokens].astype(f32) for term in (more[1][j], near[j], pair[j])
            ).astype(bf16)
            for j in range(2)
        ]
        return attended, grad_queries, summed[0][None], summed[1][None]
    joined = jnp.concatenate(grads + more, axis=2)[:, :tokens]
    summed = lax.psum_scatter(joined, "seq", scatter_dimension=2, tiled=True)
    return attended, grad_queries, summed[0][None], summed[1][None]


def solution(mesh):
    placed = (
        P(("seq", "enc"), None),
        P("enc", None, None),
        P("enc", None, None),
        P(),
        P(("seq", "enc"), None),
    )
    return jax.shard_map(
        per_device,
        mesh=mesh,
        in_specs=placed,
        out_specs=(
            P(("seq", "enc"), None),
            P(("seq", "enc"), None),
            P("enc", None, "seq"),
            P("enc", None, "seq"),
        ),
        check_vma=False,
    )
```
